512 devices in a mesh: lat: 8 (over y, core), lon: 32 (over x_lo, z), dp: 2 (over x_hi).
Axes of the slice: x: 4 (x_hi: 2, x_lo: 2; x = x_hi * 2 + x_lo), y: 4, z: 16, core: 2. Of those that a mesh axis runs over, the one named last changes fastest.
Arguments:
- field: bfloat16 [2, 2, 96, 192, 384], P('dp', None, 'lat', 'lon'), may hold values from -6 to 6
- cotangent: bfloat16 [2, 2, 96, 192, 384], P('dp', None, 'lat', 'lon'), may hold values from -6 to 6
- qkv_plain: bfloat16 [384, 1152], P(None, 'dp'), may hold values from -0.3125 to 0.3125
- proj_plain: bfloat16 [384, 384], replicated, may hold values from -0.3125 to 0.3125
- bias_plain: bfloat16 [1, 8, 12, 6336], P(None, 'lat'), may hold values from -4 to 264
- qkv_shift: bfloat16 [384, 1152], P(None, 'dp'), may hold values from -0.3125 to 0.3125
- proj_shift: bfloat16 [384, 384], replicated, may hold values from -0.3125 to 0.3125
- bias_shift: bfloat16 [1, 8, 12, 6336], P(None, 'lat'), may hold values from -4 to 264
Outputs:
- out_field: bfloat16 [2, 2, 96, 192, 384], P('dp', None, 'lat', 'lon')
- grad_field: bfloat16 [2, 2, 96, 192, 384], P('dp', None, 'lat', 'lon')
- grad_proj_plain: bfloat16 [384, 384], replicated
- grad_proj_shift: bfloat16 [384, 384], replicated
The draws below stay inside these ranges and needn't reach their ends.
All inputs are finite; a program needn't handle non-finite values.
Results may differ from the reference program's by a relative error of at most 0.015.
Values may be sent and summed in bfloat16 or wider, within the bound.
A program may use at most 128 MiB of HBM per device.

```python
import jax
import jax.numpy as jnp
from jax import lax

C = 384
HEADS = 12
LEV = 2
WLEV = 2
WLAT = 12
WLON = 6
BATCH = 2
LAT = 96
LON = 192


def table_shape():
    return (LEV // WLEV, LAT // WLAT, HEADS, WLEV * WLEV * WLAT * WLAT * (2 * WLON - 1))


def draw_bias_plain(key, part):
    key = jax.random.fold_in(key, 11)
    return jnp.clip(jax.random.normal(key, table_shape(), jnp.float32), -4.0, 4.0).astype(jnp.bfloat16)


def draw_bias_shift(key, part):
    key = jax.random.fold_in(key, 23)
    return jnp.clip(jax.random.normal(key, table_shape(), jnp.float32), -4.0, 4.0).astype(jnp.bfloat16)


def steps_of(own_key, extent, pieces, low, largest):
    factor_of = 1.0
    for position, blocks in pieces:
        heights = jax.random.uniform(jax.random.fold_in(jax.random.fold_in(own_key, 6), position), (blocks,), jnp.float32, low / len(pieces), largest / len(pieces))
        factor_of = factor_of * jnp.repeat(jnp.exp(heights), extent[position] // blocks).reshape((-1,) + (1,) * (len(extent) - 1 - position))
    return factor_of


def bell_draw(rng, extent, deviation, limit, shards=(), held_as=jnp.bfloat16):
    array = deviation * jax.random.normal(rng, extent, jnp.float32)
    if shards:
        array = array * steps_of(rng, extent, shards, -0.22, 0.18)
    return jnp.clip(array, -limit, limit).astype(held_as)


def setup_inputs(seed: int = 0) -> dict:
    seeds = jax.random.split(jax.random.key(seed), 9)
    return {
        "field": bell_draw(seeds[0], (BATCH, LEV, LAT, LON, C), 1.0, 6.0, ((0, 2), (2, 8), (3, 32))),
        "cotangent": bell_draw(seeds[1], (BATCH, LEV, LAT, LON, C), 1.0, 6.0, ((0, 2), (2, 8), (3, 32))),
        "qkv_plain": bell_draw(seeds[2], (C, 3 * C), C ** -0.5, 0.3125, ((1, 2),)),
        "proj_plain": bell_draw(seeds[3], (C, C), C ** -0.5, 0.3125),
        "bias_plain": draw_bias_plain(jax.random.fold_in(seeds[8], 71), 0),
        "qkv_shift": bell_draw(seeds[5], (C, 3 * C), C ** -0.5, 0.3125, ((1, 2),)),
        "proj_shift": bell_draw(seeds[6], (C, C), C ** -0.5, 0.3125),
        "bias_shift": draw_bias_shift(jax.random.fold_in(seeds[8], 71), 0),
    }


def to_windows(grid):
    batch, levels, rows, cols, width = grid.shape
    split = grid.reshape(batch, levels // WLEV, WLEV, rows // WLAT, WLAT, cols // WLON, WLON, width)
    split = split.transpose(0, 1, 3, 5, 2, 4, 6, 7)
    return split.reshape(batch, levels // WLEV, rows // WLAT, cols // WLON, WLEV * WLAT * WLON, width)

def from_windows(windowed):
    batch, lev_n, lat_n, lon_n, tokens, width = windowed.shape
    split = windowed.reshape(batch, lev_n, lat_n, lon_n, WLEV, WLAT, WLON, width)
    split = split.transpose(0, 1, 4, 2, 5, 3, 6, 7)
    return split.reshape(batch, lev_n * WLEV, lat_n * WLAT, lon_n * WLON, width)

def expand_bias(table):
    lev_n, lat_n = (table.shape[0], table.shape[1])
    shaped = table.astype(jnp.float32).reshape(lev_n, lat_n, HEADS, WLEV, WLEV, WLAT, WLAT, 2 * WLON - 1)
    offsets = jnp.arange(WLON)
    relative = jnp.arange(2 * WLON - 1)
    picker = (relative[None, None, :] == offsets[:, None, None] - offsets[None, :, None] + WLON - 1).astype(jnp.float32)
    full_bias = jnp.einsum('nmhabcdr,xyr->nmhacxbdy', shaped, picker)
    tokens = WLEV * WLAT * WLON
    return full_bias.reshape(lev_n, lat_n, HEADS, tokens, tokens)

def attend(windowed, w_qkv, w_proj, bias, allowed):
    width = windowed.shape[-1]
    head_size = width // HEADS
    scale = 1.0 / head_size ** 0.5
    leading = windowed.shape[:-1]
    as_float = windowed.astype(jnp.float32)
    mean_val = lax.optimization_barrier(jnp.mean(as_float, axis=-1, keepdims=True))
    mean_removed = as_float - mean_val
    reciprocal_scale = lax.rsqrt(lax.optimization_barrier(jnp.mean(mean_removed * mean_removed, axis=-1, keepdims=True)) + 1e-05)
    standardized_input = mean_removed * reciprocal_scale
    normalized_input = standardized_input.astype(jnp.bfloat16)
    qkv_rows = jnp.dot(normalized_input.reshape(-1, width), w_qkv, preferred_element_type=jnp.float32).astype(jnp.bfloat16)
    qkv_rows = qkv_rows.reshape(leading + (3, HEADS, head_size))
    query_matrix = qkv_rows[..., 0, :, :]
    key_matrix = qkv_rows[..., 1, :, :]
    value_matrix = qkv_rows[..., 2, :, :]
    scores = jnp.einsum('...qhd,...khd->...hqk', query_matrix.astype(jnp.float32), key_matrix.astype(jnp.float32)) * scale + bias
    scores = jnp.where(allowed, scores, -1e+30)
    row_max = lax.optimization_barrier(jnp.max(scores, axis=-1, keepdims=True))
    expo = jnp.exp(scores - row_max)
    attention_weights_matrix = expo / lax.optimization_barrier(jnp.sum(expo, axis=-1, keepdims=True))
    weights_bfloat = attention_weights_matrix.astype(jnp.bfloat16)
    attended_values = jnp.einsum('...hqk,...khd->...qhd', weights_bfloat.astype(jnp.float32), value_matrix.astype(jnp.float32))
    attended_values = attended_values.astype(jnp.bfloat16).reshape(leading + (width,))
    projected = jnp.dot(attended_values.reshape(-1, width), w_proj, preferred_element_type=jnp.float32).reshape(leading + (width,))
    block_output = (projected + as_float).astype(jnp.bfloat16)
    return (block_output, (standardized_input, reciprocal_scale, query_matrix, key_matrix, value_matrix, attention_weights_matrix, weights_bfloat, attended_values))

def backprop(grad_out, stored_residuals, w_qkv, w_proj):
    standardized_input, reciprocal_scale, query_matrix, key_matrix, value_matrix, attention_weights_matrix, weights_bfloat, attended_values = stored_residuals
    width = grad_out.shape[-1]
    head_size = width // HEADS
    scale = 1.0 / head_size ** 0.5
    leading = grad_out.shape[:-1]
    flat_grad = grad_out.reshape(-1, width)
    grad_proj = jnp.dot(attended_values.reshape(-1, width).T, flat_grad, preferred_element_type=jnp.float32)
    grad_mixed = jnp.dot(flat_grad, w_proj.T, preferred_element_type=jnp.float32).astype(jnp.bfloat16)
    grad_mixed = grad_mixed.reshape(leading + (HEADS, head_size))
    grad_probs = jnp.einsum('...qhd,...khd->...hqk', grad_mixed.astype(jnp.float32), value_matrix.astype(jnp.float32))
    inner = lax.optimization_barrier(jnp.sum(attention_weights_matrix * grad_probs, axis=-1, keepdims=True))
    grad_scores = (attention_weights_matrix * (grad_probs - inner)).astype(jnp.bfloat16).astype(jnp.float32)
    grad_values = jnp.einsum('...hqk,...qhd->...khd', weights_bfloat.astype(jnp.float32), grad_mixed.astype(jnp.float32)).astype(jnp.bfloat16)
    grad_query = (jnp.einsum('...hqk,...khd->...qhd', grad_scores, key_matrix.astype(jnp.float32)) * scale).astype(jnp.bfloat16)
    grad_keys = (jnp.einsum('...hqk,...qhd->...khd', grad_scores, query_matrix.astype(jnp.float32)) * scale).astype(jnp.bfloat16)
    grad_qkv = jnp.stack([grad_query, grad_keys, grad_values], axis=-3).reshape(-1, 3 * width)
    normalized_gradient = jnp.dot(grad_qkv, w_qkv.T, preferred_element_type=jnp.float32).reshape(leading + (width,))
    average_gradient = lax.optimization_barrier(jnp.mean(normalized_gradient, axis=-1, keepdims=True))
    average_product = lax.optimization_barrier(jnp.mean(normalized_gradient * standardized_input, axis=-1, keepdims=True))
    input_gradient = reciprocal_scale * (normalized_gradient - average_gradient - standardized_input * average_product)
    return ((grad_out.astype(jnp.float32) + input_gradient).astype(jnp.bfloat16), grad_proj)

def shifted_mask():
    lev_n = LEV // WLEV
    lat_n = LAT // WLAT
    lev_label = (jnp.arange(LEV) >= LEV - WLEV // 2).astype(jnp.int32)
    lat_label = (jnp.arange(LAT) >= LAT - WLAT // 2).astype(jnp.int32)
    grid = lev_label[:, None] * 2 + lat_label[None, :]
    grid = grid.reshape(lev_n, WLEV, lat_n, WLAT).transpose(0, 2, 1, 3)
    grid = jnp.broadcast_to(grid[..., None], (lev_n, lat_n, WLEV, WLAT, WLON)).reshape(lev_n, lat_n, WLEV * WLAT * WLON)
    return grid[..., :, None] == grid[..., None, :]

def plain_mask():
    tokens = WLEV * WLAT * WLON
    return jnp.ones((LEV // WLEV, LAT // WLAT, tokens, tokens), dtype=bool)

def forward_block(grid, w_qkv, w_proj, table, allowed):
    windowed = to_windows(grid).transpose(2, 0, 1, 3, 4, 5)
    bias = expand_bias(table).transpose(1, 0, 2, 3, 4)
    allow_t = allowed.transpose(1, 0, 2, 3)

    def per_band(inputs):
        band, band_bias, band_allow = inputs
        block_output, stored_residuals = attend(band, w_qkv, w_proj, band_bias[None, :, None], band_allow[None, :, None, None])
        return block_output
    outputs = lax.map(per_band, (windowed, bias, allow_t))
    return from_windows(outputs.transpose(1, 2, 0, 3, 4, 5))

def backward_block(grid, grad_grid, w_qkv, w_proj, table, allowed):
    windowed = to_windows(grid).transpose(2, 0, 1, 3, 4, 5)
    grad_windows = to_windows(grad_grid).transpose(2, 0, 1, 3, 4, 5)
    bias = expand_bias(table).transpose(1, 0, 2, 3, 4)
    allow_t = allowed.transpose(1, 0, 2, 3)

    def per_band(inputs):
        band, band_bias, band_allow, band_grad = inputs
        block_output, stored_residuals = attend(band, w_qkv, w_proj, band_bias[None, :, None], band_allow[None, :, None, None])
        return backprop(band_grad, stored_residuals, w_qkv, w_proj)
    grads, grad_projs = lax.map(per_band, (windowed, bias, allow_t, grad_windows))
    return (from_windows(grads.transpose(1, 2, 0, 3, 4, 5)), lax.optimization_barrier(jnp.sum(grad_projs, axis=0)))

def reference(field, cotangent, qkv_plain, proj_plain, bias_plain, qkv_shift, proj_shift, bias_shift):
    forward_roll = (-(WLEV // 2), -(WLAT // 2), -(WLON // 2))
    back_roll = (WLEV // 2, WLAT // 2, WLON // 2)
    allow_plain = plain_mask()
    allow_shift = shifted_mask()
    first = forward_block(field, qkv_plain, proj_plain, bias_plain, allow_plain)
    shifted = jnp.roll(first, forward_roll, axis=(1, 2, 3))
    second = forward_block(shifted, qkv_shift, proj_shift, bias_shift, allow_shift)
    out_field = jnp.roll(second, back_roll, axis=(1, 2, 3))
    grad_second = jnp.roll(cotangent, forward_roll, axis=(1, 2, 3))
    grad_shifted, grad_proj_b = backward_block(shifted, grad_second, qkv_shift, proj_shift, bias_shift, allow_shift)
    grad_first = jnp.roll(grad_shifted, back_roll, axis=(1, 2, 3))
    grad_field, grad_proj_a = backward_block(field, grad_first, qkv_plain, proj_plain, bias_plain, allow_plain)
    return (out_field, grad_field, grad_proj_a.astype(jnp.bfloat16), grad_proj_b.astype(jnp.bfloat16))
```

```python
import functools

import jax
import jax.numpy as jnp
import numpy as np
from jax import lax
from jax.experimental import pallas as pl
from jax.experimental.pallas import tpu as pltpu
from jax.sharding import PartitionSpec as P

HEADS = 12
HEAD = 32
C = 384
LEV = 2
WLAT = 12
WLON = 6
TOKENS = LEV * WLAT * WLON
QUAD = 48
GROUPS = 3
PER = HEADS // GROUPS
REL = 2 * WLON - 1
CHUNK = WLAT * REL
MESH = pl.DeviceIdType.MESH
F32 = jnp.float32
BF16 = jnp.bfloat16


def nn(a, b):
    return lax.dot_general(a, b, (((1,), (0,)), ((), ())), preferred_element_type=F32)


def nt(a, b):
    return lax.dot_general(a, b, (((1,), (1,)), ((), ())), preferred_element_type=F32)


def token(h, w, z):
    return (h * WLON + w) * LEV + z


def constants():
    gather = np.zeros((TOKENS, 4 * QUAD), np.float32)
    pick = np.zeros((TOKENS, 256), np.float32)
    for h in range(WLAT):
        for w in range(WLON):
            for z in range(LEV):
                slot = (h // 6) * 2 + w // 3
                inner = ((h % 6) * 3 + w % 3) * 2 + (1 - z)
                gather[token(h, w, z), slot * QUAD + inner] = 1
                pick[token(h, w, z), z * 127 + h * REL + WLON - 1 - w] = 1
    scatter = np.zeros((4 * QUAD, TOKENS), np.float32)
    for h in range(WLAT):
        for w in range(WLON):
            for z in range(LEV):
                slot = (h // 6) * 2 + w // 3
                scatter[slot * QUAD + ((h % 6) * 3 + w % 3) * 2 + z, token(h, w, z)] = 1
    return gather, scatter, pick


def kernel(
    sizes,
    field,
    cot,
    wp_half,
    ws_half,
    proj_p,
    proj_s,
    tab_p,
    tab_s,
    gather,
    scatter,
    pick,
    out_field,
    out_grad,
    gp_p,
    gp_s,
    wp,
    ws,
    xf,
    quads,
    xhat_p,
    rstd_p,
    xhat_s,
    rstd_s,
    s2f,
    dy2f,
    qkv_p,
    kvt_p,
    qkv_s,
    kvt_s,
    probs_p,
    ot_p,
    ot_s,
    dqkv,
    dqt,
    bias_p,
    bias_s,
    tabf,
    spread,
    send,
    recv,
    halo_ss,
    halo_rs,
    own_sem,
    w_ss,
    w_rs,
    f_ss,
    f_rs,
):
    n_lat, n_lon, n_dp = sizes
    lat, lon, dp = lax.axis_index("lat"), lax.axis_index("lon"), lax.axis_index("dp")
    core = lax.rem(lat, 2)
    sibling = (lat + 1 - 2 * core, lon, dp)
    across = (lat, lax.rem(lon + n_lon // 2, n_lon), 1 - dp)

    def near(dlat, dlon):
        return (
            lax.rem(lat + dlat + n_lat, n_lat),
            lax.rem(lon + dlon + n_lon, n_lon),
            dp,
        )

    greet = [sibling, across]
    greet += [near(a, b) for a, b in ((1, 0), (0, 1), (1, 1), (-1, 0), (0, -1), (-1, -1))]
    barrier = pltpu.get_barrier_semaphore()
    for device in greet:
        pl.semaphore_signal(barrier, inc=1, device_id=device, device_id_type=MESH)
    own = [
        pltpu.make_async_copy(wp_half, wp.at[dp], own_sem.at[0]),
        pltpu.make_async_copy(ws_half, ws.at[dp], own_sem.at[1]),
    ]
    for copy in own:
        copy.start()
    pl.semaphore_wait(barrier, len(greet))

    rows = pl.ds(pl.multiple_of(core * 288, 32), 288)

    def weights_across(half, full, i):
        return pltpu.make_async_remote_copy(
            half.at[rows],
            full.at[dp, rows],
            w_ss.at[i],
            w_rs.at[i],
            device_id=across,
            device_id_type=MESH,
        )

    def weights_beside(full, i):
        part = full.at[1 - dp, rows]
        return pltpu.make_async_remote_copy(
            part, part, f_ss.at[i], f_rs.at[i], device_id=sibling, device_id_type=MESH
        )

    first = [weights_across(wp_half, wp, 0), weights_across(ws_half, ws, 1)]
    for copy in first:
        copy.start()
    beside = [weights_beside(wp, 0), weights_beside(ws, 1)]

    def halo(i, by):
        kept = 3 if by < 0 else 0
        copies = []
        for slot in range(4):
            if slot == kept:
                recv[i, 3 - slot] = send[i, slot]
                continue
            a, b = divmod(slot, 2)
            moves = 0 if by < 0 else 1
            copies.append(
                pltpu.make_async_remote_copy(
                    send.at[i, slot],
                    recv.at[i, 3 - slot],
                    halo_ss.at[i, slot],
                    halo_rs.at[i, 3 - slot],
                    device_id=near(by if a == moves else 0, by if b == moves else 0),
                    device_id_type=MESH,
                )
            )
        for copy in copies:
            copy.start()
        return copies

    def arrived(i, copies):
        for copy in copies:
            copy.wait_recv()
        return nn(gather[...], recv[i].reshape(4 * QUAD, C))

    def to_quads(i, x):
        send[i] = nn(scatter[...], x).astype(BF16).reshape(4, QUAD, C)

    quads[...] = jnp.zeros_like(quads)
    for h in range(WLAT):
        for w in range(WLON):
            at = ((h // 6) * 2 + w // 3) * QUAD + ((h % 6) * 3 + w % 3) * 2
            quads[at : at + 2, :] = cot[h * WLON + w].astype(F32)
    send[0] = quads[...].astype(BF16).reshape(4, QUAD, C)
    halo_cot = halo(0, -1)

    for i in range(WLAT * WLON):
        xf[2 * i : 2 * i + 2, :] = field[i].astype(F32)

    def norm(x, xhat, rstd):
        mean = jnp.mean(x, axis=-1, keepdims=True)
        centred = x - mean
        r = lax.rsqrt(jnp.mean(centred * centred, axis=-1, keepdims=True) + 1e-5)
        y = centred * r
        xhat[...] = y
        rstd[...] = r
        return y.astype(BF16)

    lane256 = lax.broadcasted_iota(jnp.int32, (16, 256), 1)

    def expand(tab, bias, hide):
        tabf[...] = jnp.zeros_like(tabf)
        tabf[0:HEADS, 0 : 4 * WLAT * CHUNK] = tab[...].astype(F32)

        def row(h, carry):
            for za in range(LEV):
                parts = []
                for zb in range(LEV):
                    c = (za * 2 + zb) * WLAT + h
                    tile = c + c // 32
                    off = 4 * lax.rem(c, 32)
                    window = tabf[:, pl.ds(pl.multiple_of(tile * 128, 128), 256)]
                    parts.append(pltpu.roll(window, lax.rem(256 + 127 * zb - off, 256), 1))
                for w in range(WLON):
                    low, high = parts
                    if w:
                        low = pltpu.roll(low, 256 - w, 1)
                        high = pltpu.roll(high, 256 - w, 1)
                    at = pl.multiple_of((h * WLON + w) * 32 + za * 16, 16)
                    both = jnp.where(lane256 < 127, low, high)
                    spread[0, pl.ds(at, 16), :] = both[:, :128]
                    spread[1, pl.ds(at, 16), :] = both[:, 128:]
            return carry

        lax.fori_loop(0, WLAT, row, 0)
        for head in range(HEADS):
            lanes = [spread[half, pl.ds(head, TOKENS, stride=16), :] for half in range(2)]
            table = jnp.concatenate(lanes, axis=1).astype(BF16)
            full = nt(pick[...], table)
            bias[head] = full if hide is None else full + hide

    lane = lax.broadcasted_iota(jnp.int32, (TOKENS, 128), 1) // HEAD

    def by_head(x):
        zero = jnp.zeros_like(x)
        return jnp.concatenate([jnp.where(lane == j, x, zero) for j in range(PER)], axis=0)

    def own_lanes(x):
        total = jnp.where(lane == 0, x[0:TOKENS], 0.0)
        for j in range(1, PER):
            total += jnp.where(lane == j, x[j * TOKENS : (j + 1) * TOKENS], 0.0)
        return total

    scale = 1.0 / HEAD**0.5

    def project(n, full, qkv, kvt):
        w = full[...].reshape(3 * C, C)
        qkv[...] = nt(n, w).astype(BF16)
        kvt[...] = nt(w[C:], n).astype(BF16)

    def softmax(g, qkv, bias):
        q = qkv[:, g * 128 : (g + 1) * 128]
        k = qkv[:, C + g * 128 : C + (g + 1) * 128]
        s = nt(by_head(k), q).reshape(PER, TOKENS, TOKENS) * scale
        s = s + bias[g * PER : (g + 1) * PER]
        e = jnp.exp(s - jnp.max(s, axis=1, keepdims=True))
        return e / jnp.sum(e, axis=1, keepdims=True)

    def values(g, p, kvt, ot):
        for j in range(PER):
            at = g * 128 + j * HEAD
            vt = kvt[C + at : C + at + HEAD, :]
            ot[at : at + HEAD, :] = nn(vt, p[j]).astype(BF16)

    def grads(g, p, pb, do, qkv, kvt):
        cols = slice(g * 128, (g + 1) * 128)
        q = qkv[:, cols]
        v = qkv[:, 2 * C + g * 128 : 2 * C + (g + 1) * 128]
        dog = do[:, cols]
        dp_ = nt(by_head(v), dog).reshape(PER, TOKENS, TOKENS)
        inner = jnp.sum(p * dp_, axis=1, keepdims=True)
        ds = (p * (dp_ - inner)).astype(BF16)
        dv = own_lanes(nn(pb.reshape(PER * TOKENS, TOKENS), dog))
        dk = own_lanes(nn(ds.reshape(PER * TOKENS, TOKENS), q)) * scale
        dqkv[:, 2 * C + g * 128 : 2 * C + (g + 1) * 128] = dv.astype(BF16)
        dqkv[:, C + g * 128 : C + (g + 1) * 128] = dk.astype(BF16)
        for j in range(PER):
            at = g * 128 + j * HEAD
            dqt[at : at + HEAD, :] = nn(kvt[at : at + HEAD, :], ds[j]) * scale

    def input_grad(dy, full, xhat, rstd):
        dqkv[:, 0:C] = dqt[...].T.astype(BF16)
        dn = nn(dqkv[...], full[...].reshape(3 * C, C))
        xh = xhat[...]
        mean = jnp.mean(dn, axis=-1, keepdims=True)
        product = jnp.mean(dn * xh, axis=-1, keepdims=True)
        return (dy + rstd[...] * (dn - mean - xh * product)).astype(BF16)

    def output(x, ot, proj):
        o = ot[...].astype(F32).T.astype(BF16)
        return (x + nn(o, proj[...])).astype(BF16)

    n1 = norm(xf[...], xhat_p, rstd_p)
    expand(tab_p, bias_p, None)
    own[0].wait()
    first[0].wait_recv()
    beside[0].start()
    beside[0].wait_recv()
    project(n1, wp, qkv_p, kvt_p)
    for g in range(GROUPS):
        p = softmax(g, qkv_p, bias_p)
        probs_p[g * PER : (g + 1) * PER] = p
        values(g, p.astype(BF16), kvt_p, ot_p)
    h1 = output(xf[...], ot_p, proj_p)
    to_quads(1, h1)
    halo_h1 = halo(1, -1)

    key = lax.broadcasted_iota(jnp.int32, (TOKENS, TOKENS), 0)
    query = lax.broadcasted_iota(jnp.int32, (TOKENS, TOKENS), 1)
    edge = jnp.where(lat == n_lat - 1, TOKENS // 2, TOKENS)
    same = ((key & 1) == (query & 1)) & ((key >= edge) == (query >= edge))
    expand(tab_s, bias_s, jnp.where(same, 0.0, -1e30))
    own[1].wait()
    first[1].wait_recv()
    beside[1].start()
    dy2 = arrived(0, halo_cot)
    dy2f[...] = dy2
    do2 = nt(dy2.astype(BF16), proj_s[...]).astype(BF16)
    beside[1].wait_recv()

    s2 = arrived(1, halo_h1)
    s2f[...] = s2
    n2 = norm(s2, xhat_s, rstd_s)
    project(n2, ws, qkv_s, kvt_s)
    for g in range(GROUPS):
        p = softmax(g, qkv_s, bias_s)
        pb = p.astype(BF16)
        values(g, pb, kvt_s, ot_s)
        grads(g, p, pb, do2, qkv_s, kvt_s)
    ds2 = input_grad(dy2f[...], ws, xhat_s, rstd_s)
    to_quads(2, ds2)
    halo_g1 = halo(2, 1)

    y2 = output(s2f[...], ot_s, proj_s)
    to_quads(3, y2)
    halo_out = halo(3, 1)
    gp_s[...] = nn(ot_s[...], dy2f[...].astype(BF16))

    g1 = arrived(2, halo_g1)
    g1b = g1.astype(BF16)
    gp_p[...] = nn(ot_p[...], g1b)
    do1 = nt(g1b, proj_p[...]).astype(BF16)
    for g in range(GROUPS):
        p = probs_p[g * PER : (g + 1) * PER]
        grads(g, p, p.astype(BF16), do1, qkv_p, kvt_p)
    xf[...] = input_grad(g1, wp, xhat_p, rstd_p).astype(F32)
    for i in range(WLAT * WLON):
        out_grad[i] = xf[2 * i : 2 * i + 2, :].astype(BF16)
    s2f[...] = arrived(3, halo_out)
    for i in range(WLAT * WLON):
        out_field[i] = s2f[2 * i : 2 * i + 2, :].astype(BF16)

    for copies in (halo_cot, halo_h1, halo_g1, halo_out, first, beside):
        for copy in copies:
            copy.wait_send()


def body(sizes, field, cotangent, qkv_plain, proj_plain, bias_plain, qkv_shift, proj_shift, bias_shift):
    def rows(x):
        return x.transpose(0, 2, 3, 1, 4).reshape(WLAT * WLON, LEV, C)

    gather, scatter, pick = constants()
    operands = (
        rows(field),
        rows(cotangent),
        qkv_plain.T,
        qkv_shift.T,
        proj_plain,
        proj_shift,
        bias_plain.reshape(HEADS, -1),
        bias_shift.reshape(HEADS, -1),
        jnp.asarray(gather, BF16),
        jnp.asarray(scatter, BF16),
        jnp.asarray(pick, BF16),
    )
    vmem = pl.BlockSpec(memory_space=pltpu.VMEM)
    hbm = pl.BlockSpec(memory_space=pl.ANY)
    grid_shape = jax.ShapeDtypeStruct((WLAT * WLON, LEV, C), BF16)
    square = jax.ShapeDtypeStruct((C, C), F32)
    tokens_f32 = pltpu.VMEM((TOKENS, C), F32)
    row_stat = pltpu.VMEM((TOKENS, 1), F32)
    full_bias = pltpu.VMEM((HEADS, TOKENS, TOKENS), F32)
    out_field, out_grad, gp_p, gp_s = pl.pallas_call(
        functools.partial(kernel, sizes),
        out_shape=(grid_shape, grid_shape, square, square),
        in_specs=[vmem, vmem, hbm, hbm] + [vmem] * 7,
        out_specs=(vmem, vmem, vmem, vmem),
        scratch_shapes=[
            pltpu.VMEM((2, 3 * C // 2, C), BF16),
            pltpu.VMEM((2, 3 * C // 2, C), BF16),
            tokens_f32,
            pltpu.VMEM((4 * QUAD, C), F32),
            tokens_f32,
            row_stat,
            tokens_f32,
            row_stat,
            tokens_f32,
            tokens_f32,
            pltpu.VMEM((TOKENS, 3 * C), BF16),
            pltpu.VMEM((2 * C, TOKENS), BF16),
            pltpu.VMEM((TOKENS, 3 * C), BF16),
            pltpu.VMEM((2 * C, TOKENS), BF16),
            full_bias,
            pltpu.VMEM((C, TOKENS), BF16),
            pltpu.VMEM((C, TOKENS), BF16),
            pltpu.VMEM((TOKENS, 3 * C), BF16),
            pltpu.VMEM((C, TOKENS), F32),
            full_bias,
            full_bias,
            pltpu.VMEM((16, 6400), F32),
            pltpu.VMEM((2, TOKENS * 16, 128), F32),
            pltpu.VMEM((4, 4, QUAD, C), BF16),
            pltpu.VMEM((4, 4, QUAD, C), BF16),
            pltpu.SemaphoreType.DMA((4, 4)),
            pltpu.SemaphoreType.DMA((4, 4)),
            pltpu.SemaphoreType.DMA((2,)),
            pltpu.SemaphoreType.DMA((2,)),
            pltpu.SemaphoreType.DMA((2,)),
            pltpu.SemaphoreType.DMA((2,)),
            pltpu.SemaphoreType.DMA((2,)),
        ],
        compiler_params=pltpu.CompilerParams(
            collective_id=0, has_side_effects=True, vmem_limit_bytes=48 * 2**20
        ),
    )(*operands)

    def grid(x):
        return x.reshape(1, WLAT, WLON, LEV, C).transpose(0, 3, 1, 2, 4)

    gp_p, gp_s = lax.psum((gp_p.astype(BF16), gp_s.astype(BF16)), ("lat", "lon", "dp"))
    return grid(out_field), grid(out_grad), gp_p, gp_s


def solution(mesh):
    sizes = tuple(mesh.shape[a] for a in ("lat", "lon", "dp"))
    grid = P("dp", None, "lat", "lon", None)
    table = P(None, "lat", None, None)
    columns = P(None, "dp")
    return jax.shard_map(
        functools.partial(body, sizes),
        mesh=mesh,
        in_specs=(grid, grid, columns, P(), table, columns, P(), table),
        out_specs=(grid, grid, P(), P()),
        check_vma=False,
    )
```

```python
import functools

import jax
import jax.numpy as jnp
import numpy as np
from jax import lax
from jax.experimental import pallas as pl
from jax.experimental.pallas import tpu as pltpu
from jax.sharding import PartitionSpec as P

HEADS = 12
HEAD = 32
C = 384
LEV = 2
WLAT = 12
WLON = 6
TOKENS = LEV * WLAT * WLON
QUAD = 48
GROUPS = 3
PER = HEADS // GROUPS
REL = 2 * WLON - 1
CHUNK = WLAT * REL
MESH = pl.DeviceIdType.MESH
F32 = jnp.float32
BF16 = jnp.bfloat16


def nn(a, b):
    return lax.dot_general(a, b, (((1,), (0,)), ((), ())), preferred_element_type=F32)


def nt(a, b):
    return lax.dot_general(a, b, (((1,), (1,)), ((), ())), preferred_element_type=F32)


def token(h, w, z):
    return (h * WLON + w) * LEV + z


def constants():
    gather = np.zeros((TOKENS, 4 * QUAD), np.float32)
    pick = np.zeros((TOKENS, 256), np.float32)
    for h in range(WLAT):
        for w in range(WLON):
            for z in range(LEV):
                slot = (h // 6) * 2 + w // 3
                inner = ((h % 6) * 3 + w % 3) * 2 + (1 - z)
                gather[token(h, w, z), slot * QUAD + inner] = 1
                pick[token(h, w, z), z * 127 + h * REL + WLON - 1 - w] = 1
    scatter = np.zeros((4 * QUAD, TOKENS), np.float32)
    for h in range(WLAT):
        for w in range(WLON):
            for z in range(LEV):
                slot = (h // 6) * 2 + w // 3
                scatter[slot * QUAD + ((h % 6) * 3 + w % 3) * 2 + z, token(h, w, z)] = 1
    return gather, scatter, pick


OPERANDS = (
    ("field", (WLAT * WLON, LEV, C)),
    ("cot", (WLAT * WLON, LEV, C)),
    ("wp_half", None),
    ("ws_half", None),
    ("tab_p", (HEADS, 4 * WLAT * CHUNK)),
    ("tab_s", (HEADS, 4 * WLAT * CHUNK)),
    ("scatter", (4 * QUAD, TOKENS)),
    ("gather", (TOKENS, 4 * QUAD)),
    ("pick", (TOKENS, 256)),
    ("proj_p", (C, C)),
    ("proj_s", (C, C)),
)
LOADED = [name for name, shape in OPERANDS if shape is not None]


def scratch(plan):
    xy, z, rows = plan
    tokens_f32 = pltpu.VMEM((TOKENS, C), F32)
    row_stat = pltpu.VMEM((TOKENS, 1), F32)
    full_bias = pltpu.VMEM((HEADS, TOKENS, TOKENS), F32)
    weights = pltpu.VMEM((2, 3 * C // 2, C), BF16)
    qkv = pltpu.VMEM((TOKENS, 3 * C), BF16)
    kvt = pltpu.VMEM((2 * C, TOKENS), BF16)
    heads_t = pltpu.VMEM((C, TOKENS), BF16)
    dma = pltpu.SemaphoreType.DMA
    named = {name: pltpu.VMEM(shape, BF16) for name, shape in OPERANDS if shape is not None}
    named |= dict(
        load_sem=dma((len(OPERANDS),)),
        wp=weights,
        ws=weights,
        xf=tokens_f32,
        quads=pltpu.VMEM((4 * QUAD, C), F32),
        xhat_p=tokens_f32,
        rstd_p=row_stat,
        xhat_s=tokens_f32,
        rstd_s=row_stat,
        s2f=tokens_f32,
        dy2f=tokens_f32,
        qkv_p=qkv,
        kvt_p=kvt,
        qkv_s=qkv,
        kvt_s=kvt,
        probs_p=full_bias,
        probs_s=full_bias,
        ot_p=heads_t,
        ot_s=heads_t,
        ot_r=heads_t,
        dqkv=qkv,
        dqt=pltpu.VMEM((C, TOKENS), F32),
        bias_p=full_bias,
        bias_s=full_bias,
        tabf=pltpu.VMEM((16, 6400), F32),
        spread=pltpu.VMEM((2, TOKENS * 16, 128), F32),
        send=pltpu.VMEM((5, 4, QUAD, C), BF16),
        recv=pltpu.VMEM((5, 4, QUAD, C), BF16),
        halo_ss=dma((5, 4)),
        halo_rs=dma((5, 4)),
        w_ss=dma((2,)),
        w_rs=dma((2,)),
        f_ss=dma((2,)),
        f_rs=dma((2,)),
        part=pltpu.VMEM((2, C, C), F32),
        part16=pltpu.VMEM((2, C, C), BF16),
        half_in=pltpu.VMEM((2, C // 2, C), BF16),
        chunks=pltpu.VMEM((2, C // 2 // rows, rows, C), BF16),
        xy_in=pltpu.VMEM((2, xy, rows, C), BF16),
        z_in=pltpu.VMEM((2, z, rows, C), BF16),
        final=pltpu.VMEM((2, C // rows, rows, C), BF16),
        c_ss=dma((2,)),
        c_rs=dma((2,)),
        xy_ss=dma((2, xy)),
        xy_rs=dma((2, xy)),
        z_ss=dma((2, z)),
        z_rs=dma((2, z)),
        fin_ss=dma((2, 2 * xy)),
        fin_rs=dma((2, C // rows)),
    )
    return named


def kernel(sizes, plan, names, *refs):
    run(sizes, plan, **dict(zip(names, refs)))


def run(
    sizes,
    plan,
    out_field,
    out_grad,
    gp_p,
    gp_s,
    wp,
    ws,
    xf,
    quads,
    xhat_p,
    rstd_p,
    xhat_s,
    rstd_s,
    s2f,
    dy2f,
    qkv_p,
    kvt_p,
    qkv_s,
    kvt_s,
    probs_p,
    probs_s,
    ot_p,
    ot_s,
    ot_r,
    dqkv,
    dqt,
    bias_p,
    bias_s,
    tabf,
    spread,
    send,
    recv,
    halo_ss,
    halo_rs,
    w_ss,
    w_rs,
    f_ss,
    f_rs,
    part,
    part16,
    half_in,
    chunks,
    xy_in,
    z_in,
    final,
    c_ss,
    c_rs,
    xy_ss,
    xy_rs,
    z_ss,
    z_rs,
    fin_ss,
    fin_rs,
    load_sem,
    **local,
):
    n_lat, n_lon, n_dp = sizes
    lat, lon, dp = lax.axis_index("lat"), lax.axis_index("lon"), lax.axis_index("dp")
    core = lax.rem(lat, 2)
    sibling = (lat + 1 - 2 * core, lon, dp)
    across = (lat, lax.rem(lon + n_lon // 2, n_lon), 1 - dp)

    def near(dlat, dlon):
        return (
            lax.rem(lat + dlat + n_lat, n_lat),
            lax.rem(lon + dlon + n_lon, n_lon),
            dp,
        )

    xy, n_z, chunk_rows = plan
    n_y = n_lat // 2
    n_own = C // 2 // chunk_rows
    z = lax.rem(lon, n_z)
    spot = (lon // n_z + 2 * dp) * n_y + lat // 2

    def at_spot(e, c):
        x = e // n_y
        return (lax.rem(e, n_y) * 2 + c, lax.rem(x, 2) * n_z + z, x // 2)

    def at_z(other):
        return (lat, lon - z + other, dp)

    def peer(d):
        f = lax.rem(spot * 2 + core + d, 2 * xy)
        return at_spot(f // 2, lax.rem(f, 2))

    def each(n, do):
        def step(d, carry):
            do(d)
            return carry

        lax.fori_loop(1, n, step, 0)

    barrier = pltpu.get_barrier_semaphore()

    def greet(device):
        pl.semaphore_signal(barrier, inc=1, device_id=device, device_id_type=MESH)

    each(2 * xy, lambda d: greet(peer(d)))
    around = [(0, 1), (1, 1), (0, -1), (-1, -1)]
    for a, b in around:
        greet(near(a, b))
    each(n_z, lambda d: greet(at_z(lax.rem(z + d, n_z))))

    loads = {}
    for i, (name, shape) in enumerate(OPERANDS):
        source = local[name + "_hbm"]
        target = local[name] if shape else {"wp_half": wp, "ws_half": ws}[name].at[dp]
        loads[name] = pltpu.make_async_copy(source, target, load_sem.at[i])
        loads[name].start()
    wp_half, ws_half = local["wp_half_hbm"], local["ws_half_hbm"]
    field, cot, proj_p, proj_s, tab_p, tab_s, gather, scatter, pick = (
        local[name]
        for name in (
            "field", "cot", "proj_p", "proj_s", "tab_p", "tab_s", "gather", "scatter", "pick"
        )
    )
    pl.semaphore_wait(barrier, 2 * xy - 1 + len(around) + n_z - 1)

    rows = pl.ds(pl.multiple_of(core * 288, 32), 288)

    def weights_across(half, full, i):
        return pltpu.make_async_remote_copy(
            half.at[rows],
            full.at[dp, rows],
            w_ss.at[i],
            w_rs.at[i],
            device_id=across,
            device_id_type=MESH,
        )

    def weights_beside(full, i):
        part = full.at[1 - dp, rows]
        return pltpu.make_async_remote_copy(
            part, part, f_ss.at[i], f_rs.at[i], device_id=sibling, device_id_type=MESH
        )

    first = [weights_across(wp_half, wp, 0), weights_across(ws_half, ws, 1)]
    for copy in first:
        copy.start()
    beside = [weights_beside(wp, 0), weights_beside(ws, 1)]

    def halo(i, by):
        kept = 3 if by < 0 else 0
        copies = []
        for slot in range(4):
            if slot == kept:
                recv[i, 3 - slot] = send[i, slot]
                continue
            a, b = divmod(slot, 2)
            moves = 0 if by < 0 else 1
            copies.append(
                pltpu.make_async_remote_copy(
                    send.at[i, slot],
                    recv.at[i, 3 - slot],
                    halo_ss.at[i, slot],
                    halo_rs.at[i, 3 - slot],
                    device_id=near(by if a == moves else 0, by if b == moves else 0),
                    device_id_type=MESH,
                )
            )
        for copy in copies:
            copy.start()
        return copies

    def arrived(i, copies):
        for copy in copies:
            copy.wait_recv()
        return nn(gather[...], recv[i].reshape(4 * QUAD, C))

    def to_quads(i, x):
        send[i] = nn(scatter[...], x).astype(BF16).reshape(4, QUAD, C)

    loads["cot"].wait()
    quads[...] = jnp.zeros_like(quads)
    for h in range(WLAT):
        for w in range(WLON):
            at = ((h // 6) * 2 + w // 3) * QUAD + ((h % 6) * 3 + w % 3) * 2
            quads[at : at + 2, :] = cot[h * WLON + w].astype(F32)
    send[0] = quads[...].astype(BF16).reshape(4, QUAD, C)
    halo_cot = halo(0, -1)

    loads["field"].wait()
    for i in range(WLAT * WLON):
        xf[2 * i : 2 * i + 2, :] = field[i].astype(F32)

    def norm(x, xhat, rstd):
        mean = jnp.mean(x, axis=-1, keepdims=True)
        centred = x - mean
        r = lax.rsqrt(jnp.mean(centred * centred, axis=-1, keepdims=True) + 1e-5)
        y = centred * r
        xhat[...] = y
        rstd[...] = r
        return y.astype(BF16)

    lane256 = lax.broadcasted_iota(jnp.int32, (16, 256), 1)

    def expand(tab, bias, hide):
        tabf[...] = jnp.zeros_like(tabf)
        tabf[0:HEADS, 0 : 4 * WLAT * CHUNK] = tab[...].astype(F32)

        def row(h, carry):
            for za in range(LEV):
                parts = []
                for zb in range(LEV):
                    c = (za * 2 + zb) * WLAT + h
                    tile = c + c // 32
                    off = 4 * lax.rem(c, 32)
                    window = tabf[:, pl.ds(pl.multiple_of(tile * 128, 128), 256)]
                    parts.append(pltpu.roll(window, lax.rem(256 + 127 * zb - off, 256), 1))
                for w in range(WLON):
                    low, high = parts
                    if w:
                        low = pltpu.roll(low, 256 - w, 1)
                        high = pltpu.roll(high, 256 - w, 1)
                    at = pl.multiple_of((h * WLON + w) * 32 + za * 16, 16)
                    both = jnp.where(lane256 < 127, low, high)
                    spread[0, pl.ds(at, 16), :] = both[:, :128]
                    spread[1, pl.ds(at, 16), :] = both[:, 128:]
            return carry

        lax.fori_loop(0, WLAT, row, 0)
        for head in range(HEADS):
            lanes = [spread[half, pl.ds(head, TOKENS, stride=16), :] for half in range(2)]
            table = jnp.concatenate(lanes, axis=1).astype(BF16)
            full = nt(pick[...], table)
            bias[head] = full if hide is None else full + hide

    lane = lax.broadcasted_iota(jnp.int32, (TOKENS, 128), 1) // HEAD

    def by_head(x):
        zero = jnp.zeros_like(x)
        return jnp.concatenate([jnp.where(lane == j, x, zero) for j in range(PER)], axis=0)

    def own_lanes(x):
        total = jnp.where(lane == 0, x[0:TOKENS], 0.0)
        for j in range(1, PER):
            total += jnp.where(lane == j, x[j * TOKENS : (j + 1) * TOKENS], 0.0)
        return total

    scale = 1.0 / HEAD**0.5

    def project(n, full, qkv, kvt):
        w = full[...].reshape(3 * C, C)
        qkv[...] = nt(n, w).astype(BF16)
        kvt[...] = nt(w[C:], n).astype(BF16)

    def softmax(g, qkv, bias):
        q = qkv[:, g * 128 : (g + 1) * 128]
        k = qkv[:, C + g * 128 : C + (g + 1) * 128]
        s = nt(by_head(k), q).reshape(PER, TOKENS, TOKENS) * scale
        s = s + bias[g * PER : (g + 1) * PER]
        e = jnp.exp(s - jnp.max(s, axis=1, keepdims=True))
        return e / jnp.sum(e, axis=1, keepdims=True)

    def values(g, p, kvt, ot):
        for j in range(PER):
            at = g * 128 + j * HEAD
            vt = kvt[C + at : C + at + HEAD, :]
            ot[at : at + HEAD, :] = nn(vt, p[j]).astype(BF16)

    def grads(g, p, pb, do, qkv, kvt):
        cols = slice(g * 128, (g + 1) * 128)
        q = qkv[:, cols]
        v = qkv[:, 2 * C + g * 128 : 2 * C + (g + 1) * 128]
        dog = do[:, cols]
        dp_ = nt(by_head(v), dog).reshape(PER, TOKENS, TOKENS)
        inner = jnp.sum(p * dp_, axis=1, keepdims=True)
        ds = (p * (dp_ - inner)).astype(BF16)
        dv = own_lanes(nn(pb.reshape(PER * TOKENS, TOKENS), dog))
        dk = own_lanes(nn(ds.reshape(PER * TOKENS, TOKENS), q)) * scale
        dqkv[:, 2 * C + g * 128 : 2 * C + (g + 1) * 128] = dv.astype(BF16)
        dqkv[:, C + g * 128 : C + (g + 1) * 128] = dk.astype(BF16)
        for j in range(PER):
            at = g * 128 + j * HEAD
            dqt[at : at + HEAD, :] = nn(kvt[at : at + HEAD, :], ds[j]) * scale

    def input_grad(dy, full, xhat, rstd):
        dqkv[:, 0:C] = dqt[...].T.astype(BF16)
        dn = nn(dqkv[...], full[...].reshape(3 * C, C))
        xh = xhat[...]
        mean = jnp.mean(dn, axis=-1, keepdims=True)
        product = jnp.mean(dn * xh, axis=-1, keepdims=True)
        return (dy + rstd[...] * (dn - mean - xh * product)).astype(BF16)

    def heads(ot):
        return ot[...].astype(F32).T.astype(BF16)

    def output(x, o, proj):
        return (x + nn(o, proj[...])).astype(BF16)

    def copy_core(m):
        return pltpu.make_async_remote_copy(
            part16.at[m, pl.ds(pl.multiple_of((1 - core) * (C // 2), 64), C // 2)],
            half_in.at[m],
            c_ss.at[m],
            c_rs.at[m],
            device_id=sibling,
            device_id_type=MESH,
        )

    def copy_xy(m, to, sender, ss):
        return pltpu.make_async_remote_copy(
            chunks.at[m, lax.rem(to, n_own)],
            xy_in.at[m, sender],
            xy_ss.at[m, ss],
            xy_rs.at[m, sender],
            device_id=at_spot(to, core),
            device_id_type=MESH,
        )

    def copy_z(m, to, sender, ss):
        return pltpu.make_async_remote_copy(
            z_in.at[m, z],
            z_in.at[m, sender],
            z_ss.at[m, ss],
            z_rs.at[m, sender],
            device_id=at_z(to),
            device_id_type=MESH,
        )

    def copy_final(m, d, index):
        return pltpu.make_async_remote_copy(
            final.at[m, index],
            final.at[m, index],
            fin_ss.at[m, d],
            fin_rs.at[m, index],
            device_id=peer(d),
            device_id_type=MESH,
        )

    owner = spot < n_own
    mine = core * n_own + lax.rem(spot, n_own)

    def sum_start(m, total):
        part[m] = total
        part16[m] = total.astype(BF16)
        copy_core(m).start()

    def sum_xy(m):
        copy_core(m).wait_recv()
        at = pl.ds(pl.multiple_of(core * (C // 2), 64), C // 2)
        both = part[m, at, :] + half_in[m].astype(F32)
        chunks[m] = both.astype(BF16).reshape(n_own, chunk_rows, C)

        def go(d):
            to = lax.rem(spot + d, xy)

            @pl.when(to < n_own)
            def _():
                copy_xy(m, to, spot, d).start()

        each(xy, go)

    def sum_z(m):
        @pl.when(owner)
        def _():
            xy_in[m, spot] = chunks[m, spot]
            each(xy, lambda d: copy_xy(m, spot, lax.rem(spot + d, xy), d).wait_recv())
            z_in[m, z] = jnp.sum(xy_in[m].astype(F32), axis=0).astype(BF16)
            each(n_z, lambda d: copy_z(m, lax.rem(z + d, n_z), z, d).start())

    def sum_back(m):
        @pl.when(owner)
        def _():
            each(n_z, lambda d: copy_z(m, z, lax.rem(z + d, n_z), d).wait_recv())
            final[m, mine] = jnp.sum(z_in[m].astype(F32), axis=0).astype(BF16)
            each(2 * xy, lambda d: copy_final(m, d, mine).start())

    def sum_end(m, out):
        def take(i, carry):
            @pl.when(jnp.logical_not(owner & (i == mine)))
            def _():
                copy_final(m, 1, i).wait_recv()

            return carry

        lax.fori_loop(0, C // chunk_rows, take, 0)
        out[...] = final[m].reshape(C, C)

    def sum_sent(m):
        copy_core(m).wait_send()

        def sent(d):
            to = lax.rem(spot + d, xy)

            @pl.when(to < n_own)
            def _():
                copy_xy(m, to, spot, d).wait_send()

        each(xy, sent)

        @pl.when(owner)
        def _():
            each(n_z, lambda d: copy_z(m, lax.rem(z + d, n_z), z, d).wait_send())
            each(2 * xy, lambda d: copy_final(m, d, mine).wait_send())

    n1 = norm(xf[...], xhat_p, rstd_p)
    loads["tab_p"].wait()
    loads["pick"].wait()
    expand(tab_p, bias_p, None)
    loads["wp_half"].wait()
    first[0].wait_recv()
    beside[0].start()
    beside[0].wait_recv()
    project(n1, wp, qkv_p, kvt_p)
    for g in range(GROUPS):
        p = softmax(g, qkv_p, bias_p)
        probs_p[g * PER : (g + 1) * PER] = p
        values(g, p.astype(BF16), kvt_p, ot_p)
    loads["proj_p"].wait()
    loads["scatter"].wait()
    o1 = heads(ot_p)
    to_quads(1, output(xf[...], o1, proj_p))
    halo_h1 = halo(1, -1)
    to_quads(4, o1)
    halo_o1 = halo(4, -1)

    key = lax.broadcasted_iota(jnp.int32, (TOKENS, TOKENS), 0)
    query = lax.broadcasted_iota(jnp.int32, (TOKENS, TOKENS), 1)
    edge = jnp.where(lat == n_lat - 1, TOKENS // 2, TOKENS)
    same = ((key & 1) == (query & 1)) & ((key >= edge) == (query >= edge))
    loads["tab_s"].wait()
    expand(tab_s, bias_s, jnp.where(same, 0.0, -1e30))
    loads["ws_half"].wait()
    first[1].wait_recv()
    beside[1].start()
    loads["gather"].wait()
    dy2 = arrived(0, halo_cot)
    dy2f[...] = dy2
    loads["proj_s"].wait()
    do2 = nt(dy2.astype(BF16), proj_s[...]).astype(BF16)
    beside[1].wait_recv()

    s2 = arrived(1, halo_h1)
    s2f[...] = s2
    n2 = norm(s2, xhat_s, rstd_s)
    project(n2, ws, qkv_s, kvt_s)
    for g in range(GROUPS):
        p = softmax(g, qkv_s, bias_s)
        probs_s[g * PER : (g + 1) * PER] = p
        values(g, p.astype(BF16), kvt_s, ot_s)
    sum_start(1, nn(ot_s[...], dy2f[...].astype(BF16)))
    for g in range(GROUPS):
        p = probs_s[g * PER : (g + 1) * PER]
        grads(g, p, p.astype(BF16), do2, qkv_s, kvt_s)
        if g == 0:
            sum_xy(1)
            ot_r[...] = arrived(4, halo_o1).T.astype(BF16)
    ds2 = input_grad(dy2f[...], ws, xhat_s, rstd_s)
    sum_start(0, nn(ot_r[...], ds2))
    to_quads(2, ds2)
    halo_g1 = halo(2, 1)

    y2 = output(s2f[...], heads(ot_s), proj_s)
    to_quads(3, y2)
    halo_out = halo(3, 1)
    sum_xy(0)
    sum_z(1)

    g1 = arrived(2, halo_g1)
    do1 = nt(g1.astype(BF16), proj_p[...]).astype(BF16)
    for g in range(GROUPS):
        p = probs_p[g * PER : (g + 1) * PER]
        grads(g, p, p.astype(BF16), do1, qkv_p, kvt_p)
        if g == 1:
            sum_z(0)
    xf[...] = input_grad(g1, wp, xhat_p, rstd_p).astype(F32)
    for i in range(WLAT * WLON):
        out_grad[i] = xf[2 * i : 2 * i + 2, :].astype(BF16)
    s2f[...] = arrived(3, halo_out)
    for i in range(WLAT * WLON):
        out_field[i] = s2f[2 * i : 2 * i + 2, :].astype(BF16)
    sum_back(1)
    sum_back(0)
    for copies in (halo_cot, halo_h1, halo_o1, halo_g1, halo_out, first, beside):
        for copy in copies:
            copy.wait_send()
    sum_end(1, gp_s)
    sum_end(0, gp_p)
    sum_sent(1)
    sum_sent(0)


def body(sizes, field, cotangent, qkv_plain, proj_plain, bias_plain, qkv_shift, proj_shift, bias_shift):
    def rows(x):
        return x.transpose(0, 2, 3, 1, 4).reshape(WLAT * WLON, LEV, C)

    gather, scatter, pick = constants()
    operands = dict(
        field=rows(field),
        cot=rows(cotangent),
        wp_half=qkv_plain.T,
        ws_half=qkv_shift.T,
        proj_p=proj_plain,
        proj_s=proj_shift,
        tab_p=bias_plain.reshape(HEADS, -1),
        tab_s=bias_shift.reshape(HEADS, -1),
        gather=jnp.asarray(gather, BF16),
        scatter=jnp.asarray(scatter, BF16),
        pick=jnp.asarray(pick, BF16),
    )
    n_lat, n_lon, n_dp = sizes
    xy = n_lat // 2 * 2 * n_dp
    owners = max(d for d in (1, 2, 3, 4, 6, 12) if d <= xy)
    plan = (xy, n_lon // 2, C // 2 // owners)
    buffers = scratch(plan)
    vmem = pl.BlockSpec(memory_space=pltpu.VMEM)
    hbm = pl.BlockSpec(memory_space=pl.ANY)
    grid_shape = jax.ShapeDtypeStruct((WLAT * WLON, LEV, C), BF16)
    square = jax.ShapeDtypeStruct((C, C), BF16)
    names = [name + "_hbm" for name, _ in OPERANDS]
    names += ["out_field", "out_grad", "gp_p", "gp_s"] + list(buffers)
    out_field, out_grad, gp_p, gp_s = pl.pallas_call(
        functools.partial(kernel, sizes, plan, names),
        out_shape=(grid_shape, grid_shape, square, square),
        in_specs=[hbm] * len(OPERANDS),
        out_specs=(vmem, vmem, vmem, vmem),
        scratch_shapes=list(buffers.values()),
        compiler_params=pltpu.CompilerParams(
            collective_id=0, has_side_effects=True, vmem_limit_bytes=56 * 2**20
        ),
    )(*[operands[name] for name, _ in OPERANDS])

    def grid(x):
        return x.reshape(1, WLAT, WLON, LEV, C).transpose(0, 3, 1, 2, 4)

    return grid(out_field), grid(out_grad), gp_p, gp_s


def solution(mesh):
    sizes = tuple(mesh.shape[a] for a in ("lat", "lon", "dp"))
    grid = P("dp", None, "lat", "lon", None)
    table = P(None, "lat", None, None)
    columns = P(None, "dp")
    return jax.shard_map(
        functools.partial(body, sizes),
        mesh=mesh,
        in_specs=(grid, grid, columns, P(), table, columns, P(), table),
        out_specs=(grid, grid, P(), P()),
        check_vma=False,
    )
```

```python
import functools

import jax
import jax.numpy as jnp
import numpy as np
from jax import lax
from jax.experimental import pallas as pl
from jax.experimental.pallas import tpu as pltpu
from jax.sharding import PartitionSpec as P

HEADS = 12
HEAD = 32
C = 384
LEV = 2
WLAT = 12
WLON = 6
TOKENS = LEV * WLAT * WLON
QUAD = 48
GROUPS = 3
PER = HEADS // GROUPS
REL = 2 * WLON - 1
CHUNK = WLAT * REL
MESH = pl.DeviceIdType.MESH
F32 = jnp.float32
BF16 = jnp.bfloat16


def nn(a, b):
    return lax.dot_general(a, b, (((1,), (0,)), ((), ())), preferred_element_type=F32)


def nt(a, b):
    return lax.dot_general(a, b, (((1,), (1,)), ((), ())), preferred_element_type=F32)


def token(h, w, z):
    return (h * WLON + w) * LEV + z


def constants():
    gather = np.zeros((TOKENS, 4 * QUAD), np.float32)
    pick = np.zeros((TOKENS, 256), np.float32)
    for h in range(WLAT):
        for w in range(WLON):
            for z in range(LEV):
                slot = (h // 6) * 2 + w // 3
                inner = ((h % 6) * 3 + w % 3) * 2 + (1 - z)
                gather[token(h, w, z), slot * QUAD + inner] = 1
                pick[token(h, w, z), z * 127 + h * REL + WLON - 1 - w] = 1
    scatter = np.zeros((4 * QUAD, TOKENS), np.float32)
    for h in range(WLAT):
        for w in range(WLON):
            for z in range(LEV):
                slot = (h // 6) * 2 + w // 3
                scatter[slot * QUAD + ((h % 6) * 3 + w % 3) * 2 + z, token(h, w, z)] = 1
    return gather, scatter, pick


OPERANDS = (
    ("field", (WLAT * WLON, LEV, C)),
    ("cot", (WLAT * WLON, LEV, C)),
    ("wp_half", None),
    ("ws_half", None),
    ("tab_p", (HEADS, 4 * WLAT * CHUNK)),
    ("tab_s", (HEADS, 4 * WLAT * CHUNK)),
    ("scatter", (4 * QUAD, TOKENS)),
    ("gather", (TOKENS, 4 * QUAD)),
    ("pick", (TOKENS, 256)),
    ("proj_p", (C, C)),
    ("proj_s", (C, C)),
)
LOADED = [name for name, shape in OPERANDS if shape is not None]


def scratch(plan):
    xy, z, rows = plan
    tokens_f32 = pltpu.VMEM((TOKENS, C), F32)
    row_stat = pltpu.VMEM((TOKENS, 1), F32)
    full_bias = pltpu.VMEM((HEADS, TOKENS, TOKENS), F32)
    weights = pltpu.VMEM((2, 3 * C // 2, C), BF16)
    qkv = pltpu.VMEM((TOKENS, 3 * C), BF16)
    kvt = pltpu.VMEM((2 * C, TOKENS), BF16)
    heads_t = pltpu.VMEM((C, TOKENS), BF16)
    dma = pltpu.SemaphoreType.DMA
    named = {name: pltpu.VMEM(shape, BF16) for name, shape in OPERANDS if shape is not None}
    named |= dict(
        load_sem=dma((len(OPERANDS),)),
        wp=weights,
        ws=weights,
        xf=tokens_f32,
        quads=pltpu.VMEM((4 * QUAD, C), F32),
        xhat_p=tokens_f32,
        rstd_p=row_stat,
        xhat_s=tokens_f32,
        rstd_s=row_stat,
        s2f=tokens_f32,
        dy2f=tokens_f32,
        qkv_p=qkv,
        kvt_p=kvt,
        qkv_s=qkv,
        kvt_s=kvt,
        probs_p=full_bias,
        probs_s=full_bias,
        ot_p=heads_t,
        ot_s=heads_t,
        ot_r=heads_t,
        dqkv=qkv,
        dqt=pltpu.VMEM((C, TOKENS), F32),
        bias_p=full_bias,
        bias_s=full_bias,
        tabf=pltpu.VMEM((16, 6400), F32),
        spread=pltpu.VMEM((2, TOKENS * 16, 128), F32),
        send=pltpu.VMEM((5, 4, QUAD, C), BF16),
        recv=pltpu.VMEM((5, 4, QUAD, C), BF16),
        halo_ss=dma((5, 4)),
        halo_rs=dma((5, 4)),
        w_ss=dma((2,)),
        w_rs=dma((2,)),
        f_ss=dma((2,)),
        f_rs=dma((2,)),
        part=pltpu.VMEM((2, C, C), F32),
        part16=pltpu.VMEM((2, C, C), BF16),
        half_in=pltpu.VMEM((2, C // 2, C), BF16),
        chunks=pltpu.VMEM((2, C // 2 // rows, rows, C), BF16),
        xy_in=pltpu.VMEM((2, xy, rows, C), BF16),
        z_in=pltpu.VMEM((2, z, rows, C), BF16),
        final=pltpu.VMEM((2, C, C), BF16),
        out_sem=dma((4,)),
        field_out=pltpu.VMEM((WLAT * WLON, LEV, C), BF16),
        grad_out=pltpu.VMEM((WLAT * WLON, LEV, C), BF16),
        c_ss=dma((2,)),
        c_rs=dma((2,)),
        xy_ss=dma((2, xy)),
        xy_rs=dma((2, xy)),
        z_ss=dma((2, z)),
        z_rs=dma((2, z)),
        fin_ss=dma((2, 2 * xy)),
        roll=pltpu.SemaphoreType.REGULAR((3,)),
        fin_rs=dma((2, C // rows)),
    )
    return named


def kernel(sizes, plan, names, *refs):
    run(sizes, plan, **dict(zip(names, refs)))


def run(
    sizes,
    plan,
    out_field,
    out_grad,
    gp_p,
    gp_s,
    wp,
    ws,
    xf,
    quads,
    xhat_p,
    rstd_p,
    xhat_s,
    rstd_s,
    s2f,
    dy2f,
    qkv_p,
    kvt_p,
    qkv_s,
    kvt_s,
    probs_p,
    probs_s,
    ot_p,
    ot_s,
    ot_r,
    dqkv,
    dqt,
    bias_p,
    bias_s,
    tabf,
    spread,
    send,
    recv,
    halo_ss,
    halo_rs,
    w_ss,
    w_rs,
    f_ss,
    f_rs,
    part,
    part16,
    half_in,
    chunks,
    xy_in,
    z_in,
    final,
    c_ss,
    c_rs,
    xy_ss,
    xy_rs,
    z_ss,
    z_rs,
    fin_ss,
    fin_rs,
    roll,
    load_sem,
    out_sem,
    field_out,
    grad_out,
    **local,
):
    n_lat, n_lon, n_dp = sizes
    lat, lon, dp = lax.axis_index("lat"), lax.axis_index("lon"), lax.axis_index("dp")
    core = lax.rem(lat, 2)
    sibling = (lat + 1 - 2 * core, lon, dp)
    across = (lat, lax.rem(lon + n_lon // 2, n_lon), 1 - dp)

    def near(dlat, dlon):
        return (
            lax.rem(lat + dlat + n_lat, n_lat),
            lax.rem(lon + dlon + n_lon, n_lon),
            dp,
        )

    xy, n_z, chunk_rows = plan
    n_y = n_lat // 2
    n_own = C // 2 // chunk_rows
    z = lax.rem(lon, n_z)
    spot = (lon // n_z + 2 * dp) * n_y + lat // 2

    def at_spot(e, c):
        x = e // n_y
        return (lax.rem(e, n_y) * 2 + c, lax.rem(x, 2) * n_z + z, x // 2)

    def at_z(other):
        return (lat, lon - z + other, dp)

    def each(n, do):
        def step(d, carry):
            do(d)
            return carry

        lax.fori_loop(1, n, step, 0)

    def greet(semaphore, device):
        pl.semaphore_signal(semaphore, inc=1, device_id=device, device_id_type=MESH)

    def along_z(d):
        return (lat, lon - z + lax.rem(z + d + 8 * n_z, n_z), dp)

    beside_x = (lat, across[1], dp)
    y_up, y_down = near(2, 0), near(-2, 0)
    barrier = pltpu.get_barrier_semaphore()
    around = [across, sibling, beside_x, y_up, y_down, along_z(1), along_z(-1)]
    around += [near(a, b) for a, b in ((1, 0), (-1, 0), (0, 1), (0, -1), (1, 1), (-1, -1))]
    for device in around:
        greet(barrier, device)

    def tell(i):
        for device in (across, sibling, beside_x, y_up, y_down):
            greet(roll.at[i], device)
        for d in (2**i, -(2**i)):
            greet(roll.at[i], along_z(d))

    def told(i):
        pl.semaphore_wait(roll.at[i], 7)

    results = [
        pltpu.make_async_copy(a, b, out_sem.at[i])
        for i, (a, b) in enumerate(
            ((final.at[0], gp_p), (final.at[1], gp_s), (field_out, out_field), (grad_out, out_grad))
        )
    ]
    loads = {}
    for i, (name, shape) in enumerate(OPERANDS):
        source = local[name + "_hbm"]
        target = local[name] if shape else {"wp_half": wp, "ws_half": ws}[name].at[dp]
        loads[name] = pltpu.make_async_copy(source, target, load_sem.at[i])
        loads[name].start()
    wp_half, ws_half = local["wp_half_hbm"], local["ws_half_hbm"]
    field, cot, proj_p, proj_s, tab_p, tab_s, gather, scatter, pick = (
        local[name]
        for name in (
            "field", "cot", "proj_p", "proj_s", "tab_p", "tab_s", "gather", "scatter", "pick"
        )
    )
    pl.semaphore_wait(barrier, len(around))

    rows = pl.ds(pl.multiple_of(core * 288, 32), 288)

    def weights_across(half, full, i):
        return pltpu.make_async_remote_copy(
            half.at[rows],
            full.at[dp, rows],
            w_ss.at[i],
            w_rs.at[i],
            device_id=across,
            device_id_type=MESH,
        )

    def weights_beside(full, i):
        part = full.at[1 - dp, rows]
        return pltpu.make_async_remote_copy(
            part, part, f_ss.at[i], f_rs.at[i], device_id=sibling, device_id_type=MESH
        )

    first = [weights_across(wp_half, wp, 0), weights_across(ws_half, ws, 1)]
    first[0].start()
    beside = [weights_beside(wp, 0), weights_beside(ws, 1)]

    def halo(i, by):
        kept = 3 if by < 0 else 0
        copies = []
        for slot in range(4):
            if slot == kept:
                recv[i, 3 - slot] = send[i, slot]
                continue
            a, b = divmod(slot, 2)
            moves = 0 if by < 0 else 1
            copies.append(
                pltpu.make_async_remote_copy(
                    send.at[i, slot],
                    recv.at[i, 3 - slot],
                    halo_ss.at[i, slot],
                    halo_rs.at[i, 3 - slot],
                    device_id=near(by if a == moves else 0, by if b == moves else 0),
                    device_id_type=MESH,
                )
            )
        for copy in copies:
            copy.start()
        return copies

    def arrived(i, copies):
        for copy in copies:
            copy.wait_recv()
        return nn(gather[...], recv[i].reshape(4 * QUAD, C))

    def to_quads(i, x):
        send[i] = nn(scatter[...], x).astype(BF16).reshape(4, QUAD, C)

    loads["cot"].wait()
    quads[...] = jnp.zeros_like(quads)
    for h in range(WLAT):
        for w in range(WLON):
            at = ((h // 6) * 2 + w // 3) * QUAD + ((h % 6) * 3 + w % 3) * 2
            quads[at : at + 2, :] = cot[h * WLON + w].astype(F32)
    send[0] = quads[...].astype(BF16).reshape(4, QUAD, C)
    halo_cot = halo(0, -1)
    tell(0)

    loads["field"].wait()
    for i in range(WLAT * WLON):
        xf[2 * i : 2 * i + 2, :] = field[i].astype(F32)

    def norm(x, xhat, rstd):
        mean = jnp.mean(x, axis=-1, keepdims=True)
        centred = x - mean
        r = lax.rsqrt(jnp.mean(centred * centred, axis=-1, keepdims=True) + 1e-5)
        y = centred * r
        xhat[...] = y
        rstd[...] = r
        return y.astype(BF16)

    lane256 = lax.broadcasted_iota(jnp.int32, (16, 256), 1)

    def expand(tab, bias, hide):
        tabf[...] = jnp.zeros_like(tabf)
        tabf[0:HEADS, 0 : 4 * WLAT * CHUNK] = tab[...].astype(F32)

        def row(h, carry):
            for za in range(LEV):
                parts = []
                for zb in range(LEV):
                    c = (za * 2 + zb) * WLAT + h
                    tile = c + c // 32
                    off = 4 * lax.rem(c, 32)
                    window = tabf[:, pl.ds(pl.multiple_of(tile * 128, 128), 256)]
                    parts.append(pltpu.roll(window, lax.rem(256 + 127 * zb - off, 256), 1))
                for w in range(WLON):
                    low, high = parts
                    if w:
                        low = pltpu.roll(low, 256 - w, 1)
                        high = pltpu.roll(high, 256 - w, 1)
                    at = pl.multiple_of((h * WLON + w) * 32 + za * 16, 16)
                    both = jnp.where(lane256 < 127, low, high)
                    spread[0, pl.ds(at, 16), :] = both[:, :128]
                    spread[1, pl.ds(at, 16), :] = both[:, 128:]
            return carry

        lax.fori_loop(0, WLAT, row, 0)
        for head in range(HEADS):
            lanes = [spread[half, pl.ds(head, TOKENS, stride=16), :] for half in range(2)]
            table = jnp.concatenate(lanes, axis=1).astype(BF16)
            full = nt(pick[...], table)
            bias[head] = full if hide is None else full + hide

    lane = lax.broadcasted_iota(jnp.int32, (TOKENS, 128), 1) // HEAD

    def by_head(x):
        zero = jnp.zeros_like(x)
        return jnp.concatenate([jnp.where(lane == j, x, zero) for j in range(PER)], axis=0)

    def own_lanes(x):
        total = jnp.where(lane == 0, x[0:TOKENS], 0.0)
        for j in range(1, PER):
            total += jnp.where(lane == j, x[j * TOKENS : (j + 1) * TOKENS], 0.0)
        return total

    scale = 1.0 / HEAD**0.5

    def project(n, full, qkv, kvt):
        w = full[...].reshape(3 * C, C)
        qkv[...] = nt(n, w).astype(BF16)
        kvt[...] = nt(w[C:], n).astype(BF16)

    def softmax(g, qkv, bias):
        q = qkv[:, g * 128 : (g + 1) * 128]
        k = qkv[:, C + g * 128 : C + (g + 1) * 128]
        s = nt(by_head(k), q).reshape(PER, TOKENS, TOKENS) * scale
        s = s + bias[g * PER : (g + 1) * PER]
        e = jnp.exp(s - jnp.max(s, axis=1, keepdims=True))
        return e / jnp.sum(e, axis=1, keepdims=True)

    def values(g, p, kvt, ot):
        for j in range(PER):
            at = g * 128 + j * HEAD
            vt = kvt[C + at : C + at + HEAD, :]
            ot[at : at + HEAD, :] = nn(vt, p[j]).astype(BF16)

    def grads(g, p, pb, do, qkv, kvt):
        cols = slice(g * 128, (g + 1) * 128)
        q = qkv[:, cols]
        v = qkv[:, 2 * C + g * 128 : 2 * C + (g + 1) * 128]
        dog = do[:, cols]
        dp_ = nt(by_head(v), dog).reshape(PER, TOKENS, TOKENS)
        inner = jnp.sum(p * dp_, axis=1, keepdims=True)
        ds = (p * (dp_ - inner)).astype(BF16)
        dv = own_lanes(nn(pb.reshape(PER * TOKENS, TOKENS), dog))
        dk = own_lanes(nn(ds.reshape(PER * TOKENS, TOKENS), q)) * scale
        dqkv[:, 2 * C + g * 128 : 2 * C + (g + 1) * 128] = dv.astype(BF16)
        dqkv[:, C + g * 128 : C + (g + 1) * 128] = dk.astype(BF16)
        for j in range(PER):
            at = g * 128 + j * HEAD
            dqt[at : at + HEAD, :] = nn(kvt[at : at + HEAD, :], ds[j]) * scale

    def input_grad(dy, full, xhat, rstd):
        dqkv[:, 0:C] = dqt[...].T.astype(BF16)
        dn = nn(dqkv[...], full[...].reshape(3 * C, C))
        xh = xhat[...]
        mean = jnp.mean(dn, axis=-1, keepdims=True)
        product = jnp.mean(dn * xh, axis=-1, keepdims=True)
        return (dy + rstd[...] * (dn - mean - xh * product)).astype(BF16)

    def heads(ot):
        return ot[...].astype(F32).T.astype(BF16)

    def output(x, o, proj):
        return (x + nn(o, proj[...])).astype(BF16)

    def copy_core(m):
        return pltpu.make_async_remote_copy(
            part16.at[m, pl.ds(pl.multiple_of((1 - core) * (C // 2), 64), C // 2)],
            half_in.at[m],
            c_ss.at[m],
            c_rs.at[m],
            device_id=sibling,
            device_id_type=MESH,
        )

    def owned(m, e):
        return lax.rem(e + xy - m * n_y, xy)

    def copy_xy(m, to, sender, ss):
        return pltpu.make_async_remote_copy(
            chunks.at[m, lax.rem(owned(m, to), n_own)],
            xy_in.at[m, sender],
            xy_ss.at[m, ss],
            xy_rs.at[m, sender],
            device_id=at_spot(to, core),
            device_id_type=MESH,
        )

    def copy_z(m, to, sender, ss):
        return pltpu.make_async_remote_copy(
            z_in.at[m, z],
            z_in.at[m, sender],
            z_ss.at[m, ss],
            z_rs.at[m, sender],
            device_id=at_z(to),
            device_id_type=MESH,
        )

    def chunk(index):
        return pl.ds(pl.multiple_of(index * chunk_rows, 16), chunk_rows)

    def copy_final(m, index, ss, device):
        return pltpu.make_async_remote_copy(
            final.at[m, chunk(index)],
            final.at[m, chunk(index)],
            fin_ss.at[m, ss],
            fin_rs.at[m, index],
            device_id=device,
            device_id_type=MESH,
        )

    def copy_spread(m, d):
        device = at_spot(lax.rem(spot + d, xy), core)
        return copy_final(m, core * n_own + lax.rem(owned(m, spot), n_own), d, device)

    def copy_beside(m, i):
        return copy_final(m, core * n_own + i, xy + i, sibling)

    def far_first(k):
        return n_z // 2 + (2 * lax.rem(k, 2) - 1) * (k // 2)

    def if_owner(m):
        return pl.when(owned(m, spot) < n_own)

    def sum_start(m, total):
        part[m] = total
        part16[m] = total.astype(BF16)
        copy_core(m).start()

    def sum_xy(m):
        copy_core(m).wait_recv()
        at = pl.ds(pl.multiple_of(core * (C // 2), 64), C // 2)
        both = part[m, at, :] + half_in[m].astype(F32)
        chunks[m] = both.astype(BF16).reshape(n_own, chunk_rows, C)

        def go(d):
            to = lax.rem(spot + d, xy)

            @if_owner_of(m, to)
            def _():
                copy_xy(m, to, spot, d).start()

        each(xy, go)

    def if_owner_of(m, e):
        return pl.when(owned(m, e) < n_own)

    def sum_z(m):
        @if_owner(m)
        def _():
            xy_in[m, spot] = chunks[m, lax.rem(owned(m, spot), n_own)]
            each(xy, lambda d: copy_xy(m, spot, lax.rem(spot + d, xy), d).wait_recv())
            z_in[m, z] = jnp.sum(xy_in[m].astype(F32), axis=0).astype(BF16)

            def go(k):
                d = far_first(k)
                copy_z(m, lax.rem(z + d, n_z), z, d).start()

            each(n_z, go)

    def sum_back(m):
        @if_owner(m)
        def _():
            each(n_z, lambda d: copy_z(m, z, lax.rem(z + d, n_z), d).wait_recv())
            index = core * n_own + lax.rem(owned(m, spot), n_own)
            final[m, chunk(index), :] = jnp.sum(z_in[m].astype(F32), axis=0).astype(BF16)
            each(xy, lambda d: copy_spread(m, d).start())

    def sum_share(m):
        def take(i, carry):
            @pl.when(owned(m, spot) != i)
            def _():
                copy_final(m, core * n_own + i, 0, sibling).wait_recv()

            copy_beside(m, i).start()
            return carry

        lax.fori_loop(0, n_own, take, 0)

    def sum_end(m):
        def take(i, carry):
            copy_final(m, (1 - core) * n_own + i, 0, sibling).wait_recv()
            return carry

        lax.fori_loop(0, n_own, take, 0)
        results[m].start()

    def sum_sent(m):
        copy_core(m).wait_send()

        def sent(d):
            to = lax.rem(spot + d, xy)

            @if_owner_of(m, to)
            def _():
                copy_xy(m, to, spot, d).wait_send()

        each(xy, sent)

        @if_owner(m)
        def _():
            each(n_z, lambda d: copy_z(m, lax.rem(z + d, n_z), z, d).wait_send())
            each(xy, lambda d: copy_spread(m, d).wait_send())

        def passed(i, carry):
            copy_beside(m, i).wait_send()
            return carry

        lax.fori_loop(0, n_own, passed, 0)

    n1 = norm(xf[...], xhat_p, rstd_p)
    loads["tab_p"].wait()
    loads["pick"].wait()
    expand(tab_p, bias_p, None)
    first[0].wait_send()
    first[1].start()
    told(0)
    tell(1)
    loads["wp_half"].wait()
    first[0].wait_recv()
    beside[0].start()
    beside[0].wait_recv()
    project(n1, wp, qkv_p, kvt_p)
    for g in range(GROUPS):
        p = softmax(g, qkv_p, bias_p)
        probs_p[g * PER : (g + 1) * PER] = p
        values(g, p.astype(BF16), kvt_p, ot_p)
    loads["proj_p"].wait()
    loads["scatter"].wait()
    o1 = heads(ot_p)
    to_quads(1, output(xf[...], o1, proj_p))
    halo_h1 = halo(1, -1)
    to_quads(4, o1)
    halo_o1 = halo(4, -1)
    told(1)
    tell(2)

    key = lax.broadcasted_iota(jnp.int32, (TOKENS, TOKENS), 0)
    query = lax.broadcasted_iota(jnp.int32, (TOKENS, TOKENS), 1)
    edge = jnp.where(lat == n_lat - 1, TOKENS // 2, TOKENS)
    same = ((key & 1) == (query & 1)) & ((key >= edge) == (query >= edge))
    loads["tab_s"].wait()
    expand(tab_s, bias_s, jnp.where(same, 0.0, -1e30))
    loads["ws_half"].wait()
    first[1].wait_recv()
    beside[1].start()
    loads["gather"].wait()
    dy2 = arrived(0, halo_cot)
    dy2f[...] = dy2
    loads["proj_s"].wait()
    do2 = nt(dy2.astype(BF16), proj_s[...]).astype(BF16)
    beside[1].wait_recv()
    told(2)

    s2 = arrived(1, halo_h1)
    s2f[...] = s2
    n2 = norm(s2, xhat_s, rstd_s)
    project(n2, ws, qkv_s, kvt_s)
    for g in range(GROUPS):
        p = softmax(g, qkv_s, bias_s)
        probs_s[g * PER : (g + 1) * PER] = p
        values(g, p.astype(BF16), kvt_s, ot_s)
    sum_start(1, nn(ot_s[...], dy2f[...].astype(BF16)))
    for g in range(GROUPS):
        p = probs_s[g * PER : (g + 1) * PER]
        grads(g, p, p.astype(BF16), do2, qkv_s, kvt_s)
        if g == 0:
            sum_xy(1)
            ot_r[...] = arrived(4, halo_o1).T.astype(BF16)
    ds2 = input_grad(dy2f[...], ws, xhat_s, rstd_s)
    sum_start(0, nn(ot_r[...], ds2))
    to_quads(2, ds2)
    halo_g1 = halo(2, 1)

    y2 = output(s2f[...], heads(ot_s), proj_s)
    to_quads(3, y2)
    halo_out = halo(3, 1)
    sum_xy(0)
    sum_z(1)

    g1 = arrived(2, halo_g1)
    do1 = nt(g1.astype(BF16), proj_p[...]).astype(BF16)
    for g in range(GROUPS):
        p = probs_p[g * PER : (g + 1) * PER]
        grads(g, p, p.astype(BF16), do1, qkv_p, kvt_p)
        if g == 1:
            sum_z(0)
    xf[...] = input_grad(g1, wp, xhat_p, rstd_p).astype(F32)
    for i in range(WLAT * WLON):
        grad_out[i] = xf[2 * i : 2 * i + 2, :].astype(BF16)
    results[3].start()
    s2f[...] = arrived(3, halo_out)
    for i in range(WLAT * WLON):
        field_out[i] = s2f[2 * i : 2 * i + 2, :].astype(BF16)
    results[2].start()
    sum_back(1)
    sum_back(0)
    for copies in (halo_cot, halo_h1, halo_o1, halo_g1, halo_out, first[1:], beside):
        for copy in copies:
            copy.wait_send()
    sum_share(1)
    sum_share(0)
    sum_end(1)
    sum_end(0)
    sum_sent(1)
    sum_sent(0)
    for copy in results:
        copy.wait()


def store(*refs):
    sources, targets, staged, semaphores = refs[:4], refs[4:8], refs[8:12], refs[12]
    taken = [pltpu.make_async_copy(sources[i], staged[i], semaphores.at[i]) for i in range(4)]
    given = [pltpu.make_async_copy(staged[i], targets[i], semaphores.at[4 + i]) for i in range(4)]
    for copy in taken:
        copy.start()
    for before, after in zip(taken, given):
        before.wait()
        after.start()
    for copy in given:
        copy.wait()


def body(sizes, field, cotangent, qkv_plain, proj_plain, bias_plain, qkv_shift, proj_shift, bias_shift):
    def rows(x):
        return x.transpose(0, 2, 3, 1, 4).reshape(WLAT * WLON, LEV, C)

    gather, scatter, pick = constants()
    operands = dict(
        field=rows(field),
        cot=rows(cotangent),
        wp_half=qkv_plain.T,
        ws_half=qkv_shift.T,
        proj_p=proj_plain,
        proj_s=proj_shift,
        tab_p=bias_plain.reshape(HEADS, -1),
        tab_s=bias_shift.reshape(HEADS, -1),
        gather=jnp.asarray(gather, BF16),
        scatter=jnp.asarray(scatter, BF16),
        pick=jnp.asarray(pick, BF16),
    )
    n_lat, n_lon, n_dp = sizes
    xy = n_lat // 2 * 2 * n_dp
    owners = max(d for d in (1, 2, 3, 4, 6, 12) if d <= xy)
    plan = (xy, n_lon // 2, C // 2 // owners)
    buffers = scratch(plan)
    hbm = pl.BlockSpec(memory_space=pl.ANY)
    grid_shape = jax.ShapeDtypeStruct((WLAT * WLON, LEV, C), BF16)
    square = jax.ShapeDtypeStruct((C, C), BF16)
    names = [name + "_hbm" for name, _ in OPERANDS]
    names += ["out_field", "out_grad", "gp_p", "gp_s"] + list(buffers)
    out_field, out_grad, gp_p, gp_s = pl.pallas_call(
        functools.partial(kernel, sizes, plan, names),
        out_shape=(grid_shape, grid_shape, square, square),
        in_specs=[hbm] * len(OPERANDS),
        out_specs=[hbm] * 4,
        scratch_shapes=list(buffers.values()),
        compiler_params=pltpu.CompilerParams(
            collective_id=0, has_side_effects=True, vmem_limit_bytes=56 * 2**20
        ),
    )(*[operands[name] for name, _ in OPERANDS])

    results = (out_field, out_grad, gp_p, gp_s)
    out_field, out_grad, gp_p, gp_s = pl.pallas_call(
        store,
        out_shape=tuple(jax.ShapeDtypeStruct(x.shape, x.dtype) for x in results),
        in_specs=[hbm] * 4,
        out_specs=[hbm] * 4,
        scratch_shapes=[pltpu.VMEM(x.shape, x.dtype) for x in results]
        + [pltpu.SemaphoreType.DMA((8,))],
        compiler_params=pltpu.CompilerParams(vmem_limit_bytes=56 * 2**20),
    )(*results)

    def grid(x):
        return x.reshape(1, WLAT, WLON, LEV, C).transpose(0, 3, 1, 2, 4)

    return grid(out_field), grid(out_grad), gp_p, gp_s


def solution(mesh):
    sizes = tuple(mesh.shape[a] for a in ("lat", "lon", "dp"))
    grid = P("dp", None, "lat", "lon", None)
    table = P(None, "lat", None, None)
    columns = P(None, "dp")
    return jax.shard_map(
        functools.partial(body, sizes),
        mesh=mesh,
        in_specs=(grid, grid, columns, P(), table, columns, P(), table),
        out_specs=(grid, grid, P(), P()),
        check_vma=False,
    )
```

```python
import functools

import jax
import jax.numpy as jnp
import numpy as np
from jax import lax
from jax.experimental import pallas as pl
from jax.experimental.pallas import tpu as pltpu
from jax.sharding import PartitionSpec as P

HEADS = 12
HEAD = 32
C = 384
LEV = 2
WLAT = 12
WLON = 6
TOKENS = LEV * WLAT * WLON
QUAD = 48
GROUPS = 3
PER = HEADS // GROUPS
REL = 2 * WLON - 1
CHUNK = WLAT * REL
MESH = pl.DeviceIdType.MESH
F32 = jnp.float32
BF16 = jnp.bfloat16


def nn(a, b):
    return lax.dot_general(a, b, (((1,), (0,)), ((), ())), preferred_element_type=F32)


def nt(a, b):
    return lax.dot_general(a, b, (((1,), (1,)), ((), ())), preferred_element_type=F32)


def token(h, w, z):
    return (h * WLON + w) * LEV + z


def constants():
    gather = np.zeros((TOKENS, 4 * QUAD), np.float32)
    pick = np.zeros((TOKENS, 256), np.float32)
    for h in range(WLAT):
        for w in range(WLON):
            for z in range(LEV):
                slot = (h // 6) * 2 + w // 3
                inner = ((h % 6) * 3 + w % 3) * 2 + (1 - z)
                gather[token(h, w, z), slot * QUAD + inner] = 1
                pick[token(h, w, z), z * 127 + h * REL + WLON - 1 - w] = 1
    scatter = np.zeros((4 * QUAD, TOKENS), np.float32)
    for h in range(WLAT):
        for w in range(WLON):
            for z in range(LEV):
                slot = (h // 6) * 2 + w // 3
                scatter[slot * QUAD + ((h % 6) * 3 + w % 3) * 2 + z, token(h, w, z)] = 1
    return gather, scatter, pick


OPERANDS = (
    ("field", (WLAT * WLON, LEV, C)),
    ("cot", (WLAT * WLON, LEV, C)),
    ("wp_half", None),
    ("ws_half", None),
    ("tab_p", (HEADS, 4 * WLAT * CHUNK)),
    ("tab_s", (HEADS, 4 * WLAT * CHUNK)),
    ("scatter", (4 * QUAD, TOKENS)),
    ("gather", (TOKENS, 4 * QUAD)),
    ("pick", (TOKENS, 256)),
    ("proj_p", (C, C)),
    ("proj_s", (C, C)),
)
LOADED = [name for name, shape in OPERANDS if shape is not None]


def scratch(plan):
    xy, z, rows = plan
    tokens_f32 = pltpu.VMEM((TOKENS, C), F32)
    row_stat = pltpu.VMEM((TOKENS, 1), F32)
    full_bias = pltpu.VMEM((HEADS, TOKENS, TOKENS), F32)
    weights = pltpu.VMEM((2, 3 * C // 2, C), BF16)
    qkv = pltpu.VMEM((TOKENS, 3 * C), BF16)
    kvt = pltpu.VMEM((2 * C, TOKENS), BF16)
    heads_t = pltpu.VMEM((C, TOKENS), BF16)
    dma = pltpu.SemaphoreType.DMA
    named = {name: pltpu.VMEM(shape, BF16) for name, shape in OPERANDS if shape is not None}
    named |= dict(
        load_sem=dma((len(OPERANDS),)),
        wp=weights,
        ws=weights,
        xf=tokens_f32,
        quads=pltpu.VMEM((4 * QUAD, C), F32),
        xhat_p=tokens_f32,
        rstd_p=row_stat,
        xhat_s=tokens_f32,
        rstd_s=row_stat,
        s2f=tokens_f32,
        dy2f=tokens_f32,
        qkv_p=qkv,
        kvt_p=kvt,
        qkv_s=qkv,
        kvt_s=kvt,
        probs_p=full_bias,
        probs_s=full_bias,
        ot_p=heads_t,
        ot_s=heads_t,
        ot_r=heads_t,
        dqkv=qkv,
        dqt=pltpu.VMEM((C, TOKENS), F32),
        bias_p=full_bias,
        bias_s=full_bias,
        tabf=pltpu.VMEM((16, 6400), F32),
        spread=pltpu.VMEM((2, TOKENS * 16, 128), F32),
        send=pltpu.VMEM((5, 4, QUAD, C), BF16),
        recv=pltpu.VMEM((5, 4, QUAD, C), BF16),
        halo_ss=dma((5, 4)),
        halo_rs=dma((5, 4)),
        w_ss=dma((2,)),
        w_rs=dma((2,)),
        f_ss=dma((2,)),
        f_rs=dma((2,)),
        part=pltpu.VMEM((2, C, C), F32),
        part16=pltpu.VMEM((2, C, C), BF16),
        half_in=pltpu.VMEM((2, C // 2, C), BF16),
        chunks=pltpu.VMEM((2, C // 2 // rows, rows, C), BF16),
        xy_in=pltpu.VMEM((2, xy, rows, C), BF16),
        z_in=pltpu.VMEM((2, z, rows, C), BF16),
        final=pltpu.VMEM((2, C, C), BF16),
        out_sem=dma((4,)),
        field_out=pltpu.VMEM((WLAT * WLON, LEV, C), BF16),
        grad_out=pltpu.VMEM((WLAT * WLON, LEV, C), BF16),
        c_ss=dma((2,)),
        c_rs=dma((2,)),
        xy_ss=dma((2,)),
        xy_rs=dma((2,)),
        z_ss=dma((2, 2)),
        z_rs=dma((2, 2)),
        fin_ss=dma((2,)),
        fin_rs=dma((2,)),
        half_ss=dma((2,)),
        half_rs=dma((2,)),
        roll=pltpu.SemaphoreType.REGULAR((3,)),
    )
    return named


def kernel(sizes, plan, names, *refs):
    run(sizes, plan, **dict(zip(names, refs)))


def run(
    sizes,
    plan,
    out_field,
    out_grad,
    gp_p,
    gp_s,
    wp,
    ws,
    xf,
    quads,
    xhat_p,
    rstd_p,
    xhat_s,
    rstd_s,
    s2f,
    dy2f,
    qkv_p,
    kvt_p,
    qkv_s,
    kvt_s,
    probs_p,
    probs_s,
    ot_p,
    ot_s,
    ot_r,
    dqkv,
    dqt,
    bias_p,
    bias_s,
    tabf,
    spread,
    send,
    recv,
    halo_ss,
    halo_rs,
    w_ss,
    w_rs,
    f_ss,
    f_rs,
    part,
    part16,
    half_in,
    chunks,
    xy_in,
    z_in,
    final,
    c_ss,
    c_rs,
    xy_ss,
    xy_rs,
    z_ss,
    z_rs,
    fin_ss,
    fin_rs,
    half_ss,
    half_rs,
    roll,
    load_sem,
    out_sem,
    field_out,
    grad_out,
    **local,
):
    n_lat, n_lon, n_dp = sizes
    lat, lon, dp = lax.axis_index("lat"), lax.axis_index("lon"), lax.axis_index("dp")
    core = lax.rem(lat, 2)
    sibling = (lat + 1 - 2 * core, lon, dp)
    across = (lat, lax.rem(lon + n_lon // 2, n_lon), 1 - dp)

    def near(dlat, dlon):
        return (
            lax.rem(lat + dlat + n_lat, n_lat),
            lax.rem(lon + dlon + n_lon, n_lon),
            dp,
        )

    xy, n_z, chunk_rows = plan
    n_y = n_lat // 2
    n_own = C // 2 // chunk_rows
    z = lax.rem(lon, n_z)
    x_lo, row = lax.div(lon, n_z), lax.div(lat, 2)

    def wrap(value, size):
        return jnp.where(value >= size, value - size, value)

    def place(move):
        lo, hi, up = move
        to_lo = 1 - x_lo if lo else x_lo
        to_hi = 1 - dp if hi else dp
        to_row = wrap(row + up, n_y)
        device = (2 * to_row + core, to_lo * n_z + z, to_hi)
        return (to_lo + 2 * to_hi) * n_y + to_row, device

    def hops(move):
        lo, hi, up = move
        return (1 if lo else 2 * hi) + min(up, n_y - up)

    moves = [(lo, hi, up) for lo in range(2) for hi in range(2) for up in range(n_y)][1:]
    moves = sorted(moves, key=hops, reverse=True)
    spot = place((0, 0, 0))[0]

    def at_z(d):
        return (lat, lon - z + wrap(z + d, n_z), dp)

    def greet(semaphore, device):
        pl.semaphore_signal(semaphore, inc=1, device_id=device, device_id_type=MESH)

    def along_z(d):
        return (lat, lon - z + lax.rem(z + d + 8 * n_z, n_z), dp)

    beside_x = (lat, across[1], dp)
    y_up, y_down = near(2, 0), near(-2, 0)
    barrier = pltpu.get_barrier_semaphore()
    around = [across, sibling, beside_x, y_up, y_down, along_z(1), along_z(-1)]
    around += [near(a, b) for a, b in ((1, 0), (-1, 0), (0, 1), (0, -1), (1, 1), (-1, -1))]
    for device in around:
        greet(barrier, device)

    def tell(i):
        for device in (across, sibling, beside_x, y_up, y_down):
            greet(roll.at[i], device)
        for d in (2**i, -(2**i)):
            greet(roll.at[i], along_z(d))

    def told(i):
        pl.semaphore_wait(roll.at[i], 7)

    results = [
        pltpu.make_async_copy(a, b, out_sem.at[i])
        for i, (a, b) in enumerate(
            ((final.at[0], gp_p), (final.at[1], gp_s), (field_out, out_field), (grad_out, out_grad))
        )
    ]
    loads = {}
    for i, (name, shape) in enumerate(OPERANDS):
        source = local[name + "_hbm"]
        target = local[name] if shape else {"wp_half": wp, "ws_half": ws}[name].at[dp]
        loads[name] = pltpu.make_async_copy(source, target, load_sem.at[i])
        loads[name].start()
    wp_half, ws_half = local["wp_half_hbm"], local["ws_half_hbm"]
    field, cot, proj_p, proj_s, tab_p, tab_s, gather, scatter, pick = (
        local[name]
        for name in (
            "field", "cot", "proj_p", "proj_s", "tab_p", "tab_s", "gather", "scatter", "pick"
        )
    )
    pl.semaphore_wait(barrier, len(around))

    rows = pl.ds(pl.multiple_of(core * 288, 32), 288)

    def weights_across(half, full, i):
        return pltpu.make_async_remote_copy(
            half.at[rows],
            full.at[dp, rows],
            w_ss.at[i],
            w_rs.at[i],
            device_id=across,
            device_id_type=MESH,
        )

    def weights_beside(full, i):
        part = full.at[1 - dp, rows]
        return pltpu.make_async_remote_copy(
            part, part, f_ss.at[i], f_rs.at[i], device_id=sibling, device_id_type=MESH
        )

    first = [weights_across(wp_half, wp, 0), weights_across(ws_half, ws, 1)]
    first[0].start()
    beside = [weights_beside(wp, 0), weights_beside(ws, 1)]

    def halo(i, by):
        kept = 3 if by < 0 else 0
        copies = []
        for slot in range(4):
            if slot == kept:
                recv[i, 3 - slot] = send[i, slot]
                continue
            a, b = divmod(slot, 2)
            moves = 0 if by < 0 else 1
            copies.append(
                pltpu.make_async_remote_copy(
                    send.at[i, slot],
                    recv.at[i, 3 - slot],
                    halo_ss.at[i, slot],
                    halo_rs.at[i, 3 - slot],
                    device_id=near(by if a == moves else 0, by if b == moves else 0),
                    device_id_type=MESH,
                )
            )
        for copy in copies:
            copy.start()
        return copies

    def arrived(i, copies):
        for copy in copies:
            copy.wait_recv()
        return nn(gather[...], recv[i].reshape(4 * QUAD, C))

    def to_quads(i, x):
        send[i] = nn(scatter[...], x).astype(BF16).reshape(4, QUAD, C)

    loads["cot"].wait()
    quads[...] = jnp.zeros_like(quads)
    for h in range(WLAT):
        for w in range(WLON):
            at = ((h // 6) * 2 + w // 3) * QUAD + ((h % 6) * 3 + w % 3) * 2
            quads[at : at + 2, :] = cot[h * WLON + w].astype(F32)
    send[0] = quads[...].astype(BF16).reshape(4, QUAD, C)
    halo_cot = halo(0, -1)
    tell(0)

    loads["field"].wait()
    for i in range(WLAT * WLON):
        xf[2 * i : 2 * i + 2, :] = field[i].astype(F32)

    def norm(x, xhat, rstd):
        mean = jnp.mean(x, axis=-1, keepdims=True)
        centred = x - mean
        r = lax.rsqrt(jnp.mean(centred * centred, axis=-1, keepdims=True) + 1e-5)
        y = centred * r
        xhat[...] = y
        rstd[...] = r
        return y.astype(BF16)

    lane256 = lax.broadcasted_iota(jnp.int32, (16, 256), 1)

    def expand(tab, bias, hide):
        tabf[...] = jnp.zeros_like(tabf)
        tabf[0:HEADS, 0 : 4 * WLAT * CHUNK] = tab[...].astype(F32)

        def row(h, carry):
            for za in range(LEV):
                parts = []
                for zb in range(LEV):
                    c = (za * 2 + zb) * WLAT + h
                    tile = c + c // 32
                    off = 4 * lax.rem(c, 32)
                    window = tabf[:, pl.ds(pl.multiple_of(tile * 128, 128), 256)]
                    parts.append(pltpu.roll(window, lax.rem(256 + 127 * zb - off, 256), 1))
                for w in range(WLON):
                    low, high = parts
                    if w:
                        low = pltpu.roll(low, 256 - w, 1)
                        high = pltpu.roll(high, 256 - w, 1)
                    at = pl.multiple_of((h * WLON + w) * 32 + za * 16, 16)
                    both = jnp.where(lane256 < 127, low, high)
                    spread[0, pl.ds(at, 16), :] = both[:, :128]
                    spread[1, pl.ds(at, 16), :] = both[:, 128:]
            return carry

        lax.fori_loop(0, WLAT, row, 0)
        for head in range(HEADS):
            lanes = [spread[half, pl.ds(head, TOKENS, stride=16), :] for half in range(2)]
            table = jnp.concatenate(lanes, axis=1).astype(BF16)
            full = nt(pick[...], table)
            bias[head] = full if hide is None else full + hide

    lane = lax.broadcasted_iota(jnp.int32, (TOKENS, 128), 1) // HEAD

    def by_head(x):
        zero = jnp.zeros_like(x)
        return jnp.concatenate([jnp.where(lane == j, x, zero) for j in range(PER)], axis=0)

    def own_lanes(x):
        total = jnp.where(lane == 0, x[0:TOKENS], 0.0)
        for j in range(1, PER):
            total += jnp.where(lane == j, x[j * TOKENS : (j + 1) * TOKENS], 0.0)
        return total

    scale = 1.0 / HEAD**0.5

    def project(n, full, qkv, kvt):
        w = full[...].reshape(3 * C, C)
        qkv[...] = nt(n, w).astype(BF16)
        kvt[...] = nt(w[C:], n).astype(BF16)

    def softmax(g, qkv, bias):
        q = qkv[:, g * 128 : (g + 1) * 128]
        k = qkv[:, C + g * 128 : C + (g + 1) * 128]
        s = nt(by_head(k), q).reshape(PER, TOKENS, TOKENS) * scale
        s = s + bias[g * PER : (g + 1) * PER]
        e = jnp.exp(s - jnp.max(s, axis=1, keepdims=True))
        return e / jnp.sum(e, axis=1, keepdims=True)

    def values(g, p, kvt, ot):
        for j in range(PER):
            at = g * 128 + j * HEAD
            vt = kvt[C + at : C + at + HEAD, :]
            ot[at : at + HEAD, :] = nn(vt, p[j]).astype(BF16)

    def grads(g, p, pb, do, qkv, kvt):
        cols = slice(g * 128, (g + 1) * 128)
        q = qkv[:, cols]
        v = qkv[:, 2 * C + g * 128 : 2 * C + (g + 1) * 128]
        dog = do[:, cols]
        dp_ = nt(by_head(v), dog).reshape(PER, TOKENS, TOKENS)
        inner = jnp.sum(p * dp_, axis=1, keepdims=True)
        ds = (p * (dp_ - inner)).astype(BF16)
        dv = own_lanes(nn(pb.reshape(PER * TOKENS, TOKENS), dog))
        dk = own_lanes(nn(ds.reshape(PER * TOKENS, TOKENS), q)) * scale
        dqkv[:, 2 * C + g * 128 : 2 * C + (g + 1) * 128] = dv.astype(BF16)
        dqkv[:, C + g * 128 : C + (g + 1) * 128] = dk.astype(BF16)
        for j in range(PER):
            at = g * 128 + j * HEAD
            dqt[at : at + HEAD, :] = nn(kvt[at : at + HEAD, :], ds[j]) * scale

    def input_grad(dy, full, xhat, rstd):
        dqkv[:, 0:C] = dqt[...].T.astype(BF16)
        dn = nn(dqkv[...], full[...].reshape(3 * C, C))
        xh = xhat[...]
        mean = jnp.mean(dn, axis=-1, keepdims=True)
        product = jnp.mean(dn * xh, axis=-1, keepdims=True)
        return (dy + rstd[...] * (dn - mean - xh * product)).astype(BF16)

    def heads(ot):
        return ot[...].astype(F32).T.astype(BF16)

    def output(x, o, proj):
        return (x + nn(o, proj[...])).astype(BF16)

    def copy_core(m):
        return pltpu.make_async_remote_copy(
            part16.at[m, half(1 - core)],
            half_in.at[m],
            c_ss.at[m],
            c_rs.at[m],
            device_id=sibling,
            device_id_type=MESH,
        )

    def owned(m, e):
        e = e - m * n_y
        return jnp.where(e < 0, e + xy, e)

    mine = [jnp.minimum(owned(m, spot), n_own - 1) for m in range(2)]

    def if_owner(m):
        return pl.when(owned(m, spot) < n_own)

    def if_not_owner(m):
        return pl.when(owned(m, spot) >= n_own)

    def remote(source, target, ss, rs, device=sibling):
        return pltpu.make_async_remote_copy(
            source, target, ss, rs, device_id=device, device_id_type=MESH
        )

    def chunk(index, n=1):
        return pl.ds(pl.multiple_of(index * chunk_rows, 16), n * chunk_rows)

    def half(c):
        return pl.ds(pl.multiple_of(c * (C // 2), 64), C // 2)

    far_first = [d for i in range(n_z) for d in (n_z // 2 + i, n_z // 2 - i)]
    far_first = [d for d in dict.fromkeys(far_first) if 0 < d < n_z]
    z_steps = [far_first], [[8, 4, 12], [2, 1, 15]] if n_z == 16 else [far_first]
    z_order = [z], [lax.div(z, 4), 4 + lax.rem(z, 4)] if n_z == 16 else [z]
    z_slots = [(0, n_z)], [(0, 4), (4, 4)] if n_z == 16 else [(0, n_z)]

    def sum_start(m, total):
        part[m] = total
        part16[m] = total.astype(BF16)
        copy_core(m).start()

    def sum_xy(m):
        copy_core(m).wait_recv()
        both = part[m, half(core), :] + half_in[m].astype(F32)
        chunks[m] = both.astype(BF16).reshape(n_own, chunk_rows, C)
        for move in moves:
            to, device = place(move)
            k = owned(m, to)

            @pl.when(k < n_own)
            def _():
                source = chunks.at[m, jnp.minimum(k, n_own - 1)]
                remote(source, xy_in.at[m, spot], xy_ss.at[m], xy_rs.at[m], device).start()

    def z_send(m, i, value):
        slot = z_order[m][i]
        z_in[m, slot] = value.astype(BF16)
        for d in z_steps[m][i]:
            block = z_in.at[m, slot]
            remote(block, block, z_ss.at[m, i], z_rs.at[m, i], at_z(d)).start()

    def z_sum(m, i):
        at, n = z_slots[m][i]
        if n > 1:
            several = z_in.at[m, at : at + n - 1]
            remote(several, several, z_ss.at[m, i], z_rs.at[m, i]).wait_recv()
        return jnp.sum(z_in[m, at : at + n].astype(F32), axis=0)

    def sum_z(m):
        @if_owner(m)
        def _():
            xy_in[m, spot] = chunks[m, mine[m]]
            several = xy_in.at[m, 0 : xy - 1]
            remote(several, several, xy_ss.at[m], xy_rs.at[m]).wait_recv()
            z_send(m, 0, jnp.sum(xy_in[m].astype(F32), axis=0))

    def sum_z_again(m):
        if len(z_steps[m]) > 1:

            @if_owner(m)
            def _():
                z_send(m, 1, z_sum(m, 0))

    def sum_back(m):
        @if_owner(m)
        def _():
            block = final.at[m, chunk(core * n_own + mine[m])]
            final[m, chunk(core * n_own + mine[m]), :] = z_sum(m, len(z_steps[m]) - 1).astype(BF16)
            for move in moves:
                remote(block, block, fin_ss.at[m], fin_rs.at[m], place(move)[1]).start()

    def sum_share(m):
        def wait(n):
            several = final.at[m, 0 : n * chunk_rows]
            remote(several, several, fin_ss.at[m], fin_rs.at[m]).wait_recv()

        if_owner(m)(lambda: wait(n_own - 1))
        if_not_owner(m)(lambda: wait(n_own))
        block = final.at[m, half(core)]
        remote(block, block, half_ss.at[m], half_rs.at[m]).start()

    def sum_end(m):
        block = final.at[m, half(core)]
        remote(block, block, half_ss.at[m], half_rs.at[m]).wait_recv()
        results[m].start()

    def sum_sent(m):
        copy_core(m).wait_send()
        block = final.at[m, half(core)]
        remote(block, block, half_ss.at[m], half_rs.at[m]).wait_send()

        def wait(n):
            several = chunks.at[m, 0:n]
            remote(several, several, xy_ss.at[m], xy_rs.at[m]).wait_send()

        @if_not_owner(m)
        def _():
            wait(n_own)

        @if_owner(m)
        def _():
            wait(n_own - 1)
            several = xy_in.at[m, 0 : xy - 1]
            remote(several, several, fin_ss.at[m], fin_rs.at[m]).wait_send()
            for i, (at, n) in enumerate(z_slots[m]):
                if n > 1:
                    several = z_in.at[m, at : at + n - 1]
                    remote(several, several, z_ss.at[m, i], z_rs.at[m, i]).wait_send()

    n1 = norm(xf[...], xhat_p, rstd_p)
    loads["tab_p"].wait()
    loads["pick"].wait()
    expand(tab_p, bias_p, None)
    first[0].wait_send()
    first[1].start()
    told(0)
    tell(1)
    loads["wp_half"].wait()
    first[0].wait_recv()
    beside[0].start()
    beside[0].wait_recv()
    project(n1, wp, qkv_p, kvt_p)
    for g in range(GROUPS):
        p = softmax(g, qkv_p, bias_p)
        probs_p[g * PER : (g + 1) * PER] = p
        values(g, p.astype(BF16), kvt_p, ot_p)
    loads["proj_p"].wait()
    loads["scatter"].wait()
    o1 = heads(ot_p)
    to_quads(1, output(xf[...], o1, proj_p))
    halo_h1 = halo(1, -1)
    to_quads(4, o1)
    halo_o1 = halo(4, -1)
    told(1)
    tell(2)

    key = lax.broadcasted_iota(jnp.int32, (TOKENS, TOKENS), 0)
    query = lax.broadcasted_iota(jnp.int32, (TOKENS, TOKENS), 1)
    edge = jnp.where(lat == n_lat - 1, TOKENS // 2, TOKENS)
    same = ((key & 1) == (query & 1)) & ((key >= edge) == (query >= edge))
    loads["tab_s"].wait()
    expand(tab_s, bias_s, jnp.where(same, 0.0, -1e30))
    loads["ws_half"].wait()
    first[1].wait_recv()
    beside[1].start()
    loads["gather"].wait()
    dy2 = arrived(0, halo_cot)
    dy2f[...] = dy2
    loads["proj_s"].wait()
    do2 = nt(dy2.astype(BF16), proj_s[...]).astype(BF16)
    beside[1].wait_recv()
    told(2)

    s2 = arrived(1, halo_h1)
    s2f[...] = s2
    n2 = norm(s2, xhat_s, rstd_s)
    project(n2, ws, qkv_s, kvt_s)
    for g in range(GROUPS):
        p = softmax(g, qkv_s, bias_s)
        probs_s[g * PER : (g + 1) * PER] = p
        values(g, p.astype(BF16), kvt_s, ot_s)
    sum_start(1, nn(ot_s[...], dy2f[...].astype(BF16)))
    for g in range(GROUPS):
        p = probs_s[g * PER : (g + 1) * PER]
        grads(g, p, p.astype(BF16), do2, qkv_s, kvt_s)
        if g == 0:
            sum_xy(1)
            ot_r[...] = arrived(4, halo_o1).T.astype(BF16)
    ds2 = input_grad(dy2f[...], ws, xhat_s, rstd_s)
    sum_start(0, nn(ot_r[...], ds2))
    to_quads(2, ds2)
    halo_g1 = halo(2, 1)

    y2 = output(s2f[...], heads(ot_s), proj_s)
    to_quads(3, y2)
    halo_out = halo(3, 1)
    sum_xy(0)
    sum_z(1)

    g1 = arrived(2, halo_g1)
    do1 = nt(g1.astype(BF16), proj_p[...]).astype(BF16)
    for g in range(GROUPS):
        p = probs_p[g * PER : (g + 1) * PER]
        grads(g, p, p.astype(BF16), do1, qkv_p, kvt_p)
        if g == 1:
            sum_z(0)
    xf[...] = input_grad(g1, wp, xhat_p, rstd_p).astype(F32)
    for i in range(WLAT * WLON):
        grad_out[i] = xf[2 * i : 2 * i + 2, :].astype(BF16)
    results[3].start()
    s2f[...] = arrived(3, halo_out)
    for i in range(WLAT * WLON):
        field_out[i] = s2f[2 * i : 2 * i + 2, :].astype(BF16)
    results[2].start()
    sum_z_again(1)
    sum_back(1)
    sum_back(0)
    for copies in (halo_cot, halo_h1, halo_o1, halo_g1, halo_out, first[1:], beside):
        for copy in copies:
            copy.wait_send()
    sum_share(1)
    sum_share(0)
    sum_end(1)
    sum_end(0)
    sum_sent(1)
    sum_sent(0)
    for copy in results:
        copy.wait()


def store(*refs):
    sources, targets, staged, semaphores = refs[:4], refs[4:8], refs[8:12], refs[12]
    taken = [pltpu.make_async_copy(sources[i], staged[i], semaphores.at[i]) for i in range(4)]
    given = [pltpu.make_async_copy(staged[i], targets[i], semaphores.at[4 + i]) for i in range(4)]
    for copy in taken:
        copy.start()
    for before, after in zip(taken, given):
        before.wait()
        after.start()
    for copy in given:
        copy.wait()


def body(sizes, field, cotangent, qkv_plain, proj_plain, bias_plain, qkv_shift, proj_shift, bias_shift):
    def rows(x):
        return x.transpose(0, 2, 3, 1, 4).reshape(WLAT * WLON, LEV, C)

    gather, scatter, pick = constants()
    operands = dict(
        field=rows(field),
        cot=rows(cotangent),
        wp_half=qkv_plain.T,
        ws_half=qkv_shift.T,
        proj_p=proj_plain,
        proj_s=proj_shift,
        tab_p=bias_plain.reshape(HEADS, -1),
        tab_s=bias_shift.reshape(HEADS, -1),
        gather=jnp.asarray(gather, BF16),
        scatter=jnp.asarray(scatter, BF16),
        pick=jnp.asarray(pick, BF16),
    )
    n_lat, n_lon, n_dp = sizes
    xy = n_lat // 2 * 2 * n_dp
    owners = max(d for d in (1, 2, 3, 4, 6, 12) if d <= xy)
    plan = (xy, n_lon // 2, C // 2 // owners)
    buffers = scratch(plan)
    hbm = pl.BlockSpec(memory_space=pl.ANY)
    grid_shape = jax.ShapeDtypeStruct((WLAT * WLON, LEV, C), BF16)
    square = jax.ShapeDtypeStruct((C, C), BF16)
    names = [name + "_hbm" for name, _ in OPERANDS]
    names += ["out_field", "out_grad", "gp_p", "gp_s"] + list(buffers)
    out_field, out_grad, gp_p, gp_s = pl.pallas_call(
        functools.partial(kernel, sizes, plan, names),
        out_shape=(grid_shape, grid_shape, square, square),
        in_specs=[hbm] * len(OPERANDS),
        out_specs=[hbm] * 4,
        scratch_shapes=list(buffers.values()),
        compiler_params=pltpu.CompilerParams(
            collective_id=0, has_side_effects=True, vmem_limit_bytes=56 * 2**20
        ),
    )(*[operands[name] for name, _ in OPERANDS])

    results = (out_field, out_grad, gp_p, gp_s)
    out_field, out_grad, gp_p, gp_s = pl.pallas_call(
        store,
        out_shape=tuple(jax.ShapeDtypeStruct(x.shape, x.dtype) for x in results),
        in_specs=[hbm] * 4,
        out_specs=[hbm] * 4,
        scratch_shapes=[pltpu.VMEM(x.shape, x.dtype) for x in results]
        + [pltpu.SemaphoreType.DMA((8,))],
        compiler_params=pltpu.CompilerParams(vmem_limit_bytes=56 * 2**20),
    )(*results)

    def grid(x):
        return x.reshape(1, WLAT, WLON, LEV, C).transpose(0, 3, 1, 2, 4)

    return grid(out_field), grid(out_grad), gp_p, gp_s


def solution(mesh):
    sizes = tuple(mesh.shape[a] for a in ("lat", "lon", "dp"))
    grid = P("dp", None, "lat", "lon", None)
    table = P(None, "lat", None, None)
    columns = P(None, "dp")
    return jax.shard_map(
        functools.partial(body, sizes),
        mesh=mesh,
        in_specs=(grid, grid, columns, P(), table, columns, P(), table),
        out_specs=(grid, grid, P(), P()),
        check_vma=False,
    )
```

```python
import functools

import jax
import jax.numpy as jnp
import numpy as np
from jax import lax
from jax.experimental import pallas as pl
from jax.experimental.pallas import tpu as pltpu
from jax.sharding import PartitionSpec as P

HEADS = 12
HEAD = 32
C = 384
LEV = 2
WLAT = 12
WLON = 6
TOKENS = LEV * WLAT * WLON
QUAD = 48
GROUPS = 3
PER = HEADS // GROUPS
REL = 2 * WLON - 1
CHUNK = WLAT * REL
MESH = pl.DeviceIdType.MESH
F32 = jnp.float32
BF16 = jnp.bfloat16


def nn(a, b):
    return lax.dot_general(a, b, (((1,), (0,)), ((), ())), preferred_element_type=F32)


def nt(a, b):
    return lax.dot_general(a, b, (((1,), (1,)), ((), ())), preferred_element_type=F32)


def token(h, w, z):
    return (h * WLON + w) * LEV + z


def constants():
    gather = np.zeros((TOKENS, 4 * QUAD), np.float32)
    pick = np.zeros((TOKENS, 256), np.float32)
    for h in range(WLAT):
        for w in range(WLON):
            for z in range(LEV):
                slot = (h // 6) * 2 + w // 3
                inner = ((h % 6) * 3 + w % 3) * 2 + (1 - z)
                gather[token(h, w, z), slot * QUAD + inner] = 1
                pick[token(h, w, z), z * 127 + h * REL + WLON - 1 - w] = 1
    scatter = np.zeros((4 * QUAD, TOKENS), np.float32)
    for h in range(WLAT):
        for w in range(WLON):
            for z in range(LEV):
                slot = (h // 6) * 2 + w // 3
                scatter[slot * QUAD + ((h % 6) * 3 + w % 3) * 2 + z, token(h, w, z)] = 1
    return gather, scatter, pick


OPERANDS = (
    ("field", (WLAT * WLON, LEV, C)),
    ("cot", (WLAT * WLON, LEV, C)),
    ("wp_half", None),
    ("ws_half", None),
    ("tab_p", (HEADS, 4 * WLAT * CHUNK)),
    ("tab_s", (HEADS, 4 * WLAT * CHUNK)),
    ("scatter", (4 * QUAD, TOKENS)),
    ("gather", (TOKENS, 4 * QUAD)),
    ("pick", (TOKENS, 256)),
    ("proj_p", (C, C)),
    ("proj_s", (C, C)),
)
LOADED = [name for name, shape in OPERANDS if shape is not None]


def scratch(plan):
    xy, z, rows = plan
    tokens_f32 = pltpu.VMEM((TOKENS, C), F32)
    row_stat = pltpu.VMEM((TOKENS, 1), F32)
    full_bias = pltpu.VMEM((HEADS, TOKENS, TOKENS), F32)
    weights = pltpu.VMEM((2, 3 * C // 2, C), BF16)
    qkv = pltpu.VMEM((TOKENS, 3 * C), BF16)
    kvt = pltpu.VMEM((2 * C, TOKENS), BF16)
    heads_t = pltpu.VMEM((C, TOKENS), BF16)
    dma = pltpu.SemaphoreType.DMA
    named = {name: pltpu.VMEM(shape, BF16) for name, shape in OPERANDS if shape is not None}
    named |= dict(
        load_sem=dma((len(OPERANDS),)),
        wp=weights,
        ws=weights,
        xf=tokens_f32,
        quads=pltpu.VMEM((4 * QUAD, C), F32),
        xhat_p=tokens_f32,
        rstd_p=row_stat,
        xhat_s=tokens_f32,
        rstd_s=row_stat,
        s2f=tokens_f32,
        dy2f=tokens_f32,
        qkv_p=qkv,
        kvt_p=kvt,
        qkv_s=qkv,
        kvt_s=kvt,
        probs_p=full_bias,
        probs_s=full_bias,
        ot_p=heads_t,
        ot_s=heads_t,
        dqkv=qkv,
        dqt=pltpu.VMEM((C, TOKENS), F32),
        bias_p=full_bias,
        bias_s=full_bias,
        tabf=pltpu.VMEM((16, 6400), F32),
        spread_p=pltpu.VMEM((2, TOKENS * 16, 128), F32),
        spread_s=pltpu.VMEM((2, TOKENS * 16, 128), F32),
        send=pltpu.VMEM((5, 4, QUAD, C), BF16),
        recv=pltpu.VMEM((5, 4, QUAD, C), BF16),
        halo_ss=dma((5, 4)),
        halo_rs=dma((5, 4)),
        w_ss=dma((4,)),
        w_rs=dma((4,)),
        f_ss=dma((4,)),
        f_rs=dma((4,)),
        part=pltpu.VMEM((2, C, C), F32),
        part16=pltpu.VMEM((2, C, C), BF16),
        half_in=pltpu.VMEM((2, C // 2, C), BF16),
        chunks=pltpu.VMEM((2, C // 2 // rows, rows, C), BF16),
        xy_in=pltpu.VMEM((2, xy, rows, C), BF16),
        z_in=pltpu.VMEM((2, z, rows, C), BF16),
        final=pltpu.VMEM((2, C, C), BF16),
        out_sem=dma((4,)),
        field_out=pltpu.VMEM((WLAT * WLON, LEV, C), BF16),
        grad_out=pltpu.VMEM((WLAT * WLON, LEV, C), BF16),
        c_ss=dma((2,)),
        c_rs=dma((2,)),
        xy_ss=dma((2,)),
        xy_rs=dma((2,)),
        z_ss=dma((2, 2)),
        z_rs=dma((2, 2)),
        fin_ss=dma((2,)),
        fin_rs=dma((2,)),
        half_ss=dma((2,)),
        half_rs=dma((2,)),
        roll=pltpu.SemaphoreType.REGULAR((3,)),
    )
    return named


def kernel(sizes, plan, names, *refs):
    run(sizes, plan, **dict(zip(names, refs)))


def run(
    sizes,
    plan,
    out_field,
    out_grad,
    gp_p,
    gp_s,
    wp,
    ws,
    xf,
    quads,
    xhat_p,
    rstd_p,
    xhat_s,
    rstd_s,
    s2f,
    dy2f,
    qkv_p,
    kvt_p,
    qkv_s,
    kvt_s,
    probs_p,
    probs_s,
    ot_p,
    ot_s,
    dqkv,
    dqt,
    bias_p,
    bias_s,
    tabf,
    spread_p,
    spread_s,
    send,
    recv,
    halo_ss,
    halo_rs,
    w_ss,
    w_rs,
    f_ss,
    f_rs,
    part,
    part16,
    half_in,
    chunks,
    xy_in,
    z_in,
    final,
    c_ss,
    c_rs,
    xy_ss,
    xy_rs,
    z_ss,
    z_rs,
    fin_ss,
    fin_rs,
    half_ss,
    half_rs,
    roll,
    load_sem,
    out_sem,
    field_out,
    grad_out,
    **local,
):
    n_lat, n_lon, n_dp = sizes
    lat, lon, dp = lax.axis_index("lat"), lax.axis_index("lon"), lax.axis_index("dp")
    core = lax.rem(lat, 2)
    sibling = (lat + 1 - 2 * core, lon, dp)
    across = (lat, lax.rem(lon + n_lon // 2, n_lon), 1 - dp)

    def near(dlat, dlon):
        return (
            lax.rem(lat + dlat + n_lat, n_lat),
            lax.rem(lon + dlon + n_lon, n_lon),
            dp,
        )

    xy, n_z, chunk_rows = plan
    n_y = n_lat // 2
    n_own = C // 2 // chunk_rows
    z = lax.rem(lon, n_z)
    x_lo, row = lax.div(lon, n_z), lax.div(lat, 2)

    def wrap(value, size):
        return jnp.where(value >= size, value - size, value)

    def place(move):
        lo, hi, up = move
        to_lo = 1 - x_lo if lo else x_lo
        to_hi = 1 - dp if hi else dp
        to_row = wrap(row + up, n_y)
        device = (2 * to_row + core, to_lo * n_z + z, to_hi)
        return (to_lo + 2 * to_hi) * n_y + to_row, device

    def hops(move):
        lo, hi, up = move
        return (1 if lo else 2 * hi) + min(up, n_y - up)

    moves = [(lo, hi, up) for lo in range(2) for hi in range(2) for up in range(n_y)][1:]
    moves = sorted(moves, key=hops, reverse=True)
    spot = place((0, 0, 0))[0]

    def at_z(d):
        return (lat, lon - z + wrap(z + d, n_z), dp)

    def greet(semaphore, device):
        pl.semaphore_signal(semaphore, inc=1, device_id=device, device_id_type=MESH)

    def along_z(d):
        return (lat, lon - z + lax.rem(z + d + 8 * n_z, n_z), dp)

    beside_x = (lat, across[1], dp)
    y_up, y_down = near(2, 0), near(-2, 0)
    barrier = pltpu.get_barrier_semaphore()
    around = [across, sibling, beside_x, y_up, y_down, along_z(1), along_z(-1)]
    around += [near(a, b) for a, b in ((1, 0), (-1, 0), (0, 1), (0, -1))]
    for device in around:
        greet(barrier, device)

    def tell(i):
        for device in (across, sibling, beside_x, y_up, y_down):
            greet(roll.at[i], device)
        for d in (2**i, -(2**i)):
            greet(roll.at[i], along_z(d))
        if i == 0:
            greet(roll.at[i], near(1, 0))
            greet(roll.at[i], near(-1, 0))

    def told(i):
        pl.semaphore_wait(roll.at[i], 9 if i == 0 else 7)

    results = [
        pltpu.make_async_copy(a, b, out_sem.at[i])
        for i, (a, b) in enumerate(
            ((final.at[0], gp_p), (final.at[1], gp_s), (field_out, out_field), (grad_out, out_grad))
        )
    ]
    loads = {}
    for i, (name, shape) in enumerate(OPERANDS):
        source = local[name + "_hbm"]
        target = local[name] if shape else {"wp_half": wp, "ws_half": ws}[name].at[dp]
        loads[name] = pltpu.make_async_copy(source, target, load_sem.at[i])
        loads[name].start()
    wp_half, ws_half = local["wp_half_hbm"], local["ws_half_hbm"]
    field, cot, proj_p, proj_s, tab_p, tab_s, gather, scatter, pick = (
        local[name]
        for name in (
            "field", "cot", "proj_p", "proj_s", "tab_p", "tab_s", "gather", "scatter", "pick"
        )
    )
    pl.semaphore_wait(barrier, len(around))

    def piece(i, n):
        size = 288 // n
        return pl.ds(pl.multiple_of(core * 288 + i * size, 16), size)

    def weights_across(source, full, at, i):
        return pltpu.make_async_remote_copy(
            source.at[at],
            full.at[dp, at],
            w_ss.at[i],
            w_rs.at[i],
            device_id=across,
            device_id_type=MESH,
        )

    def weights_beside(full, at, i):
        part = full.at[1 - dp, at]
        return pltpu.make_async_remote_copy(
            part, part, f_ss.at[i], f_rs.at[i], device_id=sibling, device_id_type=MESH
        )

    places = [(wp_half, wp, piece(i, 3)) for i in range(3)] + [(ws_half, ws, piece(0, 1))]
    first = [weights_across(*place, i) for i, place in enumerate(places)]
    beside = [weights_beside(*place[1:], i) for i, place in enumerate(places)]
    for copy in first[:3]:
        copy.start()
    tell(0)

    def halo(i, by):
        kept = 3 if by < 0 else 0
        copies = []
        for slot in range(4):
            if slot == kept:
                recv[i, 3 - slot] = send[i, slot]
                continue
            a, b = divmod(slot, 2)
            moves = 0 if by < 0 else 1
            copies.append(
                pltpu.make_async_remote_copy(
                    send.at[i, slot],
                    recv.at[i, 3 - slot],
                    halo_ss.at[i, slot],
                    halo_rs.at[i, 3 - slot],
                    device_id=near(by if a == moves else 0, by if b == moves else 0),
                    device_id_type=MESH,
                )
            )
        for copy in copies:
            copy.start()
        return copies

    def arrived(i, copies):
        for copy in copies:
            copy.wait_recv()
        return nn(gather[...], recv[i].reshape(4 * QUAD, C))

    def to_quads(i, x):
        send[i] = nn(scatter[...], x).astype(BF16).reshape(4, QUAD, C)

    loads["cot"].wait()
    quads[...] = jnp.zeros_like(quads)
    for h in range(WLAT):
        for w in range(WLON):
            at = ((h // 6) * 2 + w // 3) * QUAD + ((h % 6) * 3 + w % 3) * 2
            quads[at : at + 2, :] = cot[h * WLON + w].astype(F32)
    send[0] = quads[...].astype(BF16).reshape(4, QUAD, C)

    loads["field"].wait()
    for i in range(WLAT * WLON):
        xf[2 * i : 2 * i + 2, :] = field[i].astype(F32)

    def norm(x, xhat, rstd):
        mean = jnp.mean(x, axis=-1, keepdims=True)
        centred = x - mean
        r = lax.rsqrt(jnp.mean(centred * centred, axis=-1, keepdims=True) + 1e-5)
        y = centred * r
        xhat[...] = y
        rstd[...] = r
        return y.astype(BF16)

    lane256 = lax.broadcasted_iota(jnp.int32, (16, 256), 1)

    def align(tab, spread):
        tabf[...] = jnp.zeros_like(tabf)
        tabf[0:HEADS, 0 : 4 * WLAT * CHUNK] = tab[...].astype(F32)

        def row(h, carry):
            for za in range(LEV):
                parts = []
                for zb in range(LEV):
                    c = (za * 2 + zb) * WLAT + h
                    tile = c + c // 32
                    off = 4 * lax.rem(c, 32)
                    window = tabf[:, pl.ds(pl.multiple_of(tile * 128, 128), 256)]
                    parts.append(pltpu.roll(window, lax.rem(256 + 127 * zb - off, 256), 1))
                for w in range(WLON):
                    low, high = parts
                    if w:
                        low = pltpu.roll(low, 256 - w, 1)
                        high = pltpu.roll(high, 256 - w, 1)
                    at = pl.multiple_of((h * WLON + w) * 32 + za * 16, 16)
                    both = jnp.where(lane256 < 127, low, high)
                    spread[0, pl.ds(at, 16), :] = both[:, :128]
                    spread[1, pl.ds(at, 16), :] = both[:, 128:]
            return carry

        lax.fori_loop(0, WLAT, row, 0)

    def expand(spread, bias, hide):
        for head in range(HEADS):
            lanes = [spread[half, pl.ds(head, TOKENS, stride=16), :] for half in range(2)]
            table = jnp.concatenate(lanes, axis=1).astype(BF16)
            full = nt(pick[...], table)
            bias[head] = full if hide is None else full + hide

    lane = lax.broadcasted_iota(jnp.int32, (TOKENS, 128), 1) // HEAD

    def by_head(x):
        zero = jnp.zeros_like(x)
        return jnp.concatenate([jnp.where(lane == j, x, zero) for j in range(PER)], axis=0)

    def own_lanes(x):
        total = jnp.where(lane == 0, x[0:TOKENS], 0.0)
        for j in range(1, PER):
            total += jnp.where(lane == j, x[j * TOKENS : (j + 1) * TOKENS], 0.0)
        return total

    scale = 1.0 / HEAD**0.5

    def project(n, full, qkv, kvt):
        w = full[...].reshape(3 * C, C)
        qkv[...] = nt(n, w).astype(BF16)
        kvt[...] = nt(w[C:], n).astype(BF16)

    def softmax(g, qkv, bias):
        q = qkv[:, g * 128 : (g + 1) * 128]
        k = qkv[:, C + g * 128 : C + (g + 1) * 128]
        s = nt(by_head(k), q).reshape(PER, TOKENS, TOKENS) * scale
        s = s + bias[g * PER : (g + 1) * PER]
        e = jnp.exp(s - jnp.max(s, axis=1, keepdims=True))
        return e / jnp.sum(e, axis=1, keepdims=True)

    def values(g, p, kvt, ot):
        for j in range(PER):
            at = g * 128 + j * HEAD
            vt = kvt[C + at : C + at + HEAD, :]
            ot[at : at + HEAD, :] = nn(vt, p[j]).astype(BF16)

    def grads(g, p, pb, do, qkv, kvt):
        cols = slice(g * 128, (g + 1) * 128)
        q = qkv[:, cols]
        v = qkv[:, 2 * C + g * 128 : 2 * C + (g + 1) * 128]
        dog = do[:, cols]
        dp_ = nt(by_head(v), dog).reshape(PER, TOKENS, TOKENS)
        inner = jnp.sum(p * dp_, axis=1, keepdims=True)
        ds = (p * (dp_ - inner)).astype(BF16)
        dv = own_lanes(nn(pb.reshape(PER * TOKENS, TOKENS), dog))
        dk = own_lanes(nn(ds.reshape(PER * TOKENS, TOKENS), q)) * scale
        dqkv[:, 2 * C + g * 128 : 2 * C + (g + 1) * 128] = dv.astype(BF16)
        dqkv[:, C + g * 128 : C + (g + 1) * 128] = dk.astype(BF16)
        for j in range(PER):
            at = g * 128 + j * HEAD
            dqt[at : at + HEAD, :] = nn(kvt[at : at + HEAD, :], ds[j]) * scale

    def input_grad(dy, full, xhat, rstd):
        dqkv[:, 0:C] = dqt[...].T.astype(BF16)
        dn = nn(dqkv[...], full[...].reshape(3 * C, C))
        xh = xhat[...]
        mean = jnp.mean(dn, axis=-1, keepdims=True)
        product = jnp.mean(dn * xh, axis=-1, keepdims=True)
        return (dy + rstd[...] * (dn - mean - xh * product)).astype(BF16)

    def heads(ot):
        return ot[...].astype(F32).T.astype(BF16)

    def output(x, o, proj):
        return (x + nn(o, proj[...])).astype(BF16)

    def copy_core(m):
        return pltpu.make_async_remote_copy(
            part16.at[m, half(1 - core)],
            half_in.at[m],
            c_ss.at[m],
            c_rs.at[m],
            device_id=sibling,
            device_id_type=MESH,
        )

    def owned(m, e):
        e = e - m * n_y
        return jnp.where(e < 0, e + xy, e)

    mine = [jnp.minimum(owned(m, spot), n_own - 1) for m in range(2)]

    def if_owner(m):
        return pl.when(owned(m, spot) < n_own)

    def if_not_owner(m):
        return pl.when(owned(m, spot) >= n_own)

    def remote(source, target, ss, rs, device=sibling):
        return pltpu.make_async_remote_copy(
            source, target, ss, rs, device_id=device, device_id_type=MESH
        )

    def chunk(index, n=1):
        return pl.ds(pl.multiple_of(index * chunk_rows, 16), n * chunk_rows)

    def half(c):
        return pl.ds(pl.multiple_of(c * (C // 2), 64), C // 2)

    far_first = [d for i in range(n_z) for d in (n_z // 2 + i, n_z // 2 - i)]
    far_first = [d for d in dict.fromkeys(far_first) if 0 < d < n_z]
    z_steps = [[8, 4, 12], [2, 1, 15]] if n_z == 16 else [far_first]
    z_order = [lax.div(z, 4), 4 + lax.rem(z, 4)] if n_z == 16 else [z]
    z_slots = [(0, 4), (4, 4)] if n_z == 16 else [(0, n_z)]

    def sum_start(m, total):
        part[m] = total
        part16[m] = total.astype(BF16)
        copy_core(m).start()

    def sum_xy(m):
        copy_core(m).wait_recv()
        both = part[m, half(core), :] + half_in[m].astype(F32)
        chunks[m] = both.astype(BF16).reshape(n_own, chunk_rows, C)
        for move in moves:
            to, device = place(move)
            k = owned(m, to)

            @pl.when(k < n_own)
            def _():
                source = chunks.at[m, jnp.minimum(k, n_own - 1)]
                remote(source, xy_in.at[m, spot], xy_ss.at[m], xy_rs.at[m], device).start()

    def z_send(m, i, value):
        slot = z_order[i]
        z_in[m, slot] = value.astype(BF16)
        for d in z_steps[i]:
            block = z_in.at[m, slot]
            remote(block, block, z_ss.at[m, i], z_rs.at[m, i], at_z(d)).start()

    def z_sum(m, i):
        at, n = z_slots[i]
        if n > 1:
            several = z_in.at[m, at : at + n - 1]
            remote(several, several, z_ss.at[m, i], z_rs.at[m, i]).wait_recv()
        return jnp.sum(z_in[m, at : at + n].astype(F32), axis=0)

    def sum_z(m):
        @if_owner(m)
        def _():
            xy_in[m, spot] = chunks[m, mine[m]]
            several = xy_in.at[m, 0 : xy - 1]
            remote(several, several, xy_ss.at[m], xy_rs.at[m]).wait_recv()
            z_send(m, 0, jnp.sum(xy_in[m].astype(F32), axis=0))

    def sum_z_again(m):
        if len(z_steps) > 1:

            @if_owner(m)
            def _():
                z_send(m, 1, z_sum(m, 0))

    def sum_back(m):
        @if_owner(m)
        def _():
            block = final.at[m, chunk(core * n_own + mine[m])]
            final[m, chunk(core * n_own + mine[m]), :] = z_sum(m, len(z_steps) - 1).astype(BF16)
            for move in moves:
                remote(block, block, fin_ss.at[m], fin_rs.at[m], place(move)[1]).start()

    def sum_share(m):
        def wait(n):
            several = final.at[m, 0 : n * chunk_rows]
            remote(several, several, fin_ss.at[m], fin_rs.at[m]).wait_recv()

        if_owner(m)(lambda: wait(n_own - 1))
        if_not_owner(m)(lambda: wait(n_own))
        block = final.at[m, half(core)]
        remote(block, block, half_ss.at[m], half_rs.at[m]).start()

    def sum_end(m):
        block = final.at[m, half(core)]
        remote(block, block, half_ss.at[m], half_rs.at[m]).wait_recv()
        results[m].start()

    def sum_sent(m):
        copy_core(m).wait_send()
        block = final.at[m, half(core)]
        remote(block, block, half_ss.at[m], half_rs.at[m]).wait_send()

        def wait(n):
            several = chunks.at[m, 0:n]
            remote(several, several, xy_ss.at[m], xy_rs.at[m]).wait_send()

        @if_not_owner(m)
        def _():
            wait(n_own)

        @if_owner(m)
        def _():
            wait(n_own - 1)
            several = xy_in.at[m, 0 : xy - 1]
            remote(several, several, fin_ss.at[m], fin_rs.at[m]).wait_send()
            for i, (at, n) in enumerate(z_slots):
                if n > 1:
                    several = z_in.at[m, at : at + n - 1]
                    remote(several, several, z_ss.at[m, i], z_rs.at[m, i]).wait_send()

    n1 = norm(xf[...], xhat_p, rstd_p)
    loads["tab_p"].wait()
    align(tab_p, spread_p)
    loads["pick"].wait()
    expand(spread_p, bias_p, None)
    told(0)
    tell(1)
    halo_cot = halo(0, -1)
    first[0].wait_recv()
    beside[0].start()
    loads["tab_s"].wait()
    align(tab_s, spread_s)
    first[1].wait_recv()
    beside[1].start()
    for copy in first[:3]:
        copy.wait_send()
    first[3].start()
    first[2].wait_recv()
    beside[2].start()
    loads["wp_half"].wait()
    for copy in beside[:3]:
        copy.wait_recv()
    told(1)
    tell(2)
    project(n1, wp, qkv_p, kvt_p)
    for g in range(GROUPS):
        p = softmax(g, qkv_p, bias_p)
        probs_p[g * PER : (g + 1) * PER] = p
        values(g, p.astype(BF16), kvt_p, ot_p)
    loads["proj_p"].wait()
    loads["scatter"].wait()
    o1 = heads(ot_p)
    to_quads(1, output(xf[...], o1, proj_p))
    halo_h1 = halo(1, -1)

    key = lax.broadcasted_iota(jnp.int32, (TOKENS, TOKENS), 0)
    query = lax.broadcasted_iota(jnp.int32, (TOKENS, TOKENS), 1)
    edge = jnp.where(lat == n_lat - 1, TOKENS // 2, TOKENS)
    same = ((key & 1) == (query & 1)) & ((key >= edge) == (query >= edge))
    to_quads(4, o1)
    halo_o1 = halo(4, -1)
    expand(spread_s, bias_s, jnp.where(same, 0.0, -1e30))
    first[3].wait_recv()
    beside[3].start()
    loads["gather"].wait()
    dy2 = arrived(0, halo_cot)
    dy2f[...] = dy2
    loads["proj_s"].wait()
    do2 = nt(dy2.astype(BF16), proj_s[...]).astype(BF16)
    loads["ws_half"].wait()
    beside[3].wait_recv()
    told(2)

    s2 = arrived(1, halo_h1)
    s2f[...] = s2
    n2 = norm(s2, xhat_s, rstd_s)
    project(n2, ws, qkv_s, kvt_s)
    for g in range(GROUPS):
        p = softmax(g, qkv_s, bias_s)
        probs_s[g * PER : (g + 1) * PER] = p
        values(g, p.astype(BF16), kvt_s, ot_s)
    sum_start(1, nn(ot_s[...], dy2f[...].astype(BF16)))
    for g in range(GROUPS):
        p = probs_s[g * PER : (g + 1) * PER]
        grads(g, p, p.astype(BF16), do2, qkv_s, kvt_s)
    sum_xy(1)
    ds2 = input_grad(dy2f[...], ws, xhat_s, rstd_s)
    ot_r = arrived(4, halo_o1).T.astype(BF16)
    sum_start(0, nn(ot_r, ds2))
    to_quads(2, ds2)
    halo_g1 = halo(2, 1)

    y2 = output(s2f[...], heads(ot_s), proj_s)
    to_quads(3, y2)
    halo_out = halo(3, 1)
    sum_xy(0)
    sum_z(1)

    g1 = arrived(2, halo_g1)
    do1 = nt(g1.astype(BF16), proj_p[...]).astype(BF16)
    for g in range(GROUPS):
        p = probs_p[g * PER : (g + 1) * PER]
        grads(g, p, p.astype(BF16), do1, qkv_p, kvt_p)
        if g == 1:
            sum_z(0)
    xf[...] = input_grad(g1, wp, xhat_p, rstd_p).astype(F32)
    for i in range(WLAT * WLON):
        grad_out[i] = xf[2 * i : 2 * i + 2, :].astype(BF16)
    results[3].start()
    s2f[...] = arrived(3, halo_out)
    for i in range(WLAT * WLON):
        field_out[i] = s2f[2 * i : 2 * i + 2, :].astype(BF16)
    results[2].start()
    sum_z_again(1)
    sum_z_again(0)
    sum_back(1)
    sum_back(0)
    for copies in (halo_cot, halo_h1, halo_o1, halo_g1, halo_out, first[3:], beside):
        for copy in copies:
            copy.wait_send()
    sum_share(1)
    sum_share(0)
    sum_end(1)
    sum_end(0)
    sum_sent(1)
    sum_sent(0)
    for copy in results:
        copy.wait()


def store(*refs):
    sources, targets, staged, semaphores = refs[:4], refs[4:8], refs[8:12], refs[12]
    taken = [pltpu.make_async_copy(sources[i], staged[i], semaphores.at[i]) for i in range(4)]
    given = [pltpu.make_async_copy(staged[i], targets[i], semaphores.at[4 + i]) for i in range(4)]
    for copy in taken:
        copy.start()
    for before, after in zip(taken, given):
        before.wait()
        after.start()
    for copy in given:
        copy.wait()


def body(sizes, field, cotangent, qkv_plain, proj_plain, bias_plain, qkv_shift, proj_shift, bias_shift):
    def rows(x):
        return x.transpose(0, 2, 3, 1, 4).reshape(WLAT * WLON, LEV, C)

    gather, scatter, pick = constants()
    operands = dict(
        field=rows(field),
        cot=rows(cotangent),
        wp_half=qkv_plain.T,
        ws_half=qkv_shift.T,
        proj_p=proj_plain,
        proj_s=proj_shift,
        tab_p=bias_plain.reshape(HEADS, -1),
        tab_s=bias_shift.reshape(HEADS, -1),
        gather=jnp.asarray(gather, BF16),
        scatter=jnp.asarray(scatter, BF16),
        pick=jnp.asarray(pick, BF16),
    )
    n_lat, n_lon, n_dp = sizes
    xy = n_lat // 2 * 2 * n_dp
    owners = max(d for d in (1, 2, 3, 4, 6, 12) if d <= xy)
    plan = (xy, n_lon // 2, C // 2 // owners)
    buffers = scratch(plan)
    hbm = pl.BlockSpec(memory_space=pl.ANY)
    grid_shape = jax.ShapeDtypeStruct((WLAT * WLON, LEV, C), BF16)
    square = jax.ShapeDtypeStruct((C, C), BF16)
    names = [name + "_hbm" for name, _ in OPERANDS]
    names += ["out_field", "out_grad", "gp_p", "gp_s"] + list(buffers)
    out_field, out_grad, gp_p, gp_s = pl.pallas_call(
        functools.partial(kernel, sizes, plan, names),
        out_shape=(grid_shape, grid_shape, square, square),
        in_specs=[hbm] * len(OPERANDS),
        out_specs=[hbm] * 4,
        scratch_shapes=list(buffers.values()),
        compiler_params=pltpu.CompilerParams(
            collective_id=0, has_side_effects=True, vmem_limit_bytes=56 * 2**20
        ),
    )(*[operands[name] for name, _ in OPERANDS])

    results = (out_field, out_grad, gp_p, gp_s)
    out_field, out_grad, gp_p, gp_s = pl.pallas_call(
        store,
        out_shape=tuple(jax.ShapeDtypeStruct(x.shape, x.dtype) for x in results),
        in_specs=[hbm] * 4,
        out_specs=[hbm] * 4,
        scratch_shapes=[pltpu.VMEM(x.shape, x.dtype) for x in results]
        + [pltpu.SemaphoreType.DMA((8,))],
        compiler_params=pltpu.CompilerParams(vmem_limit_bytes=56 * 2**20),
    )(*results)

    def grid(x):
        return x.reshape(1, WLAT, WLON, LEV, C).transpose(0, 3, 1, 2, 4)

    return grid(out_field), grid(out_grad), gp_p, gp_s


def solution(mesh):
    sizes = tuple(mesh.shape[a] for a in ("lat", "lon", "dp"))
    grid = P("dp", None, "lat", "lon", None)
    table = P(None, "lat", None, None)
    columns = P(None, "dp")
    return jax.shard_map(
        functools.partial(body, sizes),
        mesh=mesh,
        in_specs=(grid, grid, columns, P(), table, columns, P(), table),
        out_specs=(grid, grid, P(), P()),
        check_vma=False,
    )
```

```python
import functools

import jax
import jax.numpy as jnp
import numpy as np
from jax import lax
from jax.experimental import pallas as pl
from jax.experimental.pallas import tpu as pltpu
from jax.sharding import PartitionSpec as P

HEADS = 12
HEAD = 32
C = 384
LEV = 2
WLAT = 12
WLON = 6
TOKENS = LEV * WLAT * WLON
QUAD = 48
GROUPS = 3
PER = HEADS // GROUPS
REL = 2 * WLON - 1
CHUNK = WLAT * REL
MESH = pl.DeviceIdType.MESH
F32 = jnp.float32
BF16 = jnp.bfloat16


def nn(a, b):
    return lax.dot_general(a, b, (((1,), (0,)), ((), ())), preferred_element_type=F32)


def nt(a, b):
    return lax.dot_general(a, b, (((1,), (1,)), ((), ())), preferred_element_type=F32)


def token(h, w, z):
    return (h * WLON + w) * LEV + z


def constants():
    gather = np.zeros((TOKENS, 4 * QUAD), np.float32)
    pick = np.zeros((TOKENS, 256), np.float32)
    for h in range(WLAT):
        for w in range(WLON):
            for z in range(LEV):
                slot = (h // 6) * 2 + w // 3
                inner = ((h % 6) * 3 + w % 3) * 2 + (1 - z)
                gather[token(h, w, z), slot * QUAD + inner] = 1
                pick[token(h, w, z), z * 127 + h * REL + WLON - 1 - w] = 1
    scatter = np.zeros((4 * QUAD, TOKENS), np.float32)
    for h in range(WLAT):
        for w in range(WLON):
            for z in range(LEV):
                slot = (h // 6) * 2 + w // 3
                scatter[slot * QUAD + ((h % 6) * 3 + w % 3) * 2 + z, token(h, w, z)] = 1
    return gather, scatter, pick


OPERANDS = (
    ("field", (WLAT * WLON, LEV, C)),
    ("cot", (WLAT * WLON, LEV, C)),
    ("wp_half", None),
    ("ws_half", None),
    ("tab_p", (HEADS, 4 * WLAT * CHUNK)),
    ("tab_s", (HEADS, 4 * WLAT * CHUNK)),
    ("scatter", (4 * QUAD, TOKENS)),
    ("gather", (TOKENS, 4 * QUAD)),
    ("pick", (TOKENS, 256)),
    ("proj_p", (C, C)),
    ("proj_s", (C, C)),
)
LOADED = [name for name, shape in OPERANDS if shape is not None]


def scratch(plan):
    xy, z, rows = plan
    tokens_f32 = pltpu.VMEM((TOKENS, C), F32)
    row_stat = pltpu.VMEM((TOKENS, 1), F32)
    full_bias = pltpu.VMEM((HEADS, TOKENS, TOKENS), F32)
    weights = pltpu.VMEM((2, 3 * C // 2, C), BF16)
    qkv = pltpu.VMEM((TOKENS, 3 * C), BF16)
    kvt = pltpu.VMEM((2 * C, TOKENS), BF16)
    heads_t = pltpu.VMEM((C, TOKENS), BF16)
    dma = pltpu.SemaphoreType.DMA
    named = {name: pltpu.VMEM(shape, BF16) for name, shape in OPERANDS if shape is not None}
    named |= dict(
        load_sem=dma((len(OPERANDS),)),
        wp=weights,
        ws=weights,
        xf=tokens_f32,
        quads=pltpu.VMEM((4 * QUAD, C), F32),
        xhat_p=tokens_f32,
        rstd_p=row_stat,
        xhat_s=tokens_f32,
        rstd_s=row_stat,
        s2f=tokens_f32,
        dy2f=tokens_f32,
        qkv_p=qkv,
        kvt_p=kvt,
        qkv_s=qkv,
        kvt_s=kvt,
        probs_p=full_bias,
        probs_s=full_bias,
        ot_p=heads_t,
        ot_s=heads_t,
        dqkv=qkv,
        dqt=pltpu.VMEM((C, TOKENS), F32),
        bias_p=full_bias,
        bias_s=full_bias,
        tabf=pltpu.VMEM((16, 6400), F32),
        spread_p=pltpu.VMEM((2, TOKENS * 16, 128), F32),
        spread_s=pltpu.VMEM((2, TOKENS * 16, 128), F32),
        send=pltpu.VMEM((5, 4, QUAD, C), BF16),
        recv=pltpu.VMEM((5, 4, QUAD, C), BF16),
        halo_ss=dma((5, 4)),
        halo_rs=dma((5, 4)),
        w_ss=dma((4,)),
        w_rs=dma((4,)),
        f_ss=dma((4,)),
        f_rs=dma((4,)),
        part=pltpu.VMEM((2, C, C), F32),
        part16=pltpu.VMEM((2, C, C), BF16),
        half_in=pltpu.VMEM((2, C // 2, C), BF16),
        chunks=pltpu.VMEM((2, C // 2 // rows, rows, C), BF16),
        xy_in=pltpu.VMEM((2, xy, rows, C), BF16),
        z_in=pltpu.VMEM((2, z, rows, C), BF16),
        final=pltpu.VMEM((2, C, C), BF16),
        out_sem=dma((4,)),
        field_out=pltpu.VMEM((WLAT * WLON, LEV, C), BF16),
        grad_out=pltpu.VMEM((WLAT * WLON, LEV, C), BF16),
        c_ss=dma((2,)),
        c_rs=dma((2,)),
        xy_ss=dma((2,)),
        xy_rs=dma((2,)),
        z_ss=dma((2, 2)),
        z_rs=dma((2, 2)),
        fin_ss=dma((2,)),
        fin_rs=dma((2,)),
        half_ss=dma((2,)),
        half_rs=dma((2,)),
        roll=pltpu.SemaphoreType.REGULAR((3,)),
    )
    return named


def kernel(sizes, plan, names, *refs):
    run(sizes, plan, **dict(zip(names, refs)))


def run(
    sizes,
    plan,
    out_field,
    out_grad,
    gp_p,
    gp_s,
    wp,
    ws,
    xf,
    quads,
    xhat_p,
    rstd_p,
    xhat_s,
    rstd_s,
    s2f,
    dy2f,
    qkv_p,
    kvt_p,
    qkv_s,
    kvt_s,
    probs_p,
    probs_s,
    ot_p,
    ot_s,
    dqkv,
    dqt,
    bias_p,
    bias_s,
    tabf,
    spread_p,
    spread_s,
    send,
    recv,
    halo_ss,
    halo_rs,
    w_ss,
    w_rs,
    f_ss,
    f_rs,
    part,
    part16,
    half_in,
    chunks,
    xy_in,
    z_in,
    final,
    c_ss,
    c_rs,
    xy_ss,
    xy_rs,
    z_ss,
    z_rs,
    fin_ss,
    fin_rs,
    half_ss,
    half_rs,
    roll,
    load_sem,
    out_sem,
    field_out,
    grad_out,
    **local,
):
    n_lat, n_lon, n_dp = sizes
    lat, lon, dp = lax.axis_index("lat"), lax.axis_index("lon"), lax.axis_index("dp")
    core = lax.rem(lat, 2)
    sibling = (lat + 1 - 2 * core, lon, dp)
    across = (lat, lax.rem(lon + n_lon // 2, n_lon), 1 - dp)

    def near(dlat, dlon):
        return (
            lax.rem(lat + dlat + n_lat, n_lat),
            lax.rem(lon + dlon + n_lon, n_lon),
            dp,
        )

    xy, n_z, chunk_rows = plan
    n_y = n_lat // 2
    n_own = C // 2 // chunk_rows
    z = lax.rem(lon, n_z)
    x_lo, row = lax.div(lon, n_z), lax.div(lat, 2)

    def wrap(value, size):
        return jnp.where(value >= size, value - size, value)

    def place(move):
        lo, hi, up = move
        to_lo = 1 - x_lo if lo else x_lo
        to_hi = 1 - dp if hi else dp
        to_row = wrap(row + up, n_y)
        device = (2 * to_row + core, to_lo * n_z + z, to_hi)
        return (to_lo + 2 * to_hi) * n_y + to_row, device

    def hops(move):
        lo, hi, up = move
        return (1 if lo else 2 * hi) + min(up, n_y - up)

    moves = [(lo, hi, up) for lo in range(2) for hi in range(2) for up in range(n_y)][1:]
    moves = sorted(moves, key=hops, reverse=True)
    spot = place((0, 0, 0))[0]

    def at_z(d):
        return (lat, lon - z + wrap(z + d, n_z), dp)

    def greet(semaphore, device):
        pl.semaphore_signal(semaphore, inc=1, device_id=device, device_id_type=MESH)

    def along_z(d):
        return (lat, lon - z + lax.rem(z + d + 8 * n_z, n_z), dp)

    beside_x = (lat, across[1], dp)
    y_up, y_down = near(2, 0), near(-2, 0)
    barrier = pltpu.get_barrier_semaphore()
    around = [across, sibling, beside_x, y_up, y_down, along_z(1), along_z(-1)]
    around += [near(a, b) for a, b in ((1, 0), (-1, 0), (0, 1), (0, -1))]
    for device in around:
        greet(barrier, device)

    def tell(i):
        for device in (across, sibling, beside_x, y_up, y_down):
            greet(roll.at[i], device)
        for d in (2**i, -(2**i)):
            greet(roll.at[i], along_z(d))
        if i == 0:
            greet(roll.at[i], near(1, 0))
            greet(roll.at[i], near(-1, 0))

    def told(i):
        pl.semaphore_wait(roll.at[i], 9 if i == 0 else 7)

    results = [
        pltpu.make_async_copy(a, b, out_sem.at[i])
        for i, (a, b) in enumerate(
            ((final.at[0], gp_p), (final.at[1], gp_s), (field_out, out_field), (grad_out, out_grad))
        )
    ]
    loads = {}
    for i, (name, shape) in enumerate(OPERANDS):
        source = local[name + "_hbm"]
        target = local[name] if shape else {"wp_half": wp, "ws_half": ws}[name].at[dp]
        loads[name] = pltpu.make_async_copy(source, target, load_sem.at[i])
        loads[name].start()
    wp_half, ws_half = local["wp_half_hbm"], local["ws_half_hbm"]
    field, cot, proj_p, proj_s, tab_p, tab_s, gather, scatter, pick = (
        local[name]
        for name in (
            "field", "cot", "proj_p", "proj_s", "tab_p", "tab_s", "gather", "scatter", "pick"
        )
    )
    pl.semaphore_wait(barrier, len(around))

    def piece(i, n):
        size = 288 // n
        return pl.ds(pl.multiple_of(core * 288 + i * size, 16), size)

    def weights_across(source, full, at, i):
        return pltpu.make_async_remote_copy(
            source.at[at],
            full.at[dp, at],
            w_ss.at[i],
            w_rs.at[i],
            device_id=across,
            device_id_type=MESH,
        )

    def weights_beside(full, at, i):
        part = full.at[1 - dp, at]
        return pltpu.make_async_remote_copy(
            part, part, f_ss.at[i], f_rs.at[i], device_id=sibling, device_id_type=MESH
        )

    places = [(wp_half, wp, piece(i, 3)) for i in range(3)] + [(ws_half, ws, piece(0, 1))]
    first = [weights_across(*place, i) for i, place in enumerate(places)]
    beside = [weights_beside(*place[1:], i) for i, place in enumerate(places)]
    for copy in first[:3]:
        copy.start()
    tell(0)

    def halo(i, by):
        kept = 3 if by < 0 else 0
        copies = []
        for slot in range(4):
            if slot == kept:
                recv[i, 3 - slot] = send[i, slot]
                continue
            a, b = divmod(slot, 2)
            moves = 0 if by < 0 else 1
            copies.append(
                pltpu.make_async_remote_copy(
                    send.at[i, slot],
                    recv.at[i, 3 - slot],
                    halo_ss.at[i, slot],
                    halo_rs.at[i, 3 - slot],
                    device_id=near(by if a == moves else 0, by if b == moves else 0),
                    device_id_type=MESH,
                )
            )
        for copy in copies:
            copy.start()
        return copies

    def arrived(i, copies):
        for copy in copies:
            copy.wait_recv()
        return nn(gather[...], recv[i].reshape(4 * QUAD, C))

    def to_quads(i, x):
        send[i] = nn(scatter[...], x).astype(BF16).reshape(4, QUAD, C)

    loads["cot"].wait()
    quads[...] = jnp.zeros_like(quads)
    for h in range(WLAT):
        for w in range(WLON):
            at = ((h // 6) * 2 + w // 3) * QUAD + ((h % 6) * 3 + w % 3) * 2
            quads[at : at + 2, :] = cot[h * WLON + w].astype(F32)
    send[0] = quads[...].astype(BF16).reshape(4, QUAD, C)

    loads["field"].wait()
    for i in range(WLAT * WLON):
        xf[2 * i : 2 * i + 2, :] = field[i].astype(F32)

    def norm(x, xhat, rstd):
        mean = jnp.mean(x, axis=-1, keepdims=True)
        centred = x - mean
        r = lax.rsqrt(jnp.mean(centred * centred, axis=-1, keepdims=True) + 1e-5)
        y = centred * r
        xhat[...] = y
        rstd[...] = r
        return y.astype(BF16)

    lane256 = lax.broadcasted_iota(jnp.int32, (16, 256), 1)

    def align(tab, spread, start, stop):
        if start == 0:
            tabf[...] = jnp.zeros_like(tabf)
            tabf[0:HEADS, 0 : 4 * WLAT * CHUNK] = tab[...].astype(F32)

        def row(h, carry):
            for za in range(LEV):
                parts = []
                for zb in range(LEV):
                    c = (za * 2 + zb) * WLAT + h
                    tile = c + c // 32
                    off = 4 * lax.rem(c, 32)
                    window = tabf[:, pl.ds(pl.multiple_of(tile * 128, 128), 256)]
                    parts.append(pltpu.roll(window, lax.rem(256 + 127 * zb - off, 256), 1))
                for w in range(WLON):
                    low, high = parts
                    if w:
                        low = pltpu.roll(low, 256 - w, 1)
                        high = pltpu.roll(high, 256 - w, 1)
                    at = pl.multiple_of((h * WLON + w) * 32 + za * 16, 16)
                    both = jnp.where(lane256 < 127, low, high)
                    spread[0, pl.ds(at, 16), :] = both[:, :128]
                    spread[1, pl.ds(at, 16), :] = both[:, 128:]
            return carry

        lax.fori_loop(start, stop, row, 0)

    def expand(spread, bias, hide):
        for head in range(HEADS):
            lanes = [spread[half, pl.ds(head, TOKENS, stride=16), :] for half in range(2)]
            table = jnp.concatenate(lanes, axis=1).astype(BF16)
            full = nt(pick[...], table)
            bias[head] = full if hide is None else full + hide

    lane = lax.broadcasted_iota(jnp.int32, (TOKENS, 128), 1) // HEAD

    def by_head(x):
        zero = jnp.zeros_like(x)
        return jnp.concatenate([jnp.where(lane == j, x, zero) for j in range(PER)], axis=0)

    def own_lanes(x):
        total = jnp.where(lane == 0, x[0:TOKENS], 0.0)
        for j in range(1, PER):
            total += jnp.where(lane == j, x[j * TOKENS : (j + 1) * TOKENS], 0.0)
        return total

    scale = 1.0 / HEAD**0.5

    def project(n, full, qkv, kvt):
        w = full[...].reshape(3 * C, C)
        qkv[...] = nt(n, w).astype(BF16)
        kvt[...] = nt(w[C:], n).astype(BF16)

    def softmax(g, qkv, bias):
        q = qkv[:, g * 128 : (g + 1) * 128]
        k = qkv[:, C + g * 128 : C + (g + 1) * 128]
        s = nt(by_head(k), q).reshape(PER, TOKENS, TOKENS) * scale
        s = s + bias[g * PER : (g + 1) * PER]
        e = jnp.exp(s - jnp.max(s, axis=1, keepdims=True))
        return e / jnp.sum(e, axis=1, keepdims=True)

    def values(g, p, kvt, ot):
        for j in range(PER):
            at = g * 128 + j * HEAD
            vt = kvt[C + at : C + at + HEAD, :]
            ot[at : at + HEAD, :] = nn(vt, p[j]).astype(BF16)

    def grads(g, p, pb, do, qkv, kvt):
        cols = slice(g * 128, (g + 1) * 128)
        q = qkv[:, cols]
        v = qkv[:, 2 * C + g * 128 : 2 * C + (g + 1) * 128]
        dog = do[:, cols]
        dp_ = nt(by_head(v), dog).reshape(PER, TOKENS, TOKENS)
        inner = jnp.sum(p * dp_, axis=1, keepdims=True)
        ds = (p * (dp_ - inner)).astype(BF16)
        dv = own_lanes(nn(pb.reshape(PER * TOKENS, TOKENS), dog))
        dk = own_lanes(nn(ds.reshape(PER * TOKENS, TOKENS), q)) * scale
        dqkv[:, 2 * C + g * 128 : 2 * C + (g + 1) * 128] = dv.astype(BF16)
        dqkv[:, C + g * 128 : C + (g + 1) * 128] = dk.astype(BF16)
        for j in range(PER):
            at = g * 128 + j * HEAD
            dqt[at : at + HEAD, :] = nn(kvt[at : at + HEAD, :], ds[j]) * scale

    def input_grad(dy, full, xhat, rstd):
        dqkv[:, 0:C] = dqt[...].T.astype(BF16)
        dn = nn(dqkv[...], full[...].reshape(3 * C, C))
        xh = xhat[...]
        mean = jnp.mean(dn, axis=-1, keepdims=True)
        product = jnp.mean(dn * xh, axis=-1, keepdims=True)
        return (dy + rstd[...] * (dn - mean - xh * product)).astype(BF16)

    def heads(ot):
        return ot[...].astype(F32).T.astype(BF16)

    def output(x, o, proj):
        return (x + nn(o, proj[...])).astype(BF16)

    def copy_core(m):
        return pltpu.make_async_remote_copy(
            part16.at[m, half(1 - core)],
            half_in.at[m],
            c_ss.at[m],
            c_rs.at[m],
            device_id=sibling,
            device_id_type=MESH,
        )

    def owned(m, e):
        e = e - m * n_y
        return jnp.where(e < 0, e + xy, e)

    mine = [jnp.minimum(owned(m, spot), n_own - 1) for m in range(2)]

    def if_owner(m):
        return pl.when(owned(m, spot) < n_own)

    def if_not_owner(m):
        return pl.when(owned(m, spot) >= n_own)

    def remote(source, target, ss, rs, device=sibling):
        return pltpu.make_async_remote_copy(
            source, target, ss, rs, device_id=device, device_id_type=MESH
        )

    def chunk(index, n=1):
        return pl.ds(pl.multiple_of(index * chunk_rows, 16), n * chunk_rows)

    def half(c):
        return pl.ds(pl.multiple_of(c * (C // 2), 64), C // 2)

    far_first = [d for i in range(n_z) for d in (n_z // 2 + i, n_z // 2 - i)]
    far_first = [d for d in dict.fromkeys(far_first) if 0 < d < n_z]
    z_steps = [[8, 4, 12], [2, 1, 15]] if n_z == 16 else [far_first]
    z_order = [lax.div(z, 4), 4 + lax.rem(z, 4)] if n_z == 16 else [z]
    z_slots = [(0, 4), (4, 4)] if n_z == 16 else [(0, n_z)]

    def sum_start(m, total):
        part[m] = total
        part16[m] = total.astype(BF16)
        copy_core(m).start()

    def sum_xy(m):
        copy_core(m).wait_recv()
        both = part[m, half(core), :] + half_in[m].astype(F32)
        chunks[m] = both.astype(BF16).reshape(n_own, chunk_rows, C)
        for move in moves:
            to, device = place(move)
            k = owned(m, to)

            @pl.when(k < n_own)
            def _():
                source = chunks.at[m, jnp.minimum(k, n_own - 1)]
                remote(source, xy_in.at[m, spot], xy_ss.at[m], xy_rs.at[m], device).start()

    def z_send(m, i, value):
        slot = z_order[i]
        z_in[m, slot] = value.astype(BF16)
        for d in z_steps[i]:
            block = z_in.at[m, slot]
            remote(block, block, z_ss.at[m, i], z_rs.at[m, i], at_z(d)).start()

    def z_sum(m, i):
        at, n = z_slots[i]
        if n > 1:
            several = z_in.at[m, at : at + n - 1]
            remote(several, several, z_ss.at[m, i], z_rs.at[m, i]).wait_recv()
        return jnp.sum(z_in[m, at : at + n].astype(F32), axis=0)

    def sum_z(m):
        @if_owner(m)
        def _():
            xy_in[m, spot] = chunks[m, mine[m]]
            several = xy_in.at[m, 0 : xy - 1]
            remote(several, several, xy_ss.at[m], xy_rs.at[m]).wait_recv()
            z_send(m, 0, jnp.sum(xy_in[m].astype(F32), axis=0))

    def sum_z_again(m):
        if len(z_steps) > 1:

            @if_owner(m)
            def _():
                z_send(m, 1, z_sum(m, 0))

    def sum_back(m):
        @if_owner(m)
        def _():
            block = final.at[m, chunk(core * n_own + mine[m])]
            final[m, chunk(core * n_own + mine[m]), :] = z_sum(m, len(z_steps) - 1).astype(BF16)
            for move in moves:
                remote(block, block, fin_ss.at[m], fin_rs.at[m], place(move)[1]).start()

    def sum_share(m):
        def wait(n):
            several = final.at[m, 0 : n * chunk_rows]
            remote(several, several, fin_ss.at[m], fin_rs.at[m]).wait_recv()

        if_owner(m)(lambda: wait(n_own - 1))
        if_not_owner(m)(lambda: wait(n_own))
        block = final.at[m, half(core)]
        remote(block, block, half_ss.at[m], half_rs.at[m]).start()

    def sum_end(m):
        block = final.at[m, half(core)]
        remote(block, block, half_ss.at[m], half_rs.at[m]).wait_recv()
        results[m].start()

    def sum_sent(m):
        copy_core(m).wait_send()
        block = final.at[m, half(core)]
        remote(block, block, half_ss.at[m], half_rs.at[m]).wait_send()

        def wait(n):
            several = chunks.at[m, 0:n]
            remote(several, several, xy_ss.at[m], xy_rs.at[m]).wait_send()

        @if_not_owner(m)
        def _():
            wait(n_own)

        @if_owner(m)
        def _():
            wait(n_own - 1)
            several = xy_in.at[m, 0 : xy - 1]
            remote(several, several, fin_ss.at[m], fin_rs.at[m]).wait_send()
            for i, (at, n) in enumerate(z_slots):
                if n > 1:
                    several = z_in.at[m, at : at + n - 1]
                    remote(several, several, z_ss.at[m, i], z_rs.at[m, i]).wait_send()

    n1 = norm(xf[...], xhat_p, rstd_p)
    loads["tab_p"].wait()
    align(tab_p, spread_p, 0, WLAT)
    loads["pick"].wait()
    expand(spread_p, bias_p, None)
    told(0)
    tell(1)
    halo_cot = halo(0, -1)
    loads["tab_s"].wait()
    align(tab_s, spread_s, 0, 6)
    for arriving, passed_on in zip(first[:3], beside[:3]):
        arriving.wait_recv()
        passed_on.start()
    for copy in first[:3]:
        copy.wait_send()
    first[3].start()
    loads["wp_half"].wait()
    for copy in beside[:3]:
        copy.wait_recv()
    told(1)
    tell(2)
    project(n1, wp, qkv_p, kvt_p)
    for g in range(GROUPS):
        p = softmax(g, qkv_p, bias_p)
        probs_p[g * PER : (g + 1) * PER] = p
        values(g, p.astype(BF16), kvt_p, ot_p)
    loads["proj_p"].wait()
    loads["scatter"].wait()
    o1 = heads(ot_p)
    to_quads(1, output(xf[...], o1, proj_p))
    halo_h1 = halo(1, -1)

    loads["gather"].wait()
    dy2 = arrived(0, halo_cot)
    dy2f[...] = dy2
    loads["proj_s"].wait()
    do2 = nt(dy2.astype(BF16), proj_s[...]).astype(BF16)
    key = lax.broadcasted_iota(jnp.int32, (TOKENS, TOKENS), 0)
    query = lax.broadcasted_iota(jnp.int32, (TOKENS, TOKENS), 1)
    edge = jnp.where(lat == n_lat - 1, TOKENS // 2, TOKENS)
    same = ((key & 1) == (query & 1)) & ((key >= edge) == (query >= edge))
    to_quads(4, o1)
    halo_o1 = halo(4, -1)
    align(tab_s, spread_s, 6, WLAT)
    first[3].wait_recv()
    beside[3].start()
    expand(spread_s, bias_s, jnp.where(same, 0.0, -1e30))
    loads["ws_half"].wait()
    beside[3].wait_recv()
    told(2)

    s2 = arrived(1, halo_h1)
    s2f[...] = s2
    n2 = norm(s2, xhat_s, rstd_s)
    project(n2, ws, qkv_s, kvt_s)
    for g in range(GROUPS):
        p = softmax(g, qkv_s, bias_s)
        probs_s[g * PER : (g + 1) * PER] = p
        values(g, p.astype(BF16), kvt_s, ot_s)
    sum_start(1, nn(ot_s[...], dy2f[...].astype(BF16)))
    for g in range(GROUPS):
        p = probs_s[g * PER : (g + 1) * PER]
        grads(g, p, p.astype(BF16), do2, qkv_s, kvt_s)
    sum_xy(1)
    ds2 = input_grad(dy2f[...], ws, xhat_s, rstd_s)
    ot_r = arrived(4, halo_o1).T.astype(BF16)
    sum_start(0, nn(ot_r, ds2))
    to_quads(2, ds2)
    halo_g1 = halo(2, 1)

    y2 = output(s2f[...], heads(ot_s), proj_s)
    to_quads(3, y2)
    halo_out = halo(3, 1)
    sum_xy(0)
    sum_z(1)

    g1 = arrived(2, halo_g1)
    do1 = nt(g1.astype(BF16), proj_p[...]).astype(BF16)
    for g in range(GROUPS):
        p = probs_p[g * PER : (g + 1) * PER]
        grads(g, p, p.astype(BF16), do1, qkv_p, kvt_p)
        if g == 1:
            sum_z(0)
    xf[...] = input_grad(g1, wp, xhat_p, rstd_p).astype(F32)
    for i in range(WLAT * WLON):
        grad_out[i] = xf[2 * i : 2 * i + 2, :].astype(BF16)
    results[3].start()
    s2f[...] = arrived(3, halo_out)
    for i in range(WLAT * WLON):
        field_out[i] = s2f[2 * i : 2 * i + 2, :].astype(BF16)
    results[2].start()
    sum_z_again(1)
    sum_z_again(0)
    sum_back(1)
    sum_back(0)
    for copies in (halo_cot, halo_h1, halo_o1, halo_g1, halo_out, first[3:], beside):
        for copy in copies:
            copy.wait_send()
    sum_share(1)
    sum_share(0)
    sum_end(1)
    sum_end(0)
    sum_sent(1)
    sum_sent(0)
    for copy in results:
        copy.wait()


def store(*refs):
    sources, targets, staged, semaphores = refs[:4], refs[4:8], refs[8:12], refs[12]
    taken = [pltpu.make_async_copy(sources[i], staged[i], semaphores.at[i]) for i in range(4)]
    given = [pltpu.make_async_copy(staged[i], targets[i], semaphores.at[4 + i]) for i in range(4)]
    for copy in taken:
        copy.start()
    for before, after in zip(taken, given):
        before.wait()
        after.start()
    for copy in given:
        copy.wait()


def body(sizes, field, cotangent, qkv_plain, proj_plain, bias_plain, qkv_shift, proj_shift, bias_shift):
    def rows(x):
        return x.transpose(0, 2, 3, 1, 4).reshape(WLAT * WLON, LEV, C)

    gather, scatter, pick = constants()
    operands = dict(
        field=rows(field),
        cot=rows(cotangent),
        wp_half=qkv_plain.T,
        ws_half=qkv_shift.T,
        proj_p=proj_plain,
        proj_s=proj_shift,
        tab_p=bias_plain.reshape(HEADS, -1),
        tab_s=bias_shift.reshape(HEADS, -1),
        gather=jnp.asarray(gather, BF16),
        scatter=jnp.asarray(scatter, BF16),
        pick=jnp.asarray(pick, BF16),
    )
    n_lat, n_lon, n_dp = sizes
    xy = n_lat // 2 * 2 * n_dp
    owners = max(d for d in (1, 2, 3, 4, 6, 12) if d <= xy)
    plan = (xy, n_lon // 2, C // 2 // owners)
    buffers = scratch(plan)
    hbm = pl.BlockSpec(memory_space=pl.ANY)
    grid_shape = jax.ShapeDtypeStruct((WLAT * WLON, LEV, C), BF16)
    square = jax.ShapeDtypeStruct((C, C), BF16)
    names = [name + "_hbm" for name, _ in OPERANDS]
    names += ["out_field", "out_grad", "gp_p", "gp_s"] + list(buffers)
    out_field, out_grad, gp_p, gp_s = pl.pallas_call(
        functools.partial(kernel, sizes, plan, names),
        out_shape=(grid_shape, grid_shape, square, square),
        in_specs=[hbm] * len(OPERANDS),
        out_specs=[hbm] * 4,
        scratch_shapes=list(buffers.values()),
        compiler_params=pltpu.CompilerParams(
            collective_id=0, has_side_effects=True, vmem_limit_bytes=56 * 2**20
        ),
    )(*[operands[name] for name, _ in OPERANDS])

    results = (out_field, out_grad, gp_p, gp_s)
    out_field, out_grad, gp_p, gp_s = pl.pallas_call(
        store,
        out_shape=tuple(jax.ShapeDtypeStruct(x.shape, x.dtype) for x in results),
        in_specs=[hbm] * 4,
        out_specs=[hbm] * 4,
        scratch_shapes=[pltpu.VMEM(x.shape, x.dtype) for x in results]
        + [pltpu.SemaphoreType.DMA((8,))],
        compiler_params=pltpu.CompilerParams(vmem_limit_bytes=56 * 2**20),
    )(*results)

    def grid(x):
        return x.reshape(1, WLAT, WLON, LEV, C).transpose(0, 3, 1, 2, 4)

    return grid(out_field), grid(out_grad), gp_p, gp_s


def solution(mesh):
    sizes = tuple(mesh.shape[a] for a in ("lat", "lon", "dp"))
    grid = P("dp", None, "lat", "lon", None)
    table = P(None, "lat", None, None)
    columns = P(None, "dp")
    return jax.shard_map(
        functools.partial(body, sizes),
        mesh=mesh,
        in_specs=(grid, grid, columns, P(), table, columns, P(), table),
        out_specs=(grid, grid, P(), P()),
        check_vma=False,
    )
```

```python
import functools

import jax
import jax.numpy as jnp
import numpy as np
from jax import lax
from jax.experimental import pallas as pl
from jax.experimental.pallas import tpu as pltpu
from jax.sharding import PartitionSpec as P

HEADS = 12
HEAD = 32
C = 384
LEV = 2
WLAT = 12
WLON = 6
TOKENS = LEV * WLAT * WLON
QUAD = 48
GROUPS = 3
PER = HEADS // GROUPS
REL = 2 * WLON - 1
CHUNK = WLAT * REL
MESH = pl.DeviceIdType.MESH
F32 = jnp.float32
BF16 = jnp.bfloat16


def nn(a, b):
    return lax.dot_general(a, b, (((1,), (0,)), ((), ())), preferred_element_type=F32)


def nt(a, b):
    return lax.dot_general(a, b, (((1,), (1,)), ((), ())), preferred_element_type=F32)


def token(h, w, z):
    return (h * WLON + w) * LEV + z


def constants():
    gather = np.zeros((TOKENS, 4 * QUAD), np.float32)
    pick = np.zeros((TOKENS, 256), np.float32)
    for h in range(WLAT):
        for w in range(WLON):
            for z in range(LEV):
                slot = (h // 6) * 2 + w // 3
                inner = ((h % 6) * 3 + w % 3) * 2 + (1 - z)
                gather[token(h, w, z), slot * QUAD + inner] = 1
                pick[token(h, w, z), z * 127 + h * REL + WLON - 1 - w] = 1
    scatter = np.zeros((4 * QUAD, TOKENS), np.float32)
    for h in range(WLAT):
        for w in range(WLON):
            for z in range(LEV):
                slot = (h // 6) * 2 + w // 3
                scatter[slot * QUAD + ((h % 6) * 3 + w % 3) * 2 + z, token(h, w, z)] = 1
    return gather, scatter, pick


OPERANDS = (
    ("field", (WLAT * WLON, LEV, C)),
    ("cot", (WLAT * WLON, LEV, C)),
    ("wp_half", None),
    ("ws_half", None),
    ("tab_p", (HEADS, 4 * WLAT * CHUNK)),
    ("tab_s", (HEADS, 4 * WLAT * CHUNK)),
    ("scatter", (4 * QUAD, TOKENS)),
    ("gather", (TOKENS, 4 * QUAD)),
    ("pick", (TOKENS, 256)),
    ("proj_p", (C, C)),
    ("proj_s", (C, C)),
)
LOADED = [name for name, shape in OPERANDS if shape is not None]


def scratch(plan):
    xy, z, rows = plan
    tokens_f32 = pltpu.VMEM((TOKENS, C), F32)
    row_stat = pltpu.VMEM((TOKENS, 1), F32)
    full_bias = pltpu.VMEM((HEADS, TOKENS, TOKENS), F32)
    weights = pltpu.VMEM((2, 3 * C // 2, C), BF16)
    qkv = pltpu.VMEM((TOKENS, 3 * C), BF16)
    kvt = pltpu.VMEM((2 * C, TOKENS), BF16)
    heads_t = pltpu.VMEM((C, TOKENS), BF16)
    dma = pltpu.SemaphoreType.DMA
    named = {name: pltpu.VMEM(shape, BF16) for name, shape in OPERANDS if shape is not None}
    named |= dict(
        load_sem=dma((len(OPERANDS),)),
        wp=weights,
        ws=weights,
        xf=tokens_f32,
        quads=pltpu.VMEM((4 * QUAD, C), F32),
        xhat_p=tokens_f32,
        rstd_p=row_stat,
        xhat_s=tokens_f32,
        rstd_s=row_stat,
        s2f=tokens_f32,
        dy2f=tokens_f32,
        qkv_p=qkv,
        kvt_p=kvt,
        qkv_s=qkv,
        kvt_s=kvt,
        probs_p=full_bias,
        probs_s=full_bias,
        ot_p=heads_t,
        ot_s=heads_t,
        dqkv=qkv,
        dqt=pltpu.VMEM((C, TOKENS), F32),
        bias_p=full_bias,
        bias_s=full_bias,
        tabf=pltpu.VMEM((16, 6400), F32),
        spread_p=pltpu.VMEM((2, TOKENS * 16, 128), F32),
        spread_s=pltpu.VMEM((2, TOKENS * 16, 128), F32),
        send=pltpu.VMEM((5, 4, QUAD, C), BF16),
        recv=pltpu.VMEM((5, 4, QUAD, C), BF16),
        halo_ss=dma((5, 4)),
        halo_rs=dma((5, 4)),
        w_ss=dma((4,)),
        w_rs=dma((4,)),
        f_ss=dma((4,)),
        f_rs=dma((4,)),
        part=pltpu.VMEM((2, C, C), F32),
        part16=pltpu.VMEM((2, C, C), BF16),
        half_in=pltpu.VMEM((2, C // 2, C), BF16),
        chunks=pltpu.VMEM((2, C // 2 // rows, rows, C), BF16),
        xy_in=pltpu.VMEM((2, xy, rows, C), BF16),
        z_in=pltpu.VMEM((2, z, rows, C), BF16),
        final=pltpu.VMEM((2, C, C), BF16),
        out_sem=dma((4,)),
        field_out=pltpu.VMEM((WLAT * WLON, LEV, C), BF16),
        grad_out=pltpu.VMEM((WLAT * WLON, LEV, C), BF16),
        c_ss=dma((2,)),
        c_rs=dma((2,)),
        xy_ss=dma((2,)),
        xy_rs=dma((2,)),
        z_ss=dma((2, 2)),
        z_rs=dma((2, 2)),
        fin_ss=dma((2,)),
        fin_rs=dma((2,)),
        half_ss=dma((2,)),
        half_rs=dma((2,)),
        roll=pltpu.SemaphoreType.REGULAR((3,)),
    )
    return named


def kernel(sizes, plan, names, *refs):
    run(sizes, plan, **dict(zip(names, refs)))


def run(
    sizes,
    plan,
    out_field,
    out_grad,
    gp_p,
    gp_s,
    wp,
    ws,
    xf,
    quads,
    xhat_p,
    rstd_p,
    xhat_s,
    rstd_s,
    s2f,
    dy2f,
    qkv_p,
    kvt_p,
    qkv_s,
    kvt_s,
    probs_p,
    probs_s,
    ot_p,
    ot_s,
    dqkv,
    dqt,
    bias_p,
    bias_s,
    tabf,
    spread_p,
    spread_s,
    send,
    recv,
    halo_ss,
    halo_rs,
    w_ss,
    w_rs,
    f_ss,
    f_rs,
    part,
    part16,
    half_in,
    chunks,
    xy_in,
    z_in,
    final,
    c_ss,
    c_rs,
    xy_ss,
    xy_rs,
    z_ss,
    z_rs,
    fin_ss,
    fin_rs,
    half_ss,
    half_rs,
    roll,
    load_sem,
    out_sem,
    field_out,
    grad_out,
    **local,
):
    n_lat, n_lon, n_dp = sizes
    lat, lon, dp = lax.axis_index("lat"), lax.axis_index("lon"), lax.axis_index("dp")
    core = lax.rem(lat, 2)
    sibling = (lat + 1 - 2 * core, lon, dp)
    across = (lat, lax.rem(lon + n_lon // 2, n_lon), 1 - dp)

    def near(dlat, dlon):
        return (
            lax.rem(lat + dlat + n_lat, n_lat),
            lax.rem(lon + dlon + n_lon, n_lon),
            dp,
        )

    xy, n_z, chunk_rows = plan
    n_y = n_lat // 2
    n_own = C // 2 // chunk_rows
    z = lax.rem(lon, n_z)
    x_lo, row = lax.div(lon, n_z), lax.div(lat, 2)

    def wrap(value, size):
        return jnp.where(value >= size, value - size, value)

    def place(move):
        lo, hi, up = move
        to_lo = 1 - x_lo if lo else x_lo
        to_hi = 1 - dp if hi else dp
        to_row = wrap(row + up, n_y)
        device = (2 * to_row + core, to_lo * n_z + z, to_hi)
        return (to_lo + 2 * to_hi) * n_y + to_row, device

    def hops(move):
        lo, hi, up = move
        return (1 if lo else 2 * hi) + min(up, n_y - up)

    moves = [(lo, hi, up) for lo in range(2) for hi in range(2) for up in range(n_y)][1:]
    moves = sorted(moves, key=hops, reverse=True)
    spot = place((0, 0, 0))[0]

    def at_z(d):
        return (lat, lon - z + wrap(z + d, n_z), dp)

    def greet(semaphore, device):
        pl.semaphore_signal(semaphore, inc=1, device_id=device, device_id_type=MESH)

    def along_z(d):
        return (lat, lon - z + lax.rem(z + d + 8 * n_z, n_z), dp)

    beside_x = (lat, across[1], dp)
    y_up, y_down = near(2, 0), near(-2, 0)
    barrier = pltpu.get_barrier_semaphore()
    around = [across, sibling, beside_x, y_up, y_down, along_z(1), along_z(-1)]
    around += [near(a, b) for a, b in ((1, 0), (-1, 0), (0, 1), (0, -1))]
    for device in around:
        greet(barrier, device)

    def tell(i):
        for device in (across, sibling, beside_x, y_up, y_down):
            greet(roll.at[i], device)
        for d in (2**i, -(2**i)):
            greet(roll.at[i], along_z(d))
        if i == 0:
            greet(roll.at[i], near(1, 0))
            greet(roll.at[i], near(-1, 0))

    def told(i):
        pl.semaphore_wait(roll.at[i], 9 if i == 0 else 7)

    results = [
        pltpu.make_async_copy(a, b, out_sem.at[i])
        for i, (a, b) in enumerate(
            ((final.at[0], gp_p), (final.at[1], gp_s), (field_out, out_field), (grad_out, out_grad))
        )
    ]
    loads = {}
    for i, (name, shape) in enumerate(OPERANDS):
        source = local[name + "_hbm"]
        target = local[name] if shape else {"wp_half": wp, "ws_half": ws}[name].at[dp]
        loads[name] = pltpu.make_async_copy(source, target, load_sem.at[i])
        loads[name].start()
    wp_half, ws_half = local["wp_half_hbm"], local["ws_half_hbm"]
    field, cot, proj_p, proj_s, tab_p, tab_s, gather, scatter, pick = (
        local[name]
        for name in (
            "field", "cot", "proj_p", "proj_s", "tab_p", "tab_s", "gather", "scatter", "pick"
        )
    )
    pl.semaphore_wait(barrier, len(around))

    def piece(i, n):
        size = 288 // n
        return pl.ds(pl.multiple_of(core * 288 + i * size, 16), size)

    def weights_across(source, full, at, i):
        return pltpu.make_async_remote_copy(
            source.at[at],
            full.at[dp, at],
            w_ss.at[i],
            w_rs.at[i],
            device_id=across,
            device_id_type=MESH,
        )

    def weights_beside(full, at, i):
        part = full.at[1 - dp, at]
        return pltpu.make_async_remote_copy(
            part, part, f_ss.at[i], f_rs.at[i], device_id=sibling, device_id_type=MESH
        )

    places = [(wp_half, wp, piece(i, 3)) for i in range(3)] + [(ws_half, ws, piece(0, 1))]
    first = [weights_across(*place, i) for i, place in enumerate(places)]
    beside = [weights_beside(*place[1:], i) for i, place in enumerate(places)]
    for copy in first[:3]:
        copy.start()
    tell(0)

    def halo(i, by):
        kept = 3 if by < 0 else 0
        copies = []
        for slot in range(4):
            if slot == kept:
                recv[i, 3 - slot] = send[i, slot]
                continue
            a, b = divmod(slot, 2)
            moves = 0 if by < 0 else 1
            copies.append(
                pltpu.make_async_remote_copy(
                    send.at[i, slot],
                    recv.at[i, 3 - slot],
                    halo_ss.at[i, slot],
                    halo_rs.at[i, 3 - slot],
                    device_id=near(by if a == moves else 0, by if b == moves else 0),
                    device_id_type=MESH,
                )
            )
        for copy in copies:
            copy.start()
        return copies

    def arrived(i, copies):
        for copy in copies:
            copy.wait_recv()
        return nn(gather[...], recv[i].reshape(4 * QUAD, C))

    def to_quads(i, x):
        send[i] = nn(scatter[...], x).astype(BF16).reshape(4, QUAD, C)

    loads["cot"].wait()
    quads[...] = jnp.zeros_like(quads)
    for h in range(WLAT):
        for w in range(WLON):
            at = ((h // 6) * 2 + w // 3) * QUAD + ((h % 6) * 3 + w % 3) * 2
            quads[at : at + 2, :] = cot[h * WLON + w].astype(F32)
    send[0] = quads[...].astype(BF16).reshape(4, QUAD, C)

    loads["field"].wait()
    for i in range(WLAT * WLON):
        xf[2 * i : 2 * i + 2, :] = field[i].astype(F32)

    def norm(x, xhat, rstd):
        mean = jnp.mean(x, axis=-1, keepdims=True)
        centred = x - mean
        r = lax.rsqrt(jnp.mean(centred * centred, axis=-1, keepdims=True) + 1e-5)
        y = centred * r
        xhat[...] = y
        rstd[...] = r
        return y.astype(BF16)

    lane256 = lax.broadcasted_iota(jnp.int32, (16, 256), 1)

    def align(tab, spread, start, stop):
        if start == 0:
            tabf[...] = jnp.zeros_like(tabf)
            tabf[0:HEADS, 0 : 4 * WLAT * CHUNK] = tab[...].astype(F32)

        def row(h, carry):
            for za in range(LEV):
                parts = []
                for zb in range(LEV):
                    c = (za * 2 + zb) * WLAT + h
                    tile = c + c // 32
                    off = 4 * lax.rem(c, 32)
                    window = tabf[:, pl.ds(pl.multiple_of(tile * 128, 128), 256)]
                    parts.append(pltpu.roll(window, lax.rem(256 + 127 * zb - off, 256), 1))
                for w in range(WLON):
                    low, high = parts
                    if w:
                        low = pltpu.roll(low, 256 - w, 1)
                        high = pltpu.roll(high, 256 - w, 1)
                    at = pl.multiple_of((h * WLON + w) * 32 + za * 16, 16)
                    both = jnp.where(lane256 < 127, low, high)
                    spread[0, pl.ds(at, 16), :] = both[:, :128]
                    spread[1, pl.ds(at, 16), :] = both[:, 128:]
            return carry

        lax.fori_loop(start, stop, row, 0)

    def expand(spread, bias, hide):
        for head in range(HEADS):
            lanes = [spread[half, pl.ds(head, TOKENS, stride=16), :] for half in range(2)]
            table = jnp.concatenate(lanes, axis=1).astype(BF16)
            full = nt(pick[...], table)
            bias[head] = full if hide is None else full + hide

    lane = lax.broadcasted_iota(jnp.int32, (TOKENS, 128), 1) // HEAD

    def by_head(x):
        zero = jnp.zeros_like(x)
        return jnp.concatenate([jnp.where(lane == j, x, zero) for j in range(PER)], axis=0)

    def own_lanes(x):
        total = jnp.where(lane == 0, x[0:TOKENS], 0.0)
        for j in range(1, PER):
            total += jnp.where(lane == j, x[j * TOKENS : (j + 1) * TOKENS], 0.0)
        return total

    scale = 1.0 / HEAD**0.5

    def project(n, full, qkv, kvt):
        w = full[...].reshape(3 * C, C)
        qkv[...] = nt(n, w).astype(BF16)
        kvt[...] = nt(w[C:], n).astype(BF16)

    def softmax(g, qkv, bias):
        q = qkv[:, g * 128 : (g + 1) * 128]
        k = qkv[:, C + g * 128 : C + (g + 1) * 128]
        s = nt(by_head(k), q).reshape(PER, TOKENS, TOKENS) * scale
        s = s + bias[g * PER : (g + 1) * PER]
        e = jnp.exp(s - jnp.max(s, axis=1, keepdims=True))
        return e / jnp.sum(e, axis=1, keepdims=True)

    def values(g, p, kvt, ot):
        for j in range(PER):
            at = g * 128 + j * HEAD
            vt = kvt[C + at : C + at + HEAD, :]
            ot[at : at + HEAD, :] = nn(vt, p[j]).astype(BF16)

    def grads(g, p, pb, do, qkv, kvt):
        cols = slice(g * 128, (g + 1) * 128)
        q = qkv[:, cols]
        v = qkv[:, 2 * C + g * 128 : 2 * C + (g + 1) * 128]
        dog = do[:, cols]
        dp_ = nt(by_head(v), dog).reshape(PER, TOKENS, TOKENS)
        inner = jnp.sum(p * dp_, axis=1, keepdims=True)
        ds = (p * (dp_ - inner)).astype(BF16)
        dv = own_lanes(nn(pb.reshape(PER * TOKENS, TOKENS), dog))
        dk = own_lanes(nn(ds.reshape(PER * TOKENS, TOKENS), q)) * scale
        dqkv[:, 2 * C + g * 128 : 2 * C + (g + 1) * 128] = dv.astype(BF16)
        dqkv[:, C + g * 128 : C + (g + 1) * 128] = dk.astype(BF16)
        for j in range(PER):
            at = g * 128 + j * HEAD
            dqt[at : at + HEAD, :] = nn(kvt[at : at + HEAD, :], ds[j]) * scale

    def input_grad(dy, full, xhat, rstd):
        dqkv[:, 0:C] = dqt[...].T.astype(BF16)
        dn = nn(dqkv[...], full[...].reshape(3 * C, C))
        xh = xhat[...]
        mean = jnp.mean(dn, axis=-1, keepdims=True)
        product = jnp.mean(dn * xh, axis=-1, keepdims=True)
        return (dy + rstd[...] * (dn - mean - xh * product)).astype(BF16)

    def heads(ot):
        return ot[...].astype(F32).T.astype(BF16)

    def output(x, o, proj):
        return (x + nn(o, proj[...])).astype(BF16)

    def copy_core(m):
        return pltpu.make_async_remote_copy(
            part16.at[m, half(1 - core)],
            half_in.at[m],
            c_ss.at[m],
            c_rs.at[m],
            device_id=sibling,
            device_id_type=MESH,
        )

    def owned(m, e):
        e = e - m * n_y
        return jnp.where(e < 0, e + xy, e)

    mine = [jnp.minimum(owned(m, spot), n_own - 1) for m in range(2)]

    def if_owner(m):
        return pl.when(owned(m, spot) < n_own)

    def if_not_owner(m):
        return pl.when(owned(m, spot) >= n_own)

    def remote(source, target, ss, rs, device=sibling):
        return pltpu.make_async_remote_copy(
            source, target, ss, rs, device_id=device, device_id_type=MESH
        )

    def chunk(index, n=1):
        return pl.ds(pl.multiple_of(index * chunk_rows, 16), n * chunk_rows)

    def half(c):
        return pl.ds(pl.multiple_of(c * (C // 2), 64), C // 2)

    far_first = [d for i in range(n_z) for d in (n_z // 2 + i, n_z // 2 - i)]
    far_first = [d for d in dict.fromkeys(far_first) if 0 < d < n_z]
    z_steps = [[8, 4, 12], [2, 1, 15]] if n_z == 16 else [far_first]
    z_order = [lax.div(z, 4), 4 + lax.rem(z, 4)] if n_z == 16 else [z]
    z_slots = [(0, 4), (4, 4)] if n_z == 16 else [(0, n_z)]

    def sum_start(m, total):
        part[m] = total
        part16[m] = total.astype(BF16)
        copy_core(m).start()

    def sum_xy(m):
        copy_core(m).wait_recv()
        both = part[m, half(core), :] + half_in[m].astype(F32)
        chunks[m] = both.astype(BF16).reshape(n_own, chunk_rows, C)
        for move in moves:
            to, device = place(move)
            k = owned(m, to)

            @pl.when(k < n_own)
            def _():
                source = chunks.at[m, jnp.minimum(k, n_own - 1)]
                remote(source, xy_in.at[m, spot], xy_ss.at[m], xy_rs.at[m], device).start()

    def z_send(m, i, value):
        slot = z_order[i]
        z_in[m, slot] = value.astype(BF16)
        for d in z_steps[i]:
            block = z_in.at[m, slot]
            remote(block, block, z_ss.at[m, i], z_rs.at[m, i], at_z(d)).start()

    def z_sum(m, i):
        at, n = z_slots[i]
        if n > 1:
            several = z_in.at[m, at : at + n - 1]
            remote(several, several, z_ss.at[m, i], z_rs.at[m, i]).wait_recv()
        return jnp.sum(z_in[m, at : at + n].astype(F32), axis=0)

    def sum_z(m):
        @if_owner(m)
        def _():
            xy_in[m, spot] = chunks[m, mine[m]]
            several = xy_in.at[m, 0 : xy - 1]
            remote(several, several, xy_ss.at[m], xy_rs.at[m]).wait_recv()
            z_send(m, 0, jnp.sum(xy_in[m].astype(F32), axis=0))

    def sum_z_again(m):
        if len(z_steps) > 1:

            @if_owner(m)
            def _():
                z_send(m, 1, z_sum(m, 0))

    def sum_back(m):
        @if_owner(m)
        def _():
            block = final.at[m, chunk(core * n_own + mine[m])]
            final[m, chunk(core * n_own + mine[m]), :] = z_sum(m, len(z_steps) - 1).astype(BF16)
            for move in moves:
                remote(block, block, fin_ss.at[m], fin_rs.at[m], place(move)[1]).start()

    def sum_share(m):
        def wait(n):
            several = final.at[m, 0 : n * chunk_rows]
            remote(several, several, fin_ss.at[m], fin_rs.at[m]).wait_recv()

        if_owner(m)(lambda: wait(n_own - 1))
        if_not_owner(m)(lambda: wait(n_own))
        block = final.at[m, half(core)]
        remote(block, block, half_ss.at[m], half_rs.at[m]).start()

    def sum_end(m):
        block = final.at[m, half(core)]
        remote(block, block, half_ss.at[m], half_rs.at[m]).wait_recv()
        results[m].start()

    def sum_sent(m):
        copy_core(m).wait_send()
        block = final.at[m, half(core)]
        remote(block, block, half_ss.at[m], half_rs.at[m]).wait_send()

        def wait(n):
            several = chunks.at[m, 0:n]
            remote(several, several, xy_ss.at[m], xy_rs.at[m]).wait_send()

        @if_not_owner(m)
        def _():
            wait(n_own)

        @if_owner(m)
        def _():
            wait(n_own - 1)
            several = xy_in.at[m, 0 : xy - 1]
            remote(several, several, fin_ss.at[m], fin_rs.at[m]).wait_send()
            for i, (at, n) in enumerate(z_slots):
                if n > 1:
                    several = z_in.at[m, at : at + n - 1]
                    remote(several, several, z_ss.at[m, i], z_rs.at[m, i]).wait_send()

    n1 = norm(xf[...], xhat_p, rstd_p)
    loads["tab_p"].wait()
    align(tab_p, spread_p, 0, WLAT)
    loads["pick"].wait()
    expand(spread_p, bias_p, None)
    told(0)
    tell(1)
    halo_cot = halo(0, -1)
    loads["tab_s"].wait()
    align(tab_s, spread_s, 0, 6)
    for arriving, passed_on in zip(first[:3], beside[:3]):
        arriving.wait_recv()
        passed_on.start()
    for copy in first[:3]:
        copy.wait_send()
    first[3].start()
    loads["wp_half"].wait()
    for copy in beside[:3]:
        copy.wait_recv()
    told(1)
    tell(2)
    project(n1, wp, qkv_p, kvt_p)
    for g in range(GROUPS):
        p = softmax(g, qkv_p, bias_p)
        probs_p[g * PER : (g + 1) * PER] = p
        values(g, p.astype(BF16), kvt_p, ot_p)
    loads["proj_p"].wait()
    loads["scatter"].wait()
    o1 = heads(ot_p)
    to_quads(1, output(xf[...], o1, proj_p))
    halo_h1 = halo(1, -1)

    loads["gather"].wait()
    dy2 = arrived(0, halo_cot)
    dy2f[...] = dy2
    loads["proj_s"].wait()
    do2 = nt(dy2.astype(BF16), proj_s[...]).astype(BF16)
    key = lax.broadcasted_iota(jnp.int32, (TOKENS, TOKENS), 0)
    query = lax.broadcasted_iota(jnp.int32, (TOKENS, TOKENS), 1)
    edge = jnp.where(lat == n_lat - 1, TOKENS // 2, TOKENS)
    same = ((key & 1) == (query & 1)) & ((key >= edge) == (query >= edge))
    to_quads(4, o1)
    halo_o1 = halo(4, -1)
    align(tab_s, spread_s, 6, WLAT)
    first[3].wait_recv()
    beside[3].start()
    expand(spread_s, bias_s, jnp.where(same, 0.0, -1e30))
    loads["ws_half"].wait()
    beside[3].wait_recv()
    told(2)

    s2 = arrived(1, halo_h1)
    s2f[...] = s2
    n2 = norm(s2, xhat_s, rstd_s)
    project(n2, ws, qkv_s, kvt_s)
    for g in range(GROUPS):
        p = softmax(g, qkv_s, bias_s)
        probs_s[g * PER : (g + 1) * PER] = p
        values(g, p.astype(BF16), kvt_s, ot_s)
    sum_start(1, nn(ot_s[...], dy2f[...].astype(BF16)))
    for g in range(GROUPS):
        p = probs_s[g * PER : (g + 1) * PER]
        grads(g, p, p.astype(BF16), do2, qkv_s, kvt_s)
    sum_xy(1)
    ds2 = input_grad(dy2f[...], ws, xhat_s, rstd_s)
    ot_r = arrived(4, halo_o1).T.astype(BF16)
    sum_start(0, nn(ot_r, ds2))
    to_quads(2, ds2)
    halo_g1 = halo(2, 1)

    y2 = output(s2f[...], heads(ot_s), proj_s)
    to_quads(3, y2)
    halo_out = halo(3, 1)
    sum_xy(0)
    sum_z(1)

    g1 = arrived(2, halo_g1)
    do1 = nt(g1.astype(BF16), proj_p[...]).astype(BF16)
    for g in range(GROUPS):
        p = probs_p[g * PER : (g + 1) * PER]
        grads(g, p, p.astype(BF16), do1, qkv_p, kvt_p)
        if g == 1:
            sum_z(0)
    xf[...] = input_grad(g1, wp, xhat_p, rstd_p).astype(F32)
    for i in range(WLAT * WLON):
        grad_out[i] = xf[2 * i : 2 * i + 2, :].astype(BF16)
    results[3].start()
    s2f[...] = arrived(3, halo_out)
    for i in range(WLAT * WLON):
        field_out[i] = s2f[2 * i : 2 * i + 2, :].astype(BF16)
    results[2].start()
    sum_z_again(1)
    sum_z_again(0)
    sum_back(1)
    sum_back(0)
    sum_share(1)
    sum_share(0)
    sum_end(1)
    sum_end(0)
    for copies in (halo_cot, halo_h1, halo_o1, halo_g1, halo_out, first[3:], beside):
        for copy in copies:
            copy.wait_send()
    sum_sent(1)
    sum_sent(0)
    for copy in results:
        copy.wait()


def store(*refs):
    sources, targets, staged, semaphores = refs[:4], refs[4:8], refs[8:12], refs[12]
    taken = [pltpu.make_async_copy(sources[i], staged[i], semaphores.at[i]) for i in range(4)]
    given = [pltpu.make_async_copy(staged[i], targets[i], semaphores.at[4 + i]) for i in range(4)]
    for copy in taken:
        copy.start()
    for before, after in zip(taken, given):
        before.wait()
        after.start()
    for copy in given:
        copy.wait()


def body(sizes, field, cotangent, qkv_plain, proj_plain, bias_plain, qkv_shift, proj_shift, bias_shift):
    def rows(x):
        return x.transpose(0, 2, 3, 1, 4).reshape(WLAT * WLON, LEV, C)

    gather, scatter, pick = constants()
    operands = dict(
        field=rows(field),
        cot=rows(cotangent),
        wp_half=qkv_plain.T,
        ws_half=qkv_shift.T,
        proj_p=proj_plain,
        proj_s=proj_shift,
        tab_p=bias_plain.reshape(HEADS, -1),
        tab_s=bias_shift.reshape(HEADS, -1),
        gather=jnp.asarray(gather, BF16),
        scatter=jnp.asarray(scatter, BF16),
        pick=jnp.asarray(pick, BF16),
    )
    n_lat, n_lon, n_dp = sizes
    xy = n_lat // 2 * 2 * n_dp
    owners = max(d for d in (1, 2, 3, 4, 6, 12) if d <= xy)
    plan = (xy, n_lon // 2, C // 2 // owners)
    buffers = scratch(plan)
    hbm = pl.BlockSpec(memory_space=pl.ANY)
    grid_shape = jax.ShapeDtypeStruct((WLAT * WLON, LEV, C), BF16)
    square = jax.ShapeDtypeStruct((C, C), BF16)
    names = [name + "_hbm" for name, _ in OPERANDS]
    names += ["out_field", "out_grad", "gp_p", "gp_s"] + list(buffers)
    out_field, out_grad, gp_p, gp_s = pl.pallas_call(
        functools.partial(kernel, sizes, plan, names),
        out_shape=(grid_shape, grid_shape, square, square),
        in_specs=[hbm] * len(OPERANDS),
        out_specs=[hbm] * 4,
        scratch_shapes=list(buffers.values()),
        compiler_params=pltpu.CompilerParams(
            collective_id=0, has_side_effects=True, vmem_limit_bytes=56 * 2**20
        ),
    )(*[operands[name] for name, _ in OPERANDS])

    results = (out_field, out_grad, gp_p, gp_s)
    out_field, out_grad, gp_p, gp_s = pl.pallas_call(
        store,
        out_shape=tuple(jax.ShapeDtypeStruct(x.shape, x.dtype) for x in results),
        in_specs=[hbm] * 4,
        out_specs=[hbm] * 4,
        scratch_shapes=[pltpu.VMEM(x.shape, x.dtype) for x in results]
        + [pltpu.SemaphoreType.DMA((8,))],
        compiler_params=pltpu.CompilerParams(vmem_limit_bytes=56 * 2**20),
    )(*results)

    def grid(x):
        return x.reshape(1, WLAT, WLON, LEV, C).transpose(0, 3, 1, 2, 4)

    return grid(out_field), grid(out_grad), gp_p, gp_s


def solution(mesh):
    sizes = tuple(mesh.shape[a] for a in ("lat", "lon", "dp"))
    grid = P("dp", None, "lat", "lon", None)
    table = P(None, "lat", None, None)
    columns = P(None, "dp")
    return jax.shard_map(
        functools.partial(body, sizes),
        mesh=mesh,
        in_specs=(grid, grid, columns, P(), table, columns, P(), table),
        out_specs=(grid, grid, P(), P()),
        check_vma=False,
    )
```

```python
import functools

import jax
import jax.numpy as jnp
import numpy as np
from jax import lax
from jax.experimental import pallas as pl
from jax.experimental.pallas import tpu as pltpu
from jax.sharding import PartitionSpec as P

HEADS = 12
HEAD = 32
C = 384
LEV = 2
WLAT = 12
WLON = 6
TOKENS = LEV * WLAT * WLON
QUAD = 48
GROUPS = 3
PER = HEADS // GROUPS
REL = 2 * WLON - 1
CHUNK = WLAT * REL
MESH = pl.DeviceIdType.MESH
F32 = jnp.float32
BF16 = jnp.bfloat16


def nn(a, b):
    return lax.dot_general(a, b, (((1,), (0,)), ((), ())), preferred_element_type=F32)


def nt(a, b):
    return lax.dot_general(a, b, (((1,), (1,)), ((), ())), preferred_element_type=F32)


def token(h, w, z):
    return (h * WLON + w) * LEV + z


def constants():
    gather = np.zeros((TOKENS, 4 * QUAD), np.float32)
    pick = np.zeros((TOKENS, 256), np.float32)
    for h in range(WLAT):
        for w in range(WLON):
            for z in range(LEV):
                slot = (h // 6) * 2 + w // 3
                inner = ((h % 6) * 3 + w % 3) * 2 + (1 - z)
                gather[token(h, w, z), slot * QUAD + inner] = 1
                pick[token(h, w, z), z * 127 + h * REL + WLON - 1 - w] = 1
    scatter = np.zeros((4 * QUAD, TOKENS), np.float32)
    for h in range(WLAT):
        for w in range(WLON):
            for z in range(LEV):
                slot = (h // 6) * 2 + w // 3
                scatter[slot * QUAD + ((h % 6) * 3 + w % 3) * 2 + z, token(h, w, z)] = 1
    return gather, scatter, pick


OPERANDS = (
    ("field", (WLAT * WLON, LEV, C)),
    ("cot", (WLAT * WLON, LEV, C)),
    ("wp_half", None),
    ("ws_half", None),
    ("tab_p", (HEADS, 4 * WLAT * CHUNK)),
    ("tab_s", (HEADS, 4 * WLAT * CHUNK)),
    ("scatter", (4 * QUAD, TOKENS)),
    ("gather", (TOKENS, 4 * QUAD)),
    ("pick", (TOKENS, 256)),
    ("proj_p", (C, C)),
    ("proj_s", (C, C)),
)
LOADED = [name for name, shape in OPERANDS if shape is not None]


def scratch(plan):
    xy, z, rows = plan
    tokens_f32 = pltpu.VMEM((TOKENS, C), F32)
    row_stat = pltpu.VMEM((TOKENS, 1), F32)
    full_bias = pltpu.VMEM((HEADS, TOKENS, TOKENS), F32)
    weights = pltpu.VMEM((2, 3 * C // 2, C), BF16)
    qkv = pltpu.VMEM((TOKENS, 3 * C), BF16)
    kvt = pltpu.VMEM((2 * C, TOKENS), BF16)
    heads_t = pltpu.VMEM((C, TOKENS), BF16)
    dma = pltpu.SemaphoreType.DMA
    named = {name: pltpu.VMEM(shape, BF16) for name, shape in OPERANDS if shape is not None}
    named |= dict(
        load_sem=dma((len(OPERANDS),)),
        wp=weights,
        ws=weights,
        xf=tokens_f32,
        quads=pltpu.VMEM((4 * QUAD, C), F32),
        xhat_p=tokens_f32,
        rstd_p=row_stat,
        xhat_s=tokens_f32,
        rstd_s=row_stat,
        s2f=tokens_f32,
        dy2f=tokens_f32,
        qkv_p=qkv,
        kvt_p=kvt,
        qkv_s=qkv,
        kvt_s=kvt,
        probs_p=full_bias,
        probs_s=full_bias,
        ot_p=heads_t,
        ot_s=heads_t,
        dqkv=qkv,
        dqt=pltpu.VMEM((C, TOKENS), F32),
        bias_p=full_bias,
        bias_s=full_bias,
        tabf=pltpu.VMEM((16, 6400), F32),
        spread_p=pltpu.VMEM((2, TOKENS * 16, 128), F32),
        spread_s=pltpu.VMEM((2, TOKENS * 16, 128), F32),
        send=pltpu.VMEM((5, 4, QUAD, C), BF16),
        recv=pltpu.VMEM((5, 4, QUAD, C), BF16),
        halo_ss=dma((5, 4)),
        halo_rs=dma((5, 4)),
        w_ss=dma((4,)),
        w_rs=dma((4,)),
        f_ss=dma((4,)),
        f_rs=dma((4,)),
        left=pltpu.VMEM((2, C, TOKENS), BF16),
        part=pltpu.VMEM((2, C // 2, C), F32),
        part16=pltpu.VMEM((2, C // 2, C), BF16),
        half_in=pltpu.VMEM((2, C // 2, C), BF16),
        chunks=pltpu.VMEM((2, C // 2 // rows, rows, C), BF16),
        xy_in=pltpu.VMEM((2, xy, rows, C), BF16),
        z_in=pltpu.VMEM((2, z, rows, C), BF16),
        final=pltpu.VMEM((2, C, C), BF16),
        out_sem=dma((4,)),
        field_out=pltpu.VMEM((WLAT * WLON, LEV, C), BF16),
        grad_out=pltpu.VMEM((WLAT * WLON, LEV, C), BF16),
        c_ss=dma((2,)),
        c_rs=dma((2,)),
        xy_ss=dma((2,)),
        xy_rs=dma((2,)),
        z_ss=dma((2, 2)),
        z_rs=dma((2, 2)),
        fin_ss=dma((2,)),
        fin_rs=dma((2,)),
        half_ss=dma((2,)),
        half_rs=dma((2,)),
        roll=pltpu.SemaphoreType.REGULAR((3,)),
    )
    return named


def kernel(sizes, plan, names, *refs):
    run(sizes, plan, **dict(zip(names, refs)))


def run(
    sizes,
    plan,
    out_field,
    out_grad,
    gp_p,
    gp_s,
    wp,
    ws,
    xf,
    quads,
    xhat_p,
    rstd_p,
    xhat_s,
    rstd_s,
    s2f,
    dy2f,
    qkv_p,
    kvt_p,
    qkv_s,
    kvt_s,
    probs_p,
    probs_s,
    ot_p,
    ot_s,
    dqkv,
    dqt,
    bias_p,
    bias_s,
    tabf,
    spread_p,
    spread_s,
    send,
    recv,
    halo_ss,
    halo_rs,
    w_ss,
    w_rs,
    f_ss,
    f_rs,
    left,
    part,
    part16,
    half_in,
    chunks,
    xy_in,
    z_in,
    final,
    c_ss,
    c_rs,
    xy_ss,
    xy_rs,
    z_ss,
    z_rs,
    fin_ss,
    fin_rs,
    half_ss,
    half_rs,
    roll,
    load_sem,
    out_sem,
    field_out,
    grad_out,
    **local,
):
    n_lat, n_lon, n_dp = sizes
    lat, lon, dp = lax.axis_index("lat"), lax.axis_index("lon"), lax.axis_index("dp")
    core = lax.rem(lat, 2)
    sibling = (lat + 1 - 2 * core, lon, dp)
    across = (lat, lax.rem(lon + n_lon // 2, n_lon), 1 - dp)

    def near(dlat, dlon):
        return (
            lax.rem(lat + dlat + n_lat, n_lat),
            lax.rem(lon + dlon + n_lon, n_lon),
            dp,
        )

    xy, n_z, chunk_rows = plan
    n_y = n_lat // 2
    n_own = C // 2 // chunk_rows
    z = lax.rem(lon, n_z)
    x_lo, row = lax.div(lon, n_z), lax.div(lat, 2)

    def wrap(value, size):
        return jnp.where(value >= size, value - size, value)

    def place(move):
        lo, hi, up = move
        to_lo = 1 - x_lo if lo else x_lo
        to_hi = 1 - dp if hi else dp
        to_row = wrap(row + up, n_y)
        device = (2 * to_row + core, to_lo * n_z + z, to_hi)
        return (to_lo + 2 * to_hi) * n_y + to_row, device

    def hops(move):
        lo, hi, up = move
        return (1 if lo else 2 * hi) + min(up, n_y - up)

    moves = [(lo, hi, up) for lo in range(2) for hi in range(2) for up in range(n_y)][1:]
    moves = sorted(moves, key=hops, reverse=True)
    spot = place((0, 0, 0))[0]

    def at_z(d):
        return (lat, lon - z + wrap(z + d, n_z), dp)

    def greet(semaphore, device):
        pl.semaphore_signal(semaphore, inc=1, device_id=device, device_id_type=MESH)

    def along_z(d):
        return (lat, lon - z + lax.rem(z + d + 8 * n_z, n_z), dp)

    beside_x = (lat, across[1], dp)
    y_up, y_down = near(2, 0), near(-2, 0)
    barrier = pltpu.get_barrier_semaphore()
    around = [across, sibling, beside_x, y_up, y_down, along_z(1), along_z(-1)]
    around += [near(a, b) for a, b in ((1, 0), (-1, 0), (0, 1), (0, -1))]
    for device in around:
        greet(barrier, device)

    def tell(i):
        for device in (across, sibling, beside_x, y_up, y_down):
            greet(roll.at[i], device)
        for d in (2**i, -(2**i)):
            greet(roll.at[i], along_z(d))
        if i == 0:
            greet(roll.at[i], near(1, 0))
            greet(roll.at[i], near(-1, 0))

    def told(i):
        pl.semaphore_wait(roll.at[i], 9 if i == 0 else 7)

    results = [
        pltpu.make_async_copy(a, b, out_sem.at[i])
        for i, (a, b) in enumerate(
            ((final.at[0], gp_p), (final.at[1], gp_s), (field_out, out_field), (grad_out, out_grad))
        )
    ]
    loads = {}
    for i, (name, shape) in enumerate(OPERANDS):
        source = local[name + "_hbm"]
        target = local[name] if shape else {"wp_half": wp, "ws_half": ws}[name].at[dp]
        loads[name] = pltpu.make_async_copy(source, target, load_sem.at[i])
        loads[name].start()
    wp_half, ws_half = local["wp_half_hbm"], local["ws_half_hbm"]
    field, cot, proj_p, proj_s, tab_p, tab_s, gather, scatter, pick = (
        local[name]
        for name in (
            "field", "cot", "proj_p", "proj_s", "tab_p", "tab_s", "gather", "scatter", "pick"
        )
    )
    pl.semaphore_wait(barrier, len(around))

    def piece(i, n):
        size = 288 // n
        return pl.ds(pl.multiple_of(core * 288 + i * size, 16), size)

    def weights_across(source, full, at, i):
        return pltpu.make_async_remote_copy(
            source.at[at],
            full.at[dp, at],
            w_ss.at[i],
            w_rs.at[i],
            device_id=across,
            device_id_type=MESH,
        )

    def weights_beside(full, at, i):
        part = full.at[1 - dp, at]
        return pltpu.make_async_remote_copy(
            part, part, f_ss.at[i], f_rs.at[i], device_id=sibling, device_id_type=MESH
        )

    places = [(wp_half, wp, piece(i, 3)) for i in range(3)] + [(ws_half, ws, piece(0, 1))]
    first = [weights_across(*place, i) for i, place in enumerate(places)]
    beside = [weights_beside(*place[1:], i) for i, place in enumerate(places)]
    for copy in first[:3]:
        copy.start()
    tell(0)

    def halo(i, by):
        kept = 3 if by < 0 else 0
        copies = []
        for slot in range(4):
            if slot == kept:
                recv[i, 3 - slot] = send[i, slot]
                continue
            a, b = divmod(slot, 2)
            moves = 0 if by < 0 else 1
            copies.append(
                pltpu.make_async_remote_copy(
                    send.at[i, slot],
                    recv.at[i, 3 - slot],
                    halo_ss.at[i, slot],
                    halo_rs.at[i, 3 - slot],
                    device_id=near(by if a == moves else 0, by if b == moves else 0),
                    device_id_type=MESH,
                )
            )
        for copy in copies:
            copy.start()
        return copies

    def arrived(i, copies):
        for copy in copies:
            copy.wait_recv()
        return nn(gather[...], recv[i].reshape(4 * QUAD, C))

    def to_quads(i, x):
        send[i] = nn(scatter[...], x).astype(BF16).reshape(4, QUAD, C)

    loads["cot"].wait()
    quads[...] = jnp.zeros_like(quads)
    for h in range(WLAT):
        for w in range(WLON):
            at = ((h // 6) * 2 + w // 3) * QUAD + ((h % 6) * 3 + w % 3) * 2
            quads[at : at + 2, :] = cot[h * WLON + w].astype(F32)
    send[0] = quads[...].astype(BF16).reshape(4, QUAD, C)

    loads["field"].wait()
    for i in range(WLAT * WLON):
        xf[2 * i : 2 * i + 2, :] = field[i].astype(F32)

    def norm(x, xhat, rstd):
        mean = jnp.mean(x, axis=-1, keepdims=True)
        centred = x - mean
        r = lax.rsqrt(jnp.mean(centred * centred, axis=-1, keepdims=True) + 1e-5)
        y = centred * r
        xhat[...] = y
        rstd[...] = r
        return y.astype(BF16)

    lane256 = lax.broadcasted_iota(jnp.int32, (16, 256), 1)

    def align(tab, spread, start, stop):
        if start == 0:
            tabf[...] = jnp.zeros_like(tabf)
            tabf[0:HEADS, 0 : 4 * WLAT * CHUNK] = tab[...].astype(F32)

        def row(h, carry):
            for za in range(LEV):
                parts = []
                for zb in range(LEV):
                    c = (za * 2 + zb) * WLAT + h
                    tile = c + c // 32
                    off = 4 * lax.rem(c, 32)
                    window = tabf[:, pl.ds(pl.multiple_of(tile * 128, 128), 256)]
                    parts.append(pltpu.roll(window, lax.rem(256 + 127 * zb - off, 256), 1))
                for w in range(WLON):
                    low, high = parts
                    if w:
                        low = pltpu.roll(low, 256 - w, 1)
                        high = pltpu.roll(high, 256 - w, 1)
                    at = pl.multiple_of((h * WLON + w) * 32 + za * 16, 16)
                    both = jnp.where(lane256 < 127, low, high)
                    spread[0, pl.ds(at, 16), :] = both[:, :128]
                    spread[1, pl.ds(at, 16), :] = both[:, 128:]
            return carry

        lax.fori_loop(start, stop, row, 0)

    def expand(spread, bias, hide):
        for head in range(HEADS):
            lanes = [spread[half, pl.ds(head, TOKENS, stride=16), :] for half in range(2)]
            table = jnp.concatenate(lanes, axis=1).astype(BF16)
            full = nt(pick[...], table)
            bias[head] = full if hide is None else full + hide

    lane = lax.broadcasted_iota(jnp.int32, (TOKENS, 128), 1) // HEAD

    def by_head(x):
        zero = jnp.zeros_like(x)
        return jnp.concatenate([jnp.where(lane == j, x, zero) for j in range(PER)], axis=0)

    def own_lanes(x):
        total = jnp.where(lane == 0, x[0:TOKENS], 0.0)
        for j in range(1, PER):
            total += jnp.where(lane == j, x[j * TOKENS : (j + 1) * TOKENS], 0.0)
        return total

    scale = 1.0 / HEAD**0.5

    def project(n, full, qkv, kvt):
        w = full[...].reshape(3 * C, C)
        qkv[...] = nt(n, w).astype(BF16)
        kvt[...] = nt(w[C:], n).astype(BF16)

    def softmax(g, qkv, bias):
        q = qkv[:, g * 128 : (g + 1) * 128]
        k = qkv[:, C + g * 128 : C + (g + 1) * 128]
        s = nt(by_head(k), q).reshape(PER, TOKENS, TOKENS) * scale
        s = s + bias[g * PER : (g + 1) * PER]
        e = jnp.exp(s - jnp.max(s, axis=1, keepdims=True))
        return e / jnp.sum(e, axis=1, keepdims=True)

    def values(g, p, kvt, ot):
        for j in range(PER):
            at = g * 128 + j * HEAD
            vt = kvt[C + at : C + at + HEAD, :]
            ot[at : at + HEAD, :] = nn(vt, p[j]).astype(BF16)

    def grads(g, p, pb, do, qkv, kvt):
        cols = slice(g * 128, (g + 1) * 128)
        q = qkv[:, cols]
        v = qkv[:, 2 * C + g * 128 : 2 * C + (g + 1) * 128]
        dog = do[:, cols]
        dp_ = nt(by_head(v), dog).reshape(PER, TOKENS, TOKENS)
        inner = jnp.sum(p * dp_, axis=1, keepdims=True)
        ds = (p * (dp_ - inner)).astype(BF16)
        dv = own_lanes(nn(pb.reshape(PER * TOKENS, TOKENS), dog))
        dk = own_lanes(nn(ds.reshape(PER * TOKENS, TOKENS), q)) * scale
        dqkv[:, 2 * C + g * 128 : 2 * C + (g + 1) * 128] = dv.astype(BF16)
        dqkv[:, C + g * 128 : C + (g + 1) * 128] = dk.astype(BF16)
        for j in range(PER):
            at = g * 128 + j * HEAD
            dqt[at : at + HEAD, :] = nn(kvt[at : at + HEAD, :], ds[j]) * scale

    def input_grad(dy, full, xhat, rstd):
        dqkv[:, 0:C] = dqt[...].T.astype(BF16)
        dn = nn(dqkv[...], full[...].reshape(3 * C, C))
        xh = xhat[...]
        mean = jnp.mean(dn, axis=-1, keepdims=True)
        product = jnp.mean(dn * xh, axis=-1, keepdims=True)
        return (dy + rstd[...] * (dn - mean - xh * product)).astype(BF16)

    def heads(ot):
        return ot[...].astype(F32).T.astype(BF16)

    def output(x, o, proj):
        return (x + nn(o, proj[...])).astype(BF16)

    def copy_core(m):
        return pltpu.make_async_remote_copy(
            part16.at[m],
            half_in.at[m],
            c_ss.at[m],
            c_rs.at[m],
            device_id=sibling,
            device_id_type=MESH,
        )

    def owned(m, e):
        e = e - m * n_y
        return jnp.where(e < 0, e + xy, e)

    mine = [jnp.minimum(owned(m, spot), n_own - 1) for m in range(2)]

    def if_owner(m):
        return pl.when(owned(m, spot) < n_own)

    def if_not_owner(m):
        return pl.when(owned(m, spot) >= n_own)

    def remote(source, target, ss, rs, device=sibling):
        return pltpu.make_async_remote_copy(
            source, target, ss, rs, device_id=device, device_id_type=MESH
        )

    def chunk(index, n=1):
        return pl.ds(pl.multiple_of(index * chunk_rows, 16), n * chunk_rows)

    def half(c):
        return pl.ds(pl.multiple_of(c * (C // 2), 64), C // 2)

    far_first = [d for i in range(n_z) for d in (n_z // 2 + i, n_z // 2 - i)]
    far_first = [d for d in dict.fromkeys(far_first) if 0 < d < n_z]
    z_steps = [[8, 4, 12], [2, 1, 15]] if n_z == 16 else [far_first]
    z_order = [lax.div(z, 4), 4 + lax.rem(z, 4)] if n_z == 16 else [z]
    z_slots = [(0, 4), (4, 4)] if n_z == 16 else [(0, n_z)]

    def sum_start(m, ot, dy):
        left[m] = ot
        part16[m] = nn(left[m, half(1 - core), :], dy).astype(BF16)
        copy_core(m).start()
        part[m] = nn(left[m, half(core), :], dy)

    def sum_xy(m):
        copy_core(m).wait_recv()
        both = part[m] + half_in[m].astype(F32)
        chunks[m] = both.astype(BF16).reshape(n_own, chunk_rows, C)
        for move in moves:
            to, device = place(move)
            k = owned(m, to)

            @pl.when(k < n_own)
            def _():
                source = chunks.at[m, jnp.minimum(k, n_own - 1)]
                remote(source, xy_in.at[m, spot], xy_ss.at[m], xy_rs.at[m], device).start()

    def z_send(m, i, value):
        slot = z_order[i]
        z_in[m, slot] = value.astype(BF16)
        for d in z_steps[i]:
            block = z_in.at[m, slot]
            remote(block, block, z_ss.at[m, i], z_rs.at[m, i], at_z(d)).start()

    def z_sum(m, i):
        at, n = z_slots[i]
        if n > 1:
            several = z_in.at[m, at : at + n - 1]
            remote(several, several, z_ss.at[m, i], z_rs.at[m, i]).wait_recv()
        return jnp.sum(z_in[m, at : at + n].astype(F32), axis=0)

    def sum_z(m):
        @if_owner(m)
        def _():
            xy_in[m, spot] = chunks[m, mine[m]]
            several = xy_in.at[m, 0 : xy - 1]
            remote(several, several, xy_ss.at[m], xy_rs.at[m]).wait_recv()
            z_send(m, 0, jnp.sum(xy_in[m].astype(F32), axis=0))

    def sum_z_again(m):
        if len(z_steps) > 1:

            @if_owner(m)
            def _():
                z_send(m, 1, z_sum(m, 0))

    def sum_back(m):
        @if_owner(m)
        def _():
            block = final.at[m, chunk(core * n_own + mine[m])]
            final[m, chunk(core * n_own + mine[m]), :] = z_sum(m, len(z_steps) - 1).astype(BF16)
            for move in moves:
                remote(block, block, fin_ss.at[m], fin_rs.at[m], place(move)[1]).start()

    def sum_share(m):
        def wait(n):
            several = final.at[m, 0 : n * chunk_rows]
            remote(several, several, fin_ss.at[m], fin_rs.at[m]).wait_recv()

        if_owner(m)(lambda: wait(n_own - 1))
        if_not_owner(m)(lambda: wait(n_own))
        block = final.at[m, half(core)]
        remote(block, block, half_ss.at[m], half_rs.at[m]).start()

    def sum_end(m):
        block = final.at[m, half(core)]
        remote(block, block, half_ss.at[m], half_rs.at[m]).wait_recv()
        results[m].start()

    def sum_sent(m):
        copy_core(m).wait_send()
        block = final.at[m, half(core)]
        remote(block, block, half_ss.at[m], half_rs.at[m]).wait_send()

        def wait(n):
            several = chunks.at[m, 0:n]
            remote(several, several, xy_ss.at[m], xy_rs.at[m]).wait_send()

        @if_not_owner(m)
        def _():
            wait(n_own)

        @if_owner(m)
        def _():
            wait(n_own - 1)
            several = xy_in.at[m, 0 : xy - 1]
            remote(several, several, fin_ss.at[m], fin_rs.at[m]).wait_send()
            for i, (at, n) in enumerate(z_slots):
                if n > 1:
                    several = z_in.at[m, at : at + n - 1]
                    remote(several, several, z_ss.at[m, i], z_rs.at[m, i]).wait_send()

    n1 = norm(xf[...], xhat_p, rstd_p)
    loads["tab_p"].wait()
    align(tab_p, spread_p, 0, WLAT)
    loads["pick"].wait()
    expand(spread_p, bias_p, None)
    told(0)
    tell(1)
    halo_cot = halo(0, -1)
    loads["tab_s"].wait()
    align(tab_s, spread_s, 0, 6)
    for arriving, passed_on in zip(first[:3], beside[:3]):
        arriving.wait_recv()
        passed_on.start()
    for copy in first[:3]:
        copy.wait_send()
    first[3].start()
    loads["wp_half"].wait()
    for copy in beside[:3]:
        copy.wait_recv()
    told(1)
    tell(2)
    project(n1, wp, qkv_p, kvt_p)
    for g in range(GROUPS):
        p = softmax(g, qkv_p, bias_p)
        probs_p[g * PER : (g + 1) * PER] = p
        values(g, p.astype(BF16), kvt_p, ot_p)
    loads["proj_p"].wait()
    loads["scatter"].wait()
    o1 = heads(ot_p)
    to_quads(1, output(xf[...], o1, proj_p))
    halo_h1 = halo(1, -1)

    loads["gather"].wait()
    dy2 = arrived(0, halo_cot)
    dy2f[...] = dy2
    loads["proj_s"].wait()
    do2 = nt(dy2.astype(BF16), proj_s[...]).astype(BF16)
    key = lax.broadcasted_iota(jnp.int32, (TOKENS, TOKENS), 0)
    query = lax.broadcasted_iota(jnp.int32, (TOKENS, TOKENS), 1)
    edge = jnp.where(lat == n_lat - 1, TOKENS // 2, TOKENS)
    same = ((key & 1) == (query & 1)) & ((key >= edge) == (query >= edge))
    to_quads(4, o1)
    halo_o1 = halo(4, -1)
    align(tab_s, spread_s, 6, WLAT)
    first[3].wait_recv()
    beside[3].start()
    expand(spread_s, bias_s, jnp.where(same, 0.0, -1e30))
    loads["ws_half"].wait()
    beside[3].wait_recv()
    told(2)

    s2 = arrived(1, halo_h1)
    s2f[...] = s2
    n2 = norm(s2, xhat_s, rstd_s)
    project(n2, ws, qkv_s, kvt_s)
    for g in range(GROUPS):
        p = softmax(g, qkv_s, bias_s)
        probs_s[g * PER : (g + 1) * PER] = p
        values(g, p.astype(BF16), kvt_s, ot_s)
    sum_start(1, ot_s[...], dy2f[...].astype(BF16))
    for g in range(GROUPS):
        p = probs_s[g * PER : (g + 1) * PER]
        grads(g, p, p.astype(BF16), do2, qkv_s, kvt_s)
    sum_xy(1)
    ds2 = input_grad(dy2f[...], ws, xhat_s, rstd_s)
    ot_r = arrived(4, halo_o1).T.astype(BF16)
    sum_start(0, ot_r, ds2)
    to_quads(2, ds2)
    halo_g1 = halo(2, 1)

    y2 = output(s2f[...], heads(ot_s), proj_s)
    to_quads(3, y2)
    halo_out = halo(3, 1)
    sum_xy(0)
    sum_z(1)

    g1 = arrived(2, halo_g1)
    do1 = nt(g1.astype(BF16), proj_p[...]).astype(BF16)
    for g in range(GROUPS):
        p = probs_p[g * PER : (g + 1) * PER]
        grads(g, p, p.astype(BF16), do1, qkv_p, kvt_p)
        if g == 1:
            sum_z(0)
    xf[...] = input_grad(g1, wp, xhat_p, rstd_p).astype(F32)
    for i in range(WLAT * WLON):
        grad_out[i] = xf[2 * i : 2 * i + 2, :].astype(BF16)
    results[3].start()
    s2f[...] = arrived(3, halo_out)
    for i in range(WLAT * WLON):
        field_out[i] = s2f[2 * i : 2 * i + 2, :].astype(BF16)
    results[2].start()
    sum_z_again(1)
    sum_z_again(0)
    sum_back(1)
    sum_back(0)
    sum_share(1)
    sum_share(0)
    sum_end(1)
    sum_end(0)
    for copies in (halo_cot, halo_h1, halo_o1, halo_g1, halo_out, first[3:], beside):
        for copy in copies:
            copy.wait_send()
    sum_sent(1)
    sum_sent(0)
    for copy in results:
        copy.wait()


def store(*refs):
    sources, targets, staged, semaphores = refs[:4], refs[4:8], refs[8:12], refs[12]
    taken = [pltpu.make_async_copy(sources[i], staged[i], semaphores.at[i]) for i in range(4)]
    given = [pltpu.make_async_copy(staged[i], targets[i], semaphores.at[4 + i]) for i in range(4)]
    for copy in taken:
        copy.start()
    for before, after in zip(taken, given):
        before.wait()
        after.start()
    for copy in given:
        copy.wait()


def body(sizes, field, cotangent, qkv_plain, proj_plain, bias_plain, qkv_shift, proj_shift, bias_shift):
    def rows(x):
        return x.transpose(0, 2, 3, 1, 4).reshape(WLAT * WLON, LEV, C)

    gather, scatter, pick = constants()
    operands = dict(
        field=rows(field),
        cot=rows(cotangent),
        wp_half=qkv_plain.T,
        ws_half=qkv_shift.T,
        proj_p=proj_plain,
        proj_s=proj_shift,
        tab_p=bias_plain.reshape(HEADS, -1),
        tab_s=bias_shift.reshape(HEADS, -1),
        gather=jnp.asarray(gather, BF16),
        scatter=jnp.asarray(scatter, BF16),
        pick=jnp.asarray(pick, BF16),
    )
    n_lat, n_lon, n_dp = sizes
    xy = n_lat // 2 * 2 * n_dp
    owners = max(d for d in (1, 2, 3, 4, 6, 12) if d <= xy)
    plan = (xy, n_lon // 2, C // 2 // owners)
    buffers = scratch(plan)
    hbm = pl.BlockSpec(memory_space=pl.ANY)
    grid_shape = jax.ShapeDtypeStruct((WLAT * WLON, LEV, C), BF16)
    square = jax.ShapeDtypeStruct((C, C), BF16)
    names = [name + "_hbm" for name, _ in OPERANDS]
    names += ["out_field", "out_grad", "gp_p", "gp_s"] + list(buffers)
    out_field, out_grad, gp_p, gp_s = pl.pallas_call(
        functools.partial(kernel, sizes, plan, names),
        out_shape=(grid_shape, grid_shape, square, square),
        in_specs=[hbm] * len(OPERANDS),
        out_specs=[hbm] * 4,
        scratch_shapes=list(buffers.values()),
        compiler_params=pltpu.CompilerParams(
            collective_id=0, has_side_effects=True, vmem_limit_bytes=56 * 2**20
        ),
    )(*[operands[name] for name, _ in OPERANDS])

    results = (out_field, out_grad, gp_p, gp_s)
    out_field, out_grad, gp_p, gp_s = pl.pallas_call(
        store,
        out_shape=tuple(jax.ShapeDtypeStruct(x.shape, x.dtype) for x in results),
        in_specs=[hbm] * 4,
        out_specs=[hbm] * 4,
        scratch_shapes=[pltpu.VMEM(x.shape, x.dtype) for x in results]
        + [pltpu.SemaphoreType.DMA((8,))],
        compiler_params=pltpu.CompilerParams(vmem_limit_bytes=56 * 2**20),
    )(*results)

    def grid(x):
        return x.reshape(1, WLAT, WLON, LEV, C).transpose(0, 3, 1, 2, 4)

    return grid(out_field), grid(out_grad), gp_p, gp_s


def solution(mesh):
    sizes = tuple(mesh.shape[a] for a in ("lat", "lon", "dp"))
    grid = P("dp", None, "lat", "lon", None)
    table = P(None, "lat", None, None)
    columns = P(None, "dp")
    return jax.shard_map(
        functools.partial(body, sizes),
        mesh=mesh,
        in_specs=(grid, grid, columns, P(), table, columns, P(), table),
        out_specs=(grid, grid, P(), P()),
        check_vma=False,
    )
```
